32 devices in a mesh: dp: 16 (over z, x, core), tensor: 2 (over y).
Axes of the slice: x: 2, y: 2, z: 4, core: 2. Of those that a mesh axis runs over, the one named last changes fastest.
Arguments:
- tokens: bfloat16 [8192, 2048], P(('dp', 'tensor')), may hold values from -6 to 6
- cotangent: bfloat16 [8192, 2048], P(('dp', 'tensor')), may hold values from -6 to 6
- segment_ids: int32 [8192], P('dp'), may hold values from 0 to 4, as said below
- joint_weight: float32 [2048, 3, 2048], P('dp', None, 'tensor'), may hold values from -0.125 to 0.125
- dense_weight: float32 [2048, 2048], P('dp', 'tensor'), may hold values from -0.75 to 0.75
- expand_weight: float32 [2048, 8192], P('dp', 'tensor'), may hold values from -0.125 to 0.125
- shrink_weight: float32 [2048, 8192], P('dp', 'tensor'), may hold values from -0.0625 to 0.0625
- head_bias: float32 [64, 3, 32], P('dp', None, 'tensor'), may hold values from -3 to 3
- unit_bias: float32 [64, 128], P('dp', 'tensor'), may hold values from -3 to 3
- row_vectors: float32 [4, 2048], P(None, ('dp', 'tensor')), may hold values from -0.9 to 1.45, as said below
- joint_mean: float32 [2048, 3, 2048], P('dp', None, 'tensor'), may hold values from -32 to 32
- joint_square: float32 [2048, 3, 2048], P('dp', None, 'tensor'), may hold values from 106.496 to 434.176
- dense_mean: float32 [2048, 2048], P('dp', 'tensor'), may hold values from -12 to 12
- dense_square: float32 [2048, 2048], P('dp', 'tensor'), may hold values from 17.2032 to 68.8128
- expand_mean: float32 [2048, 8192], P('dp', 'tensor'), may hold values from -16 to 16
- expand_square: float32 [2048, 8192], P('dp', 'tensor'), may hold values from 39.3216 to 155.648
- shrink_mean: float32 [2048, 8192], P('dp', 'tensor'), may hold values from -40 to 40
- shrink_square: float32 [2048, 8192], P('dp', 'tensor'), may hold values from 180.224 to 729.088
- head_mean: float32 [64, 3, 32], P('dp', None, 'tensor'), may hold values from -32 to 32
- head_square: float32 [64, 3, 32], P('dp', None, 'tensor'), may hold values from 106.496 to 434.176
- unit_mean: float32 [64, 128], P('dp', 'tensor'), may hold values from -16 to 16
- unit_square: float32 [64, 128], P('dp', 'tensor'), may hold values from 39.3216 to 155.648
- rows_mean: float32 [4, 2048], P(None, ('dp', 'tensor')), may hold values from -96 to 96
- rows_square: float32 [4, 2048], P(None, ('dp', 'tensor')), may hold values from 983.04 to 3850.24
Outputs:
- layer_output: bfloat16 [8192, 2048], P(('dp', 'tensor'))
- input_grad: float32 [8192, 2048], P(('dp', 'tensor'))
- new_joint: float32 [2048, 3, 2048], P('dp', None, 'tensor')
- new_joint_mean: float32 [2048, 3, 2048], P('dp', None, 'tensor')
- new_joint_square: float32 [2048, 3, 2048], P('dp', None, 'tensor')
- new_dense: float32 [2048, 2048], P('dp', 'tensor')
- new_dense_mean: float32 [2048, 2048], P('dp', 'tensor')
- new_dense_square: float32 [2048, 2048], P('dp', 'tensor')
- new_expand: float32 [2048, 8192], P('dp', 'tensor')
- new_expand_mean: float32 [2048, 8192], P('dp', 'tensor')
- new_expand_square: float32 [2048, 8192], P('dp', 'tensor')
- new_shrink: float32 [2048, 8192], P('dp', 'tensor')
- new_shrink_mean: float32 [2048, 8192], P('dp', 'tensor')
- new_shrink_square: float32 [2048, 8192], P('dp', 'tensor')
- new_head: float32 [64, 3, 32], P('dp', None, 'tensor')
- new_head_mean: float32 [64, 3, 32], P('dp', None, 'tensor')
- new_head_square: float32 [64, 3, 32], P('dp', None, 'tensor')
- new_unit: float32 [64, 128], P('dp', 'tensor')
- new_unit_mean: float32 [64, 128], P('dp', 'tensor')
- new_unit_square: float32 [64, 128], P('dp', 'tensor')
- new_rows: float32 [4, 2048], P(None, ('dp', 'tensor'))
- new_rows_mean: float32 [4, 2048], P(None, ('dp', 'tensor'))
- new_rows_square: float32 [4, 2048], P(None, ('dp', 'tensor'))
The draws below stay inside these ranges and needn't reach their ends.
Inputs may be any that keep to these rules, and one draw needn't show every extreme that they name: `segment_ids`: in each aligned block of 512 slots (one data group) the live slots carry ids 1, 2, 3, 4 in order, each at least once, followed by 1 to 128 padding slots with id 0; slots 512 // 2 - 1 and 256 lie in one document. `row_vectors`: row 0 lies in 0.55 to 1.45; rows 1 to 3 lie in -0.9 to 0.9.
All inputs are finite; a program needn't handle non-finite values.
Results may differ from the reference program's by a relative error of at most 0.0076.
The reference program's roundings to bfloat16 on the way count: a program that leaves them out, or rounds other values in their place, can miss the bound.
Values may be sent and summed in bfloat16 or wider, within the bound.
No kernel may reach another device: no remote copies, remote signals or barrier semaphores. Data moves between devices by JAX's collectives and lax.ppermute only.
A program may use at most 256 MiB of HBM per device.

```python
import math
import jax
import jax.numpy as jnp
from jax import lax

D = 2048
HEADS = 32
HD = 64
FF = 8192
ROTARY = 32
TOK_DEV = 512
STEP = 10
TOKENS = 8192


def draw_segment_ids(key, part):
    key = jax.random.fold_in(key, 11)
    key_pad, key_one, key_two, key_three = jax.random.split(key, 4)
    groups = TOKENS // TOK_DEV
    quarter = TOK_DEV // 4
    padding = jax.random.randint(key_pad, (groups, 1), 1, quarter + 1)
    live_count = TOK_DEV - padding
    cut_one = jax.random.randint(key_one, (groups, 1), TOK_DEV // 16, quarter)
    cut_two = cut_one + jax.random.randint(key_two, (groups, 1), TOK_DEV // 16, quarter)
    cut_three = jax.random.randint(key_three, (groups, 1), TOK_DEV * 5 // 8, TOK_DEV * 3 // 4)
    places = jnp.arange(TOK_DEV, dtype=jnp.int32)[None, :]
    labels = 1 + (places >= cut_one).astype(jnp.int32) + (places >= cut_two).astype(jnp.int32) + (places >= cut_three).astype(jnp.int32)
    labels = jnp.where(places < live_count, labels, 0)
    return labels.reshape(-1).astype(jnp.int32)


def draw_row_vectors(key, part):
    key = jax.random.fold_in(key, 7)
    key_gain, key_rest = jax.random.split(key)
    gain = 1.0 + 0.15 * jnp.clip(jax.random.normal(key_gain, (1, D), jnp.float32), -3.0, 3.0)
    others = 0.3 * jnp.clip(jax.random.normal(key_rest, (3, D), jnp.float32), -3.0, 3.0)
    return jnp.concatenate([gain, others], axis=0).astype(jnp.float32)


def spiked(array, key, source, target, blocks, factor):
    owner, partner = [(jnp.arange(array.shape[axis_at]) // (array.shape[axis_at] // blocks)).reshape([-1 if axis == axis_at else 1 for axis in range(array.ndim)]) for axis_at in (source, target)]
    chosen = jax.random.permutation(key, blocks)[partner]
    strong = (owner == chosen) | (owner == (partner + blocks // 2) % blocks)
    return jnp.where(strong, factor * array, array)


def block_levels(own_key, dims, cuts, least, top_value):
    level, own = 1.0, jax.random.fold_in(own_key, 6)
    for position, shards_of in cuts:
        draws = jnp.exp(jax.random.uniform(jax.random.fold_in(own, position), (shards_of,), jnp.float32, least / len(cuts), top_value / len(cuts)))
        level = level * jnp.repeat(draws, dims[position] // shards_of).reshape([-1 if axis == position else 1 for axis in range(len(dims))])
    return level


def noise(stream_key, dims, width, bound, cuts=(), held_as=jnp.bfloat16):
    result = width * jax.random.normal(stream_key, dims, jnp.float32)
    if cuts:
        result = result * block_levels(stream_key, dims, cuts, -0.22, 0.18)
    return jnp.clip(result, -bound, bound).astype(held_as)


def bell_draw_with(own_key, extent, deviation, limit, cuts, heavy, kind=jnp.bfloat16):
    drawn = deviation * jax.random.normal(own_key, extent, jnp.float32)
    if cuts:
        drawn = drawn * block_levels(own_key, extent, cuts, -0.22, 0.18)
    return jnp.clip(spiked(drawn, jax.random.fold_in(own_key, 3), *heavy), -limit, limit).astype(kind)


def setup_inputs(seed: int = 0) -> dict:
    keys = jax.random.split(jax.random.key(seed), 25)
    return {
        "tokens": noise(keys[0], (TOKENS, D), 1.0, 6.0, ((0, 32),)),
        "cotangent": bell_draw_with(keys[1], (TOKENS, D), 1.0, 6.0, ((0, 32),), (0, 1, 32, 2.75)),
        "segment_ids": draw_segment_ids(jax.random.fold_in(keys[24], 71), 0),
        "joint_weight": noise(keys[3], (D, 3, D), D ** -0.5, 0.125, ((0, 16), (2, 2)), jnp.float32),
        "dense_weight": noise(keys[4], (D, D), (D // 32) ** -0.5, 0.75, ((0, 16), (1, 2)), jnp.float32),
        "expand_weight": noise(keys[5], (D, FF), D ** -0.5, 0.125, ((0, 16), (1, 2)), jnp.float32),
        "shrink_weight": noise(keys[6], (D, FF), FF ** -0.5, 0.0625, ((0, 16), (1, 2)), jnp.float32),
        "head_bias": noise(keys[7], (HD, 3, HEADS), 0.3, 3.0, ((0, 16), (2, 2)), jnp.float32),
        "unit_bias": noise(keys[8], (HD, FF // HD), 0.3, 3.0, ((0, 16), (1, 2)), jnp.float32),
        "row_vectors": draw_row_vectors(jax.random.fold_in(keys[24], 71), 0),
        "joint_mean": noise(keys[10], (D, 3, D), (0.056 * TOKENS ** 0.5), 32.0, ((0, 16), (2, 2)), jnp.float32),
        "joint_square": jnp.clip(jnp.exp(math.log(434.176) - 1.40534252 * jax.random.uniform(keys[11], (D, 3, D), jnp.float32) ** block_levels(keys[11], (D, 3, D), ((0, 16), (2, 2)), -0.2, 0.2)), 106.496, 434.176),
        "dense_mean": noise(keys[12], (D, D), (0.022 * TOKENS ** 0.5), 12.0, ((0, 16), (1, 2)), jnp.float32),
        "dense_square": jnp.clip(jnp.exp(math.log(68.8128) - 1.3862944 * jax.random.uniform(keys[13], (D, D), jnp.float32) ** block_levels(keys[13], (D, D), ((0, 16), (1, 2)), -0.2, 0.2)), 17.2032, 68.8128),
        "expand_mean": noise(keys[14], (D, FF), (0.033 * TOKENS ** 0.5), 16.0, ((0, 16), (1, 2)), jnp.float32),
        "expand_square": jnp.clip(jnp.exp(math.log(155.648) - 1.375823 * jax.random.uniform(keys[15], (D, FF), jnp.float32) ** block_levels(keys[15], (D, FF), ((0, 16), (1, 2)), -0.2, 0.2)), 39.3216, 155.648),
        "shrink_mean": noise(keys[16], (D, FF), (0.072 * TOKENS ** 0.5), 40.0, ((0, 16), (1, 2)), jnp.float32),
        "shrink_square": jnp.clip(jnp.exp(math.log(729.088) - 1.397594 * jax.random.uniform(keys[17], (D, FF), jnp.float32) ** block_levels(keys[17], (D, FF), ((0, 16), (1, 2)), -0.2, 0.2)), 180.224, 729.088),
        "head_mean": noise(keys[18], (HD, 3, HEADS), (0.056 * TOKENS ** 0.5), 32.0, ((0, 16), (2, 2)), jnp.float32),
        "head_square": jnp.clip(jnp.exp(math.log(434.176) - 1.40534252 * jax.random.uniform(keys[19], (HD, 3, HEADS), jnp.float32) ** block_levels(keys[19], (HD, 3, HEADS), ((0, 16), (2, 2)), -0.2, 0.2)), 106.496, 434.176),
        "unit_mean": noise(keys[20], (HD, FF // HD), (0.033 * TOKENS ** 0.5), 16.0, ((0, 16), (1, 2)), jnp.float32),
        "unit_square": jnp.clip(jnp.exp(math.log(155.648) - 1.375823 * jax.random.uniform(keys[21], (HD, FF // HD), jnp.float32) ** block_levels(keys[21], (HD, FF // HD), ((0, 16), (1, 2)), -0.2, 0.2)), 39.3216, 155.648),
        "rows_mean": noise(keys[22], (4, D), (0.17 * TOKENS ** 0.5), 96.0, ((1, 32),), jnp.float32),
        "rows_square": jnp.clip(jnp.exp(math.log(3850.24) - 1.36524097 * jax.random.uniform(keys[23], (4, D), jnp.float32) ** block_levels(keys[23], (4, D), ((1, 32),), -0.2, 0.2)), 983.04, 3850.24),
    }


@jax.custom_vjp
def low(v):
    return lax.optimization_barrier(v.astype(jnp.bfloat16)).astype(jnp.float32)

@jax.custom_vjp
def low_back(v):
    return v

def low_keep(v):
    return (low(v), None)

def low_pass(kept, grad):
    return (grad,)

def back_keep(v):
    return (v, None)

def back_low(kept, grad):
    return (low(grad),)
low.defvjp(low_keep, low_pass)
low_back.defvjp(back_keep, back_low)
EPS_NORM = 1e-05
BETA_ONE = 0.9
BETA_TWO = 0.95
EPS_ADAM = 1e-08
WEIGHT_DECAY = 0.1
HIGHEST = lax.Precision.HIGHEST

def rotate(vectors, cosine, sine_table):
    half_rot = ROTARY // 2
    lead_half = vectors[..., :half_rot]
    tail_half = vectors[..., half_rot:ROTARY]
    others = vectors[..., ROTARY:]
    return jnp.concatenate([lead_half * cosine - tail_half * sine_table, tail_half * cosine + lead_half * sine_table, others], axis=-1)

def doc_positions(segments):
    row_count = segments.shape[0]
    places = jnp.arange(row_count, dtype=jnp.int32)
    same_doc = segments[:, None] == segments[None, :]
    starts = lax.optimization_barrier(jnp.min(jnp.where(same_doc, places[None, :], row_count), axis=1))
    allowed = same_doc & (places[None, :] <= places[:, None])
    return ((places - starts).astype(jnp.float32), allowed)

def rotary_tables(positions):
    half_rot = ROTARY // 2
    frequency = 10000.0 ** (-jnp.arange(half_rot, dtype=jnp.float32) / half_rot)
    angles = positions[:, None] * frequency[None, :]
    return (jnp.cos(angles)[:, None, :], jnp.sin(angles)[:, None, :])

def adam_update(weight, gradient, moment, square, step_rate, decay_rate):
    new_moment = BETA_ONE * moment + (1.0 - BETA_ONE) * gradient
    new_square = BETA_TWO * square + (1.0 - BETA_TWO) * gradient * gradient
    fix_one = 1.0 - BETA_ONE ** STEP
    fix_two = 1.0 - BETA_TWO ** STEP
    update = new_moment / fix_one / (jnp.sqrt(new_square / fix_two) + EPS_ADAM)
    return (weight - step_rate * (update + decay_rate * weight), new_moment, new_square)

def group_forward(group_inputs, segments, layer):
    gain, shift, dense_bias, shrink_bias, joint, head_shift, dense, expand, unit_shift, shrink = layer
    row_count = group_inputs.shape[0]
    centered = group_inputs - lax.optimization_barrier(jnp.mean(group_inputs, axis=-1, keepdims=True))
    inverse = lax.rsqrt(lax.optimization_barrier(jnp.mean(centered * centered, axis=-1, keepdims=True)) + EPS_NORM)
    normed = low(centered * inverse * gain + shift)
    positions, allowed = doc_positions(segments)
    cosine, sine_table = rotary_tables(positions)
    joint_out = low_back(jnp.einsum('td,djc->tjc', normed, joint, precision=HIGHEST) + head_shift)
    queries = low(rotate(joint_out[:, 0].reshape(row_count, HEADS, HD), cosine, sine_table))
    keys_rot = low(rotate(joint_out[:, 1].reshape(row_count, HEADS, HD), cosine, sine_table))
    values = low(joint_out[:, 2].reshape(row_count, HEADS, HD))
    scores = low_back(jnp.einsum('qhe,khe->hqk', queries, keys_rot, precision=HIGHEST) * HD ** (-0.5))
    attn_probs = jax.nn.softmax(jnp.where(allowed[None], scores, -1e+30), axis=-1)
    context = jnp.einsum('hqk,khe->qhe', low(attn_probs), values, precision=HIGHEST).reshape(row_count, D)
    context = low_back(low(context))
    hidden_pre = low_back(jnp.dot(normed, expand, precision=HIGHEST) + unit_shift)
    hidden = low(jax.nn.gelu(hidden_pre, approximate=True))
    branch = jnp.dot(context, dense.T, precision=HIGHEST) + jnp.dot(hidden, shrink.T, precision=HIGHEST)
    return group_inputs + branch + dense_bias + shrink_bias

def reference(tokens, cotangent, segment_ids, joint_weight, dense_weight, expand_weight, shrink_weight, head_bias, unit_bias, row_vectors, joint_mean, joint_square, dense_mean, dense_square, expand_mean, expand_square, shrink_mean, shrink_square, head_mean, head_square, unit_mean, unit_square, rows_mean, rows_square):
    groups = TOKENS // TOK_DEV
    seg_groups = segment_ids.reshape(groups, TOK_DEV)

    def forward(joint_master, dense_master, expand_master, shrink_master, head_master, unit_master, rows_master, inputs):
        layer = (rows_master[0], rows_master[1], rows_master[2], rows_master[3], low(joint_master), low(head_master).transpose(1, 2, 0).reshape(3, D), low(dense_master), low(expand_master), low(unit_master).T.reshape(FF), low(shrink_master))
        block = jax.checkpoint(group_forward)

        def scan_step(carried, pieces):
            return (carried, block(pieces[0], pieces[1], layer))
        carried, outputs = lax.scan(scan_step, jnp.zeros((), jnp.float32), (inputs.reshape(groups, TOK_DEV, D), seg_groups))
        return outputs.reshape(TOKENS, D)
    live_rows = (segment_ids > 0).astype(jnp.float32)
    output, pullback = jax.vjp(forward, joint_weight, dense_weight, expand_weight, shrink_weight, head_bias, unit_bias, row_vectors, tokens.astype(jnp.float32))
    gradients = pullback(cotangent.astype(jnp.float32) * live_rows[:, None])
    joint_new = adam_update(joint_weight, gradients[0], joint_mean, joint_square, D ** (-0.5), WEIGHT_DECAY)
    dense_new = adam_update(dense_weight, gradients[1], dense_mean, dense_square, (D // 32) ** (-0.5), WEIGHT_DECAY)
    expand_new = adam_update(expand_weight, gradients[2], expand_mean, expand_square, D ** (-0.5), WEIGHT_DECAY)
    shrink_new = adam_update(shrink_weight, gradients[3], shrink_mean, shrink_square, FF ** (-0.5), WEIGHT_DECAY)
    head_new = adam_update(head_bias, gradients[4], head_mean, head_square, 0.1, 0.0)
    unit_new = adam_update(unit_bias, gradients[5], unit_mean, unit_square, 0.1, 0.0)
    rows_new = adam_update(row_vectors, gradients[6], rows_mean, rows_square, 0.1, 0.0)
    return (output.astype(jnp.bfloat16), gradients[7], joint_new[0], joint_new[1], joint_new[2], dense_new[0], dense_new[1], dense_new[2], expand_new[0], expand_new[1], expand_new[2], shrink_new[0], shrink_new[1], shrink_new[2], head_new[0], head_new[1], head_new[2], unit_new[0], unit_new[1], unit_new[2], rows_new[0], rows_new[1], rows_new[2])
```

```python
import functools

import jax
import jax.numpy as jnp
from jax import lax
from jax.sharding import PartitionSpec as P

D = 2048
HD = 64
FF = 8192
ROTARY = 32
STEP = 10


EPS_NORM = 1e-05
BETA_ONE = 0.9
BETA_TWO = 0.95
EPS_ADAM = 1e-08
WEIGHT_DECAY = 0.1


def rotate(vectors, cosine, sine_table):
    half_rot = ROTARY // 2
    lead_half = vectors[..., :half_rot]
    tail_half = vectors[..., half_rot:ROTARY]
    others = vectors[..., ROTARY:]
    return jnp.concatenate(
        [
            lead_half * cosine - tail_half * sine_table,
            tail_half * cosine + lead_half * sine_table,
            others,
        ],
        axis=-1,
    )


def doc_positions(segments):
    row_count = segments.shape[0]
    places = jnp.arange(row_count, dtype=jnp.int32)
    same_doc = segments[:, None] == segments[None, :]
    starts = jnp.min(jnp.where(same_doc, places[None, :], row_count), axis=1)
    allowed = same_doc & (places[None, :] <= places[:, None])
    return ((places - starts).astype(jnp.float32), allowed)


def rotary_tables(positions):
    half_rot = ROTARY // 2
    frequency = 10000.0 ** (-jnp.arange(half_rot, dtype=jnp.float32) / half_rot)
    angles = positions[:, None] * frequency[None, :]
    return (jnp.cos(angles)[:, None, :], jnp.sin(angles)[:, None, :])


def adam_update(weight, gradient, moment, square, step_rate, decay_rate):
    new_moment = BETA_ONE * moment + (1.0 - BETA_ONE) * gradient
    new_square = BETA_TWO * square + (1.0 - BETA_TWO) * gradient * gradient
    fix_one = 1.0 - BETA_ONE**STEP
    fix_two = 1.0 - BETA_TWO**STEP
    update = new_moment / fix_one / (jnp.sqrt(new_square / fix_two) + EPS_ADAM)
    return (weight - step_rate * (update + decay_rate * weight), new_moment, new_square)


def gelu_tanh(values):
    return jax.nn.gelu(values, approximate=True)


AXES = ("dp", "tensor")
LOW = jnp.bfloat16
WIDE = jnp.float32


class Place:
    def __init__(self, dp_size, tensor_size):
        self.rings = dp_size // 4
        self.tensors = tensor_size
        self.index = lax.axis_index("dp")
        self.z = self.index // 4
        self.x = (self.index // 2) % 2
        self.c = self.index % 2
        self.y = lax.axis_index("tensor")

    def move(self, array, z=0, zbit=0, x=0, c=0, y=0):
        pairs = []
        for oz in range(self.rings):
            for ox in range(2):
                for oc in range(2):
                    for oy in range(self.tensors):
                        to_z = ((oz + z) % self.rings) ^ zbit
                        to_dp = (to_z * 2 + (ox ^ x)) * 2 + (oc ^ c)
                        source = ((oz * 2 + ox) * 2 + oc) * self.tensors + oy
                        pairs.append((source, to_dp * self.tensors + (oy ^ y)))
        return lax.ppermute(array, AXES, pairs)


def pick(array, index, axis=0):
    return lax.dynamic_index_in_dim(array, index, axis, keepdims=False)


def put_rows(buffer, block, row):
    return lax.dynamic_update_slice_in_dim(buffer, block, row, 0)


def in_order(place, near, side_c, side_x, side_xc):
    zero = [jnp.where(place.c == 0, near, side_c), jnp.where(place.c == 0, side_c, near)]
    one = [jnp.where(place.c == 0, side_x, side_xc), jnp.where(place.c == 0, side_xc, side_x)]
    first = [jnp.where(place.x == 0, a, b) for a, b in zip(zero, one)]
    second = [jnp.where(place.x == 0, b, a) for a, b in zip(zero, one)]
    return first + second


def spread_columns(place, low_parts):
    def half(which):
        return jnp.concatenate([pick(p, which, 1) for p in low_parts], axis=-1)

    kept, sent = half(place.x), half(1 - place.x)
    got = place.move(sent.transpose(1, 0, 2), x=1)
    kept = kept.transpose(1, 0, 2)
    across = place.move(jnp.stack([pick(kept, 1 - place.c), pick(got, 1 - place.c)]), c=1)
    return jnp.concatenate(
        in_order(place, pick(kept, place.c), across[0], pick(got, place.c), across[1]), axis=0
    )


def ring_gather(place, block):
    rows = block.shape[0]
    n = place.rings
    whole = jnp.zeros((n * rows, block.shape[1]), block.dtype)
    whole = put_rows(whole, block, place.z * rows)
    up = down = block
    for step in range(1, n // 2 + 1):
        above, below = ((place.z + step) % n) * rows, ((place.z - step) % n) * rows
        if step < n // 2:
            up, down = place.move(up, z=1), place.move(down, z=-1)
            whole = put_rows(put_rows(whole, up, below), down, above)
        else:
            half = rows // 2
            whole = put_rows(whole, place.move(up[:half], z=1), below)
            whole = put_rows(whole, place.move(down[half:], z=-1), above + half)
    return whole


def ring_reduce(place, parts):
    n = place.rings
    rows = parts.shape[0] // n
    half = rows // 2

    def block(step):
        return lax.dynamic_slice_in_dim(parts, ((place.z + step) % n) * rows, rows, 0)

    far = block(n // 2)
    up = place.move(far[:half], z=1)
    down = place.move(far[half:], z=-1)
    for step in range(n // 2 - 1, 0, -1):
        above, below = block(step).astype(WIDE), block(-step).astype(WIDE)
        if step == n // 2 - 1:
            above = jnp.concatenate([above[:half] + up.astype(WIDE), above[half:]])
            below = jnp.concatenate([below[:half], below[half:] + down.astype(WIDE)])
        else:
            above, below = above + up.astype(WIDE), below + down.astype(WIDE)
        up = place.move(above.astype(LOW), z=1)
        down = place.move(below.astype(LOW), z=-1)
    return block(0).astype(WIDE) + up.astype(WIDE) + down.astype(WIDE)


def return_columns(place, summed):
    rows = summed.shape[0] // 4
    blocks = summed.astype(LOW).reshape(2, 2, rows, -1)
    across = place.move(pick(blocks, 1 - place.c, 1), c=1)
    mine = pick(blocks, place.c, 1)
    got = place.move(jnp.stack([pick(mine, 1 - place.x), pick(across, 1 - place.x)]), x=1)
    pieces = in_order(place, pick(mine, place.x), pick(across, place.x), got[0], got[1])
    return jnp.stack(pieces, axis=1)


def plane_gather(place, rows):
    half = rows.shape[0] // 2
    by_x = place.move(rows, x=1)
    by_y = place.move(rows, y=1)
    corner = jnp.concatenate([place.move(by_x[:half], y=1), place.move(by_y[half:], x=1)])

    def by_place(same, other):
        return jnp.where(place.y == 0, jnp.stack([same, other]), jnp.stack([other, same]))

    near = by_place(rows, by_y)
    side = by_place(by_x, corner)
    across = place.move(jnp.stack([near, side]), c=1)
    pieces = in_order(place, near, across[0], side, across[1])
    return jnp.concatenate(pieces).reshape(-1, rows.shape[1])


def plane_reduce(place, parts):
    rows = parts.shape[0] // 8
    half = rows // 2
    low = parts.astype(LOW).reshape(2, 2, 2, rows, -1)
    got = place.move(pick(low, 1 - place.c, 1), c=1)
    both = (pick(low, place.c, 1).astype(WIDE) + got.astype(WIDE)).astype(LOW)
    first, second = both[:, :, :half], both[:, :, half:]
    got_x = place.move(pick(first, 1 - place.x, 0), x=1)
    got_y = place.move(pick(second, 1 - place.y, 1), y=1)
    first = pick(first, place.x, 0).astype(WIDE) + got_x.astype(WIDE)
    second = pick(second, place.y, 1).astype(WIDE) + got_y.astype(WIDE)
    last_y = place.move(pick(first, 1 - place.y).astype(LOW), y=1)
    last_x = place.move(pick(second, 1 - place.x).astype(LOW), x=1)
    return jnp.concatenate(
        [
            pick(first, place.y) + last_y.astype(WIDE),
            pick(second, place.x) + last_x.astype(WIDE),
        ]
    )


def gather_small(place, vector):
    whole = vector[None]

    def join(got, bit):
        return jnp.where(
            bit == 0, jnp.concatenate([whole, got]), jnp.concatenate([got, whole])
        )

    whole = join(place.move(whole, y=1), place.y)
    whole = join(place.move(whole, c=1), place.c)
    whole = join(place.move(whole, x=1), place.x)
    bit = 1
    while bit < place.rings:
        whole = join(place.move(whole, zbit=bit), (place.z // bit) % 2)
        bit *= 2
    return whole


def reduce_small(place, own, shared):
    width = own.shape[0]
    both = jnp.concatenate([own, shared])
    got = place.move(both, c=1)
    own = jnp.where(
        place.c == 0, jnp.stack([own, got[:width]]), jnp.stack([got[:width], own])
    )
    shared = shared + got[width:]
    got = place.move(jnp.concatenate([own.reshape(-1), shared]), x=1)
    other = got[: 2 * width].reshape(2, width)
    own = jnp.where(place.x == 0, jnp.concatenate([own, other]), jnp.concatenate([other, own]))
    shared = shared + got[2 * width :]
    shared = shared + place.move(shared, y=1)
    both = jnp.concatenate([own.reshape(-1), shared])
    bit = 1
    while bit < place.rings:
        both = both + place.move(both, zbit=bit)
        bit *= 2
    return both[: 4 * width].reshape(4, width), both[4 * width :]


def attention_back(
    d_context, query_rot, key_rot, value_low, allowed, log_total, cosine, sine_table
):
    score_scale = HD ** (-0.5)
    scores = (
        jnp.einsum("bqhe,bkhe->bhqk", query_rot, key_rot, preferred_element_type=WIDE)
        * score_scale
    )
    attn_probs = jnp.where(allowed[:, None], jnp.exp(scores - log_total), 0.0)
    d_probs = jnp.einsum("bqhe,bkhe->bhqk", d_context, value_low, preferred_element_type=WIDE)
    delta = jnp.sum(attn_probs * d_probs, axis=-1, keepdims=True)
    d_scores = (attn_probs * (d_probs - delta)).astype(LOW)
    d_query = (
        jnp.einsum("bhqk,bkhe->bqhe", d_scores, key_rot, preferred_element_type=WIDE)
        * score_scale
    )
    d_key = (
        jnp.einsum("bhqk,bqhe->bkhe", d_scores, query_rot, preferred_element_type=WIDE)
        * score_scale
    )
    d_value = jnp.einsum(
        "bhqk,bqhe->bkhe", attn_probs.astype(LOW), d_context, preferred_element_type=WIDE
    )
    stacked = jnp.stack(
        [rotate(d_query, cosine, -sine_table), rotate(d_key, cosine, -sine_table), d_value], axis=2
    )
    return stacked.reshape(-1, 3 * stacked.shape[3] * stacked.shape[4]).astype(LOW)


def body(
    dp_size,
    tensor_size,
    tokens,
    cotangent,
    segment_ids,
    joint_weight,
    dense_weight,
    expand_weight,
    shrink_weight,
    head_bias,
    unit_bias,
    row_vectors,
    joint_mean,
    joint_square,
    dense_mean,
    dense_square,
    expand_mean,
    expand_square,
    shrink_mean,
    shrink_square,
    head_mean,
    head_square,
    unit_mean,
    unit_square,
    rows_mean,
    rows_square,
):
    place = Place(dp_size, tensor_size)
    devices = dp_size * tensor_size
    my_rows = tokens.shape[0]
    features = tokens.shape[1]
    group_slots = segment_ids.shape[0]
    shard_rows = joint_weight.shape[0]
    heads = head_bias.shape[2] // 4
    units = unit_bias.shape[1] // 4
    joint_width, unit_width = heads * HD, units * HD

    small = gather_small(
        place,
        jnp.concatenate(
            [
                row_vectors.reshape(-1),
                head_bias.reshape(-1),
                unit_bias.reshape(-1),
                segment_ids.astype(WIDE),
            ]
        ),
    )
    cuts = [row_vectors.size, row_vectors.size + head_bias.size]
    cuts.append(cuts[1] + unit_bias.size)
    rows_small, head_small, unit_small, ids_small = jnp.split(small, cuts, axis=1)
    row_whole = rows_small.reshape(devices, 4, -1).transpose(1, 0, 2).reshape(4, features)
    quarter = place.x * 2 + place.c
    head_small = pick(head_small.reshape((dp_size, tensor_size) + head_bias.shape), place.y, 1)
    head_low = lax.dynamic_slice_in_dim(head_small, quarter * heads, heads, 3).reshape(HD, 3, heads)
    head_shift = head_low.astype(LOW).astype(WIDE).transpose(1, 2, 0).reshape(-1)
    unit_small = pick(unit_small.reshape((dp_size, tensor_size) + unit_bias.shape), place.y, 1)
    unit_low = lax.dynamic_slice_in_dim(unit_small, quarter * units, units, 2).reshape(HD, units)
    unit_shift = unit_low.astype(LOW).astype(WIDE).T.reshape(-1)
    ids = lax.dynamic_slice_in_dim(
        ids_small.reshape(place.rings * 4, tensor_size, group_slots)[:, 0], place.z * 4, 4, 0
    )

    def columns(weight, kinds):
        low = weight.astype(LOW).reshape(shard_rows, kinds, 2, 2, -1)
        return low.transpose(0, 2, 3, 1, 4).reshape(shard_rows, 2, 2, -1)

    joint = ring_gather(place, spread_columns(place, [columns(joint_weight, 3)]))
    inputs_all = plane_gather(place, tokens)
    expand = ring_gather(place, spread_columns(place, [columns(expand_weight, 1)]))
    back = ring_gather(
        place, spread_columns(place, [columns(dense_weight, 1), columns(shrink_weight, 1)])
    )
    my_ids = lax.dynamic_slice_in_dim(segment_ids, place.y * my_rows, my_rows)
    masked = cotangent * (my_ids > 0).astype(LOW)[:, None]
    grad_all = plane_gather(place, masked)

    def unit_of(rows):
        rows = rows.astype(WIDE)
        centered = rows - jnp.mean(rows, axis=-1, keepdims=True)
        inverse = lax.rsqrt(jnp.mean(centered * centered, axis=-1, keepdims=True) + EPS_NORM)
        return centered * inverse, inverse

    gain, shift = row_whole[0], row_whole[1]
    unit_all = unit_of(inputs_all)[0]
    normed = (unit_all * gain + shift).astype(LOW)
    positions, allowed = jax.vmap(doc_positions)(ids)
    cosine, sine_table = jax.vmap(rotary_tables)(positions)

    joint_out = jnp.dot(normed, joint, preferred_element_type=WIDE) + head_shift
    joint_out = joint_out.reshape(4, group_slots, 3, heads, HD)
    query_rot = rotate(joint_out[:, :, 0], cosine, sine_table).astype(LOW)
    key_rot = rotate(joint_out[:, :, 1], cosine, sine_table).astype(LOW)
    value_low = joint_out[:, :, 2].astype(LOW)
    scores = jnp.einsum("bqhe,bkhe->bhqk", query_rot, key_rot, preferred_element_type=WIDE)
    scores = jnp.where(allowed[:, None], scores * HD ** (-0.5), -1e30)
    row_top = jnp.max(scores, axis=-1, keepdims=True)
    exp_scores = jnp.exp(scores - row_top)
    row_total = jnp.sum(exp_scores, axis=-1, keepdims=True)
    attn_probs = exp_scores / row_total
    log_total = row_top + jnp.log(row_total)
    context = jnp.einsum(
        "bhqk,bkhe->bqhe", attn_probs.astype(LOW), value_low, preferred_element_type=WIDE
    )
    context = context.reshape(-1, joint_width).astype(LOW)

    hidden_pre = jnp.dot(normed, expand, preferred_element_type=WIDE) + unit_shift
    hidden_full, gelu_back = jax.vjp(gelu_tanh, hidden_pre)
    feed = jnp.concatenate([context, hidden_full.astype(LOW)], axis=1)
    d_back = lax.dot_general(grad_all, feed, (((0,), (0,)), ((), ())), preferred_element_type=WIDE)
    g_back = ring_reduce(place, d_back.astype(LOW))
    d_feed = jnp.dot(grad_all, back, preferred_element_type=WIDE)
    d_context = d_feed[:, :joint_width].astype(LOW).reshape(4, group_slots, heads, HD)
    d_pre = gelu_back(d_feed[:, joint_width:])[0].astype(LOW)
    d_expand = lax.dot_general(normed, d_pre, (((0,), (0,)), ((), ())), preferred_element_type=WIDE)
    g_expand = ring_reduce(place, d_expand.astype(LOW))
    d_joint = attention_back(
        d_context, query_rot, key_rot, value_low, allowed, log_total, cosine, sine_table
    )
    d_joint_w = lax.dot_general(
        normed, d_joint, (((0,), (0,)), ((), ())), preferred_element_type=WIDE
    )
    g_joint = ring_reduce(place, d_joint_w.astype(LOW))
    across = (((1,), (1,)), ((), ()))
    d_normed = lax.dot_general(
        d_joint, joint, across, preferred_element_type=WIDE
    ) + lax.dot_general(d_pre, expand, across, preferred_element_type=WIDE)
    branch = lax.dot_general(feed, back, across, preferred_element_type=WIDE)

    own_sums = jnp.concatenate(
        [jnp.sum(d_joint, axis=0, dtype=WIDE), jnp.sum(d_pre, axis=0, dtype=WIDE)]
    )
    row_sums = jnp.concatenate(
        [
            jnp.sum(d_normed * unit_all, axis=0),
            jnp.sum(d_normed, axis=0),
            jnp.sum(masked, axis=0, dtype=WIDE),
        ]
    )
    own_sums, row_sums = reduce_small(place, own_sums, row_sums)
    branch = plane_reduce(place, branch)
    d_normed = plane_reduce(place, d_normed)

    inputs = tokens.astype(WIDE)
    layer_output = (inputs + branch + row_whole[2] + row_whole[3]).astype(LOW)
    unit_rows, inverse = unit_of(tokens)
    d_unit_rows = d_normed * gain
    d_inputs = inverse * (
        d_unit_rows
        - jnp.mean(d_unit_rows, axis=-1, keepdims=True)
        - unit_rows * jnp.mean(d_unit_rows * unit_rows, axis=-1, keepdims=True)
    )
    input_grad = masked.astype(WIDE) + d_inputs

    g_back = return_columns(place, g_back).astype(WIDE)
    g_expand = return_columns(place, g_expand).astype(WIDE).reshape(expand_weight.shape)
    g_joint = return_columns(place, g_joint).astype(WIDE)
    g_dense = g_back[:, :, :joint_width].reshape(dense_weight.shape)
    g_shrink = g_back[:, :, joint_width:].reshape(shrink_weight.shape)
    g_joint = g_joint.reshape(shard_rows, 4, 3, -1).transpose(0, 2, 1, 3).reshape(joint_weight.shape)

    features_here = HD // dp_size
    g_head = own_sums[:, : 3 * joint_width].reshape(4, 3, heads, HD)
    g_head = lax.dynamic_slice_in_dim(g_head, place.index * features_here, features_here, 3)
    g_head = g_head.transpose(3, 1, 0, 2).reshape(head_bias.shape)
    g_unit = own_sums[:, 3 * joint_width :].reshape(4 * units, HD)
    g_unit = lax.dynamic_slice_in_dim(g_unit, place.index * features_here, features_here, 1).T
    row_sums = row_sums.reshape(3, features)
    row_width = row_vectors.shape[1]
    g_rows = lax.dynamic_slice_in_dim(
        row_sums, (place.index * tensor_size + place.y) * row_width, row_width, 1
    )
    g_rows = jnp.concatenate([g_rows, g_rows[2:]])
    joint_new = adam_update(
        joint_weight, g_joint, joint_mean, joint_square, D ** (-0.5), WEIGHT_DECAY
    )
    dense_new = adam_update(
        dense_weight, g_dense, dense_mean, dense_square, (D // 32) ** (-0.5), WEIGHT_DECAY
    )
    expand_new = adam_update(
        expand_weight, g_expand, expand_mean, expand_square, D ** (-0.5), WEIGHT_DECAY
    )
    shrink_new = adam_update(
        shrink_weight, g_shrink, shrink_mean, shrink_square, FF ** (-0.5), WEIGHT_DECAY
    )
    head_new = adam_update(head_bias, g_head, head_mean, head_square, 0.1, 0.0)
    unit_new = adam_update(unit_bias, g_unit, unit_mean, unit_square, 0.1, 0.0)
    rows_new = adam_update(row_vectors, g_rows, rows_mean, rows_square, 0.1, 0.0)
    return (
        layer_output,
        input_grad,
        joint_new[0],
        joint_new[1],
        joint_new[2],
        dense_new[0],
        dense_new[1],
        dense_new[2],
        expand_new[0],
        expand_new[1],
        expand_new[2],
        shrink_new[0],
        shrink_new[1],
        shrink_new[2],
        head_new[0],
        head_new[1],
        head_new[2],
        unit_new[0],
        unit_new[1],
        unit_new[2],
        rows_new[0],
        rows_new[1],
        rows_new[2],
    )


def solution(mesh):
    return jax.shard_map(
        functools.partial(body, mesh.shape["dp"], mesh.shape["tensor"]),
        mesh=mesh,
        in_specs=(
            P(("dp", "tensor"), None),
            P(("dp", "tensor"), None),
            P("dp"),
            P("dp", None, "tensor"),
            P("dp", "tensor"),
            P("dp", "tensor"),
            P("dp", "tensor"),
            P("dp", None, "tensor"),
            P("dp", "tensor"),
            P(None, ("dp", "tensor")),
            P("dp", None, "tensor"),
            P("dp", None, "tensor"),
            P("dp", "tensor"),
            P("dp", "tensor"),
            P("dp", "tensor"),
            P("dp", "tensor"),
            P("dp", "tensor"),
            P("dp", "tensor"),
            P("dp", None, "tensor"),
            P("dp", None, "tensor"),
            P("dp", "tensor"),
            P("dp", "tensor"),
            P(None, ("dp", "tensor")),
            P(None, ("dp", "tensor")),
        ),
        out_specs=(
            P(("dp", "tensor"), None),
            P(("dp", "tensor"), None),
            P("dp", None, "tensor"),
            P("dp", None, "tensor"),
            P("dp", None, "tensor"),
            P("dp", "tensor"),
            P("dp", "tensor"),
            P("dp", "tensor"),
            P("dp", "tensor"),
            P("dp", "tensor"),
            P("dp", "tensor"),
            P("dp", "tensor"),
            P("dp", "tensor"),
            P("dp", "tensor"),
            P("dp", None, "tensor"),
            P("dp", None, "tensor"),
            P("dp", None, "tensor"),
            P("dp", "tensor"),
            P("dp", "tensor"),
            P("dp", "tensor"),
            P(None, ("dp", "tensor")),
            P(None, ("dp", "tensor")),
            P(None, ("dp", "tensor")),
        ),
        check_vma=False,
    )
```

```python
import functools
import math

import jax
import jax.numpy as jnp
from jax import lax
from jax.experimental import pallas as pl
from jax.experimental.pallas import tpu as pltpu
from jax.sharding import PartitionSpec as P

D = 2048
HD = 64
FF = 8192
ROTARY = 32
STEP = 10


EPS_NORM = 1e-05
BETA_ONE = 0.9
BETA_TWO = 0.95
EPS_ADAM = 1e-08
WEIGHT_DECAY = 0.1


def doc_positions(segments):
    row_count = segments.shape[0]
    places = jnp.arange(row_count, dtype=jnp.int32)
    same_doc = segments[:, None] == segments[None, :]
    starts = jnp.min(jnp.where(same_doc, places[None, :], row_count), axis=1)
    allowed = same_doc & (places[None, :] <= places[:, None])
    return ((places - starts).astype(jnp.float32), allowed)


def adam_update(weight, gradient, moment, square, step_rate, decay_rate):
    new_moment = BETA_ONE * moment + (1.0 - BETA_ONE) * gradient
    new_square = BETA_TWO * square + (1.0 - BETA_TWO) * gradient * gradient
    fix_one = 1.0 - BETA_ONE**STEP
    fix_two = 1.0 - BETA_TWO**STEP
    update = new_moment / fix_one / (jnp.sqrt(new_square / fix_two) + EPS_ADAM)
    return (weight - step_rate * (update + decay_rate * weight), new_moment, new_square)


AXES = ("dp", "tensor")
LOW = jnp.bfloat16
WIDE = jnp.float32


def after(array, *others):
    others = [o for o in others if o is not None]
    return lax.optimization_barrier((array, *others))[0] if others else array


def cost(flops, nbytes):
    return pl.CostEstimate(flops=int(flops) >> 10, bytes_accessed=int(nbytes) >> 10, transcendentals=0)


class Place:
    def __init__(self, dp_size, tensor_size):
        count = dp_size.bit_length() - 1
        self.dp_size, self.tensors, self.count = dp_size, tensor_size, count
        self.core, self.side = 1, 1 << (count - 2)
        self.ring = [1 << b for b in range(count - 1, 0, -1) if 1 << b != self.side]
        self.index = lax.axis_index("dp")
        self.y = lax.axis_index("tensor")
        self.quarter = self.bit(self.side) * 2 + self.bit(self.core)
        self.masks = [0]
        for bit in reversed(self.ring):
            self.masks = self.masks + [m | bit for m in self.masks]
        self.last = {}

    def bit(self, mask):
        return (self.index // mask) % 2

    def move(self, array, mask, y=0, lane=None):
        pairs = []
        for dp in range(self.dp_size):
            for oy in range(self.tensors):
                pairs.append((dp * self.tensors + oy, (dp ^ mask) * self.tensors + (oy ^ y)))
        if lane is not None:
            array = after(array, self.last.get(lane))
        got = lax.ppermute(array, AXES, pairs)
        if lane is not None:
            self.last[lane] = got
        return got

    def to_own_order(self, array):
        lead = array.shape[:-1]
        split = array.reshape(lead + (2,) * self.count + (-1,))
        first = len(lead)
        ring_axes = [first + self.count - bit.bit_length() for bit in self.ring]
        for bit, axis in zip(self.ring, ring_axes):
            split = jnp.where(self.bit(bit) == 0, split, jnp.flip(split, axis))
        rest = [first + b for b in range(self.count + 1) if first + b not in ring_axes]
        split = split.transpose(list(range(first)) + ring_axes + rest)
        return split.reshape(array.shape)

    def to_index_order(self, array):
        lead = array.shape[:-1]
        split = array.reshape(lead + (2,) * self.count + (-1,))
        first = len(lead)
        ring_axes = [first + self.count - bit.bit_length() for bit in self.ring]
        rest = [first + b for b in range(self.count + 1) if first + b not in ring_axes]
        order = list(range(first)) + ring_axes + rest
        split = split.transpose([order.index(i) for i in range(len(order))])
        for bit, axis in zip(self.ring, ring_axes):
            split = jnp.where(self.bit(bit) == 0, split, jnp.flip(split, axis))
        return split.reshape(array.shape)


def pick(array, index, axis=0):
    return lax.dynamic_index_in_dim(array, index, axis, keepdims=False)


def swap_quarters(place, pieces):
    return [
        pieces[0],
        place.move(pieces[1], place.core),
        place.move(pieces[2], place.side),
        place.move(pieces[3], place.side | place.core),
    ]


def arrange_kernel(back, statics, own_ref, array_ref, out_ref):
    width = array_ref.shape[1] // len(statics)
    for r, static in enumerate(statics):
        at = pl.multiple_of((own_ref[0] ^ static) * width, 128)
        here = slice(r * width, (r + 1) * width)
        if back:
            out_ref[:, pl.ds(at, width)] = array_ref[:, here]
        else:
            out_ref[:, here] = array_ref[:, pl.ds(at, width)]


def arrange(place, array, back=False):
    if array.shape[1] // place.dp_size % 128:
        return place.to_index_order(array) if back else place.to_own_order(array)
    ring = sum(place.ring)
    inner = (0, place.core, place.side, place.side | place.core)
    statics = [mask | i for mask in place.masks for i in inner]
    return pl.pallas_call(
        functools.partial(arrange_kernel, back, statics),
        in_specs=[
            pl.BlockSpec(memory_space=pltpu.SMEM),
            pl.BlockSpec(memory_space=pltpu.VMEM),
        ],
        out_specs=pl.BlockSpec(memory_space=pltpu.VMEM),
        out_shape=jax.ShapeDtypeStruct(array.shape, array.dtype),
        compiler_params=pltpu.CompilerParams(vmem_limit_bytes=24 << 20),
        cost_estimate=cost(0, 4 * array.size),
    )((place.index & ring).reshape(1), array)


class Gather:
    def __init__(self, place, block, *halves):
        self.place, self.halves = place, halves
        first, second = place.ring[:2]
        self.both = first | second
        self.first, self.second = first, second
        self.parts = {0: [block], first: [None, None], second: [None], self.both: [None, None]}

    def along_first(self, half, *others):
        got = self.place.move(after(self.halves[half], *others), self.first)
        self.parts[self.first][half] = got
        return got

    def along_second(self, *others):
        got = self.place.move(after(self.parts[0][0], *others), self.second)
        self.parts[self.second][0] = got
        return got

    def onward(self, half, *others):
        got = self.place.move(after(self.parts[self.first][half], *others), self.second)
        self.parts[self.both][half] = got
        return got

    def whole(self):
        for bit in self.place.ring[2:]:
            for mask in list(self.parts):
                self.parts[mask | bit] = [self.place.move(p, bit) for p in self.parts[mask]]
        return [part for m in self.place.masks for part in self.parts[m]]


class Reduce:
    def __init__(self, place, *pairs):
        self.place = place
        self.far, self.near = gradient_blocks(place, *pairs)

    def along(self, number, *others, before=()):
        got = self.place.move(after(self.far, *others), self.place.ring[number])
        total = after(self.near, *before).astype(WIDE) + got.astype(WIDE)
        total = total.astype(LOW)
        if number == -1:
            number = len(self.place.ring) - 1
        if number:
            blocks = total.reshape(1 << number, -1, total.shape[1])
            self.far = blocks[1::2].reshape(-1, total.shape[1])
            self.near = blocks[0::2].reshape(-1, total.shape[1])
        self.total = total
        return total

    def rest(self):
        for number in range(len(self.place.ring) - 2, 0, -1):
            self.along(number)


class GroupSum:
    def __init__(self, place, far, near, eighths):
        self.place, self.far, self.near, self.eighths = place, far, near, eighths

    def by_core(self, *others):
        got = self.place.move(after(self.far, *others), self.place.core)
        rows = self.near.shape[0] // 4
        both = (self.near.astype(WIDE) + got.astype(WIDE)).reshape(2, 2, rows, -1)
        cut = rows * self.eighths // 8
        self.first, self.second = both[:, :, :cut], both[:, :, cut:]
        self.sent = [self.first[1].astype(LOW), self.second[:, 1].astype(LOW)]
        return self.sent

    def hop(self, *others):
        place, (first, second) = self.place, self.sent
        got_side = place.move(after(first, *others), place.side)
        got_y = place.move(after(second, *others), 0, 1)
        self.first = self.first[0] + got_side.astype(WIDE)
        self.second = self.second[:, 0] + got_y.astype(WIDE)
        self.sent = [self.first[1].astype(LOW), self.second[1].astype(LOW)]
        return self.sent

    def last_hop(self, *others):
        place, (first, second) = self.place, self.sent
        got_y = place.move(after(first, *others), 0, 1)
        got_side = place.move(after(second, *others), place.side)
        return jnp.concatenate(
            [self.first[0] + got_y.astype(WIDE), self.second[0] + got_side.astype(WIDE)]
        )


class SmallGather:
    def __init__(self, place, vector):
        self.place, self.rows, self.bits = place, vector[None], []

    def step(self, mask, y=0, *others):
        got = self.place.move(after(self.rows, *others), mask, y)
        self.rows = jnp.concatenate([self.rows, got])
        self.bits.append(2 * mask + y)
        return self.rows

    def whole(self):
        place = self.place
        for b in range(place.count):
            if 2 << b not in self.bits:
                self.step(1 << b)
        length = self.rows.shape[1]
        split = self.rows.reshape((2,) * len(self.bits) + (length,))
        axes = []
        for b in [2 << b for b in range(place.count - 1, -1, -1)] + [1]:
            axis = len(self.bits) - 1 - self.bits.index(b)
            own = place.y if b == 1 else place.bit(b // 2)
            split = jnp.where(own == 0, split, jnp.flip(split, axis))
            axes.append(axis)
        return split.transpose(axes + [len(axes)]).reshape(-1, length)


def reduce_small(place, own, shared):
    width = own.shape[0]
    core, side = place.bit(place.core), place.bit(place.side)
    got = place.move(jnp.concatenate([own, shared]), place.core)
    own, other = own[None], got[None, :width]
    own = jnp.where(core == 0, jnp.concatenate([own, other]), jnp.concatenate([other, own]))
    shared = shared + got[width:]
    got = place.move(jnp.concatenate([own.reshape(-1), shared]), place.side)
    other = got[: 2 * width].reshape(2, width)
    own = jnp.where(side == 0, jnp.concatenate([own, other]), jnp.concatenate([other, own]))
    shared = shared + got[2 * width :]
    shared = shared + place.move(shared, 0, 1)
    both = jnp.concatenate([own.reshape(-1), shared])
    for bit in place.ring:
        both = both + place.move(both, bit)
    return both[: 4 * width].reshape(4, width), both[4 * width :]


FLIPS = (0, 1, 2, 3)


def pack_kernel(quarter_ref, *refs):
    shards, outs = refs[: len(refs) - 4], refs[len(refs) - 4 :]
    for flip, out in zip(FLIPS, outs):
        quarter = quarter_ref[0] ^ flip
        column = 0
        for shard in shards:
            width = shard.shape[2] // 4
            for kind in range(shard.shape[0]):
                at = pl.multiple_of(quarter * width, 128)
                out[:, column : column + width] = shard[kind, :, pl.ds(at, width)].astype(LOW)
                column += width


def pack(place, *shards):
    rows = shards[0].shape[1]
    width = sum(s.shape[0] * s.shape[2] for s in shards) // 4
    return pl.pallas_call(
        pack_kernel,
        in_specs=[pl.BlockSpec(memory_space=pltpu.SMEM)]
        + [pl.BlockSpec(memory_space=pltpu.VMEM)] * len(shards),
        out_specs=[pl.BlockSpec(memory_space=pltpu.VMEM)] * 4,
        out_shape=[jax.ShapeDtypeStruct((rows, width), LOW)] * 4,
        compiler_params=pltpu.CompilerParams(vmem_limit_bytes=24 << 20),
        cost_estimate=cost(0, 24 * rows * width),
    )(place.quarter.reshape(1), *shards)


def stack_kernel(count, quarter_ref, *refs):
    pieces, outs = refs[:count], refs[count:]
    third = len(outs) // 3
    outs, halves = outs[:third], (outs[third : 2 * third], outs[2 * third :])
    rows = sum(piece.shape[0] for piece in pieces) // 4
    flip = 0
    for piece in pieces:
        for part in range(piece.shape[0] // rows):
            at = pl.multiple_of((quarter_ref[0] ^ flip) * rows, 16)
            column = 0
            for out in outs:
                width = out.shape[1]
                out[pl.ds(at, rows), :] = piece[
                    part * rows : (part + 1) * rows, column : column + width
                ]
                column += width
            flip += 1
    for out, early, late in zip(outs, *halves):
        early[...] = out[: 2 * rows]
        late[...] = out[2 * rows :]


def stack(place, pieces, widths):
    rows = sum(piece.shape[0] for piece in pieces)
    outs = pl.pallas_call(
        functools.partial(stack_kernel, len(pieces)),
        in_specs=[pl.BlockSpec(memory_space=pltpu.SMEM)]
        + [pl.BlockSpec(memory_space=pltpu.VMEM)] * len(pieces),
        out_specs=[pl.BlockSpec(memory_space=pltpu.VMEM)] * (3 * len(widths)),
        out_shape=[
            jax.ShapeDtypeStruct((r, w), LOW) for r in (rows, rows // 2, rows // 2) for w in widths
        ],
        compiler_params=pltpu.CompilerParams(vmem_limit_bytes=24 << 20),
        cost_estimate=cost(0, 4 * rows * sum(widths)),
    )(place.quarter.reshape(1), *pieces)
    return list(zip(outs[: len(widths)], outs[len(widths) : 2 * len(widths)], outs[-len(widths) :]))


def adam_kernel(step_rate, column, quarter_ref, near_ref, core_ref, side_ref, both_ref, *refs):
    weight, moment, square, new_weight, new_moment, new_square = refs
    distance = pl.program_id(0) ^ quarter_ref[0]
    for flip, piece in zip(FLIPS, (near_ref, core_ref, side_ref, both_ref)):

        @pl.when(distance == flip)
        def _():
            width = weight.shape[2]
            for kind in range(weight.shape[0]):
                start = column + kind * width
                results = adam_update(
                    weight[kind],
                    piece[:, start : start + width].astype(WIDE),
                    moment[kind],
                    square[kind],
                    step_rate,
                    WEIGHT_DECAY,
                )
                new_weight[kind], new_moment[kind], new_square[kind] = results


def adam_shard(place, pieces, column, weight, moment, square, step_rate):
    kinds, rows, width = weight.shape
    block = pl.BlockSpec((kinds, rows, width // 4), lambda q: (0, 0, q))
    return pl.pallas_call(
        functools.partial(adam_kernel, step_rate, column),
        grid=(4,),
        in_specs=[pl.BlockSpec(memory_space=pltpu.SMEM)]
        + [pl.BlockSpec(pieces[0].shape, lambda q: (0, 0))] * 4
        + [block] * 3,
        out_specs=[block] * 3,
        out_shape=[jax.ShapeDtypeStruct(weight.shape, WIDE)] * 3,
        compiler_params=pltpu.CompilerParams(vmem_limit_bytes=32 << 20),
        cost_estimate=cost(20 * weight.size, 26 * weight.size),
    )(place.quarter.reshape(1), *pieces, weight, moment, square)


def join_kernel(starts, *refs):
    arrays, out = refs[:-1], refs[-1]
    step = pl.program_id(0)
    for array, start, end in zip(arrays, starts, starts[1:]):

        @pl.when((step >= start) & (step < end))
        def _():
            out[...] = array[...]


def join(*arrays):
    tile = arrays[0].shape[0] // 2
    starts = [0]
    for array in arrays:
        starts.append(starts[-1] + array.shape[0] // tile)
    width = arrays[0].shape[1]

    def spec(start, end):
        return pl.BlockSpec((tile, width), lambda i: (jnp.clip(i - start, 0, end - start - 1), 0))

    return pl.pallas_call(
        functools.partial(join_kernel, starts),
        grid=(starts[-1],),
        in_specs=[spec(*ends) for ends in zip(starts, starts[1:])],
        out_specs=pl.BlockSpec((tile, width), lambda i: (i, 0)),
        out_shape=jax.ShapeDtypeStruct((starts[-1] * tile, width), arrays[0].dtype),
        compiler_params=pltpu.CompilerParams(vmem_limit_bytes=32 << 20),
        cost_estimate=cost(0, 4 * starts[-1] * tile * width),
    )(*arrays)


def norm_kernel(count, *refs):
    pieces, far_ref, vectors_ref, normed_ref = refs[:count], *refs[count:]

    def write(ref):
        rows = ref[...].astype(WIDE)
        centered = rows - jnp.mean(rows, axis=-1, keepdims=True)
        inverse = lax.rsqrt(jnp.mean(centered * centered, axis=-1, keepdims=True) + EPS_NORM)
        normed_ref[...] = (centered * inverse * vectors_ref[0:1] + vectors_ref[1:2]).astype(LOW)

    step = pl.program_id(0)
    for i, piece in enumerate(pieces):
        pl.when(step == i)(functools.partial(write, piece))
    pl.when(step >= count)(functools.partial(write, far_ref))


def norm(pieces, far, vectors):
    rows, features = pieces[0].shape
    count = len(pieces)
    return pl.pallas_call(
        functools.partial(norm_kernel, count),
        grid=(2 * count,),
        in_specs=[pl.BlockSpec((rows, features), lambda i: (0, 0))] * count
        + [
            pl.BlockSpec((rows, features), lambda i: (jnp.maximum(i - count, 0), 0)),
            pl.BlockSpec(vectors.shape, lambda i: (0, 0)),
        ],
        out_specs=pl.BlockSpec((rows, features), lambda i: (i, 0)),
        out_shape=jax.ShapeDtypeStruct((2 * count * rows, features), LOW),
        compiler_params=pltpu.CompilerParams(vmem_limit_bytes=32 << 20),
        cost_estimate=cost(0, 8 * count * rows * features),
    )(*pieces, far, vectors)


VMEM_LIMIT = 56 << 20


def dot(left, right, left_axis, right_axis):
    return lax.dot_general(
        left, right, (((left_axis,), (right_axis,)), ((), ())), preferred_element_type=WIDE
    )


def lay(block_lists, cuts, weights_ref, arrived):
    @pl.when(pl.program_id(0) == 0)
    def _():
        copies, column = [], 0
        for blocks, (start, width) in zip(block_lists, cuts):
            at = 0
            for block in blocks:
                depth = block.shape[0]
                copy = pltpu.make_async_copy(
                    block.at[:, pl.ds(start, width)],
                    weights_ref.at[pl.ds(at, depth), pl.ds(column, width)],
                    arrived.at[len(copies)],
                )
                copy.start()
                copies.append(copy)
                at += depth
            column += width
        for copy in copies:
            copy.wait()


def laid(features, width, *block_lists):
    count = sum(len(blocks) for blocks in block_lists)
    return [pltpu.VMEM((features, width), LOW), pltpu.SemaphoreType.DMA((count,))]


ANYWHERE = pl.BlockSpec(memory_space=pl.ANY)


def whole_spec(array):
    return pl.BlockSpec(array.shape, lambda i: (0, 0))


def row_spec(rows, array):
    return pl.BlockSpec((rows, array.shape[1]), lambda i: (i, 0))


GELU_A, GELU_B = (2 / math.pi) ** 0.5, 0.044715


def hidden_kernel(rows_ref, shift_ref, *refs):
    blocks, (pre_ref, hidden_ref, weights_ref, arrived) = refs[:-4], refs[-4:]
    lay([blocks], [(0, pre_ref.shape[1])], weights_ref, arrived)
    pre = dot(rows_ref[...], weights_ref[...], 1, 0) + shift_ref[...]
    pre_ref[...] = pre
    bend = jnp.tanh(GELU_A * (pre + GELU_B * (pre * pre * pre)))
    hidden_ref[...] = (0.5 * pre * (1.0 + bend)).astype(LOW)


def hidden_units(rows, shift, blocks):
    count, features = rows.shape
    width = blocks[0].shape[1]
    tile = count // 4
    return pl.pallas_call(
        hidden_kernel,
        grid=(4,),
        in_specs=[row_spec(tile, rows), whole_spec(shift)] + [ANYWHERE] * len(blocks),
        out_specs=[pl.BlockSpec((tile, width), lambda i: (i, 0))] * 2,
        out_shape=[
            jax.ShapeDtypeStruct((count, width), WIDE),
            jax.ShapeDtypeStruct((count, width), LOW),
        ],
        scratch_shapes=laid(features, width, blocks),
        compiler_params=pltpu.CompilerParams(vmem_limit_bytes=VMEM_LIMIT),
        cost_estimate=cost(2 * rows.size * width, 2 * rows.size + 6 * count * width),
    )(rows, shift, *blocks)


def d_pre_kernel(rows_ref, pre_ref, *refs):
    blocks, (d_pre_ref, sums_ref, weights_ref, arrived) = refs[:-4], refs[-4:]

    @pl.when(pl.program_id(0) == 0)
    def _():
        sums_ref[...] = jnp.zeros_like(sums_ref)

    lay([blocks], [(0, pre_ref.shape[1])], weights_ref, arrived)
    d_hidden = dot(rows_ref[...], weights_ref[...], 1, 0)
    pre = pre_ref[...]
    square = pre * pre
    bend = jnp.tanh(GELU_A * (pre + GELU_B * (square * pre)))
    slope = 0.5 * (1.0 + bend) + 0.5 * pre * (1.0 - bend * bend) * (
        GELU_A * (1.0 + 3.0 * GELU_B * square)
    )
    low = (d_hidden * slope).astype(LOW)
    d_pre_ref[...] = low
    sums_ref[...] += jnp.sum(low.astype(WIDE), axis=0, keepdims=True)


def d_pre_units(rows, pre, blocks):
    count, width = pre.shape
    tile = count // 4
    return pl.pallas_call(
        d_pre_kernel,
        grid=(4,),
        in_specs=[row_spec(tile, rows), row_spec(tile, pre)] + [ANYWHERE] * len(blocks),
        out_specs=[
            pl.BlockSpec((tile, width), lambda i: (i, 0)),
            pl.BlockSpec((1, width), lambda i: (0, 0)),
        ],
        out_shape=[
            jax.ShapeDtypeStruct((count, width), LOW),
            jax.ShapeDtypeStruct((1, width), WIDE),
        ],
        scratch_shapes=laid(rows.shape[1], width, blocks),
        compiler_params=pltpu.CompilerParams(vmem_limit_bytes=VMEM_LIMIT),
        cost_estimate=cost(2 * rows.size * width, 2 * rows.size + 6 * count * width),
    )(rows, pre, *blocks)


def gradient_kernel(pairs, steps, *refs):
    operands, (far_ref, near_ref) = refs[: 2 * pairs], refs[2 * pairs :]

    def write(out):
        column = 0
        for i in range(pairs):
            part = dot(operands[2 * i][...], operands[2 * i + 1][...], 0, 0).astype(LOW)
            out[:, column : column + part.shape[1]] = part
            column += part.shape[1]

    pl.when(pl.program_id(0) < steps)(lambda: write(far_ref))
    pl.when(pl.program_id(0) >= steps)(lambda: write(near_ref))


def gradient_blocks(place, *pairs):
    count, features = pairs[0][0].shape
    steps = len(place.masks) // 2
    rows = features // (2 * steps)
    width = sum(right.shape[1] for _, right in pairs)

    def block_of(i):
        return (0, jnp.where(i < steps, 2 * i + 1, 2 * (i - steps)))

    specs = []
    for _, right in pairs:
        specs += [pl.BlockSpec((count, rows), block_of), whole_spec(right)]
    return pl.pallas_call(
        functools.partial(gradient_kernel, len(pairs), steps),
        grid=(2 * steps,),
        in_specs=specs,
        out_specs=[
            pl.BlockSpec((rows, width), lambda i: (jnp.minimum(i, steps - 1), 0)),
            pl.BlockSpec((rows, width), lambda i: (jnp.maximum(i - steps, 0), 0)),
        ],
        out_shape=[jax.ShapeDtypeStruct((steps * rows, width), LOW)] * 2,
        compiler_params=pltpu.CompilerParams(vmem_limit_bytes=VMEM_LIMIT),
        cost_estimate=cost(2 * count * features * width, 2 * count * (features + width)),
    )(*[array for pair in pairs for array in pair])


def spread_kernel(cuts, counts, summed, *refs):
    if summed:
        (normed_ref, vectors_ref), refs = refs[:2], refs[2:]
        sums_ref, refs = refs[-3], refs[:-3] + refs[-2:]
    lefts, rest = refs[: len(cuts)], refs[len(cuts) :]
    block_lists = []
    for count in counts:
        block_lists.append(rest[:count])
        rest = rest[count:]
    far_ref, near_ref, weights_ref, arrived = rest
    lay(block_lists, cuts, weights_ref, arrived)
    left = jnp.concatenate([ref[...] for ref in lefts], axis=1)

    def write(out):
        total = dot(left, weights_ref[...], 1, 1)
        out[...] = total.astype(LOW)
        if summed:
            unit = normed_ref[...].astype(WIDE) - vectors_ref[1:2]
            sums_ref[0:1] += jnp.sum(total * unit, axis=0, keepdims=True)
            sums_ref[1:2] += jnp.sum(total, axis=0, keepdims=True)

    if summed:

        @pl.when(pl.program_id(0) == 0)
        def _():
            sums_ref[...] = jnp.zeros_like(sums_ref)

    pl.when(pl.program_id(0) < 2)(lambda: write(far_ref))
    pl.when(pl.program_id(0) >= 2)(lambda: write(near_ref))


def spread(lefts, block_lists, cuts, *unit):
    count = lefts[0].shape[0]
    tile = count // 4
    features = sum(b.shape[0] for b in block_lists[0])
    depth = sum(width for _, width in cuts)
    return pl.pallas_call(
        functools.partial(spread_kernel, cuts, [len(b) for b in block_lists], bool(unit)),
        grid=(4,),
        in_specs=[
            pl.BlockSpec((tile, rows.shape[1]), lambda i: ((i + 2) % 4, 0)) for rows in unit[:1]
        ]
        + [whole_spec(vectors) for vectors in unit[1:]]
        + [pl.BlockSpec((tile, left.shape[1]), lambda i: ((i + 2) % 4, 0)) for left in lefts]
        + [ANYWHERE] * sum(len(blocks) for blocks in block_lists),
        out_specs=[
            pl.BlockSpec((tile, features), lambda i: (jnp.minimum(i, 1), 0)),
            pl.BlockSpec((tile, features), lambda i: (jnp.maximum(i - 2, 0), 0)),
        ]
        + [pl.BlockSpec((2, features), lambda i: (0, 0)) for _ in unit[:1]],
        out_shape=[jax.ShapeDtypeStruct((count // 2, features), LOW)] * 2
        + [jax.ShapeDtypeStruct((2, features), WIDE) for _ in unit[:1]],
        scratch_shapes=laid(features, depth, *block_lists),
        compiler_params=pltpu.CompilerParams(vmem_limit_bytes=VMEM_LIMIT),
        cost_estimate=cost(2 * count * features * depth, 2 * count * (features + depth)),
    )(*unit, *lefts, *[b for blocks in block_lists for b in blocks])


PAIR = 2 * HD
SCALE = HD ** (-0.5)
TILES = 2


def turn(pair, cosine, sine):
    half = ROTARY // 2
    lane = lax.broadcasted_iota(jnp.int32, pair.shape, 1) % HD
    partner = jnp.where(lane < half, pltpu.roll(pair, PAIR - half, 1), pltpu.roll(pair, half, 1))
    return pair * cosine + partner * sine


def two_heads(pair):
    lane = lax.broadcasted_iota(jnp.int32, pair.shape, 1) // HD
    zero = jnp.zeros_like(pair)
    return jnp.concatenate([jnp.where(lane == head, pair, zero) for head in range(2)])


def either(stacked):
    rows = stacked.shape[0] // 2
    lane = lax.broadcasted_iota(jnp.int32, (rows, PAIR), 1) // HD
    return jnp.where(lane == 0, stacked[:rows], stacked[rows:])


def seen(ids_col, ids_row, first, rows, width):
    key = lax.broadcasted_iota(jnp.int32, (width, rows), 0)
    query = lax.broadcasted_iota(jnp.int32, (width, rows), 1) + first
    mask = (ids_col[:width] == ids_row[:, first : first + rows]) & (key <= query)
    return jnp.concatenate([mask, mask], axis=1)


def halves(y_ref, rows, cos_ref, sin_ref):
    places = [pl.ds(pl.multiple_of((y_ref[0] ^ t) * rows, 128), rows) for t in range(TILES)]
    cuts = [slice(t * rows, (t + 1) * rows) for t in range(TILES)]
    return places, [(cos_ref[cut], sin_ref[cut]) for cut in cuts]


def forward_kernel(y_ref, rows_ref, shift_ref, cos_ref, sin_ref, col_ref, row_ref, *refs):
    blocks, outs, (joint_ref, weights_ref, arrived) = refs[:-6], refs[-6:-3], refs[-3:]
    turned_ref, context_ref, log_ref = outs
    slots, width = context_ref.shape
    lay([blocks], [(0, 3 * width)], weights_ref, arrived)
    joint_ref[...] = dot(rows_ref[...], weights_ref[...], 1, 0)
    ids_col, ids_row = col_ref[...], row_ref[0]
    rows = slots // TILES
    masks = [seen(ids_col, ids_row, t * rows, rows, (t + 1) * rows) for t in range(TILES)]
    places, tables = halves(y_ref, rows, cos_ref, sin_ref)
    log_ref[...] = jnp.zeros_like(log_ref)
    for p in range(width // PAIR):
        columns = [slice(j * width + p * PAIR, j * width + (p + 1) * PAIR) for j in range(3)]
        query, key, value = [], [], []
        for place, table in zip(places, tables):
            parts = [joint_ref[place, c] + shift_ref[:, c] for c in columns]
            query.append(turn(parts[0], *table).astype(LOW))
            key.append(turn(parts[1], *table).astype(LOW))
            value.append(parts[2].astype(LOW))
            for c, array in zip(columns, (query, key, value)):
                turned_ref[place, c] = array[-1]
        key, value = jnp.concatenate(key), jnp.concatenate(value)
        for t in range(TILES):
            keys = (t + 1) * rows
            scores = dot(key[:keys], two_heads(query[t] * SCALE), 1, 1)
            scores = jnp.where(masks[t], scores, -1e30)
            top = jnp.max(scores, axis=0, keepdims=True)
            raised = jnp.exp(scores - top)
            total = jnp.sum(raised, axis=0, keepdims=True)
            probs = (raised * (1.0 / total)).astype(LOW)
            out = dot(probs, value[:keys], 0, 0)
            log_total = top + jnp.log(total)
            for head in range(2):
                log_ref[2 * p + head : 2 * p + head + 1, t * rows : (t + 1) * rows] = log_total[
                    :, head * rows : (head + 1) * rows
                ]
            context_ref[places[t], p * PAIR : (p + 1) * PAIR] = either(out).astype(LOW)


def backward_kernel(y_ref, turned_ref, rows_ref, log_ref, cos_ref, sin_ref, col_ref, row_ref, *refs):
    blocks, outs, (back_ref, weights_ref, arrived) = refs[:-5], refs[-5:-3], refs[-3:]
    joint_ref, sums_ref = outs
    slots, width = back_ref.shape
    lay([blocks], [(3 * width, width)], weights_ref, arrived)
    back_ref[...] = dot(rows_ref[...], weights_ref[...], 1, 0).astype(LOW)
    ids_col, ids_row = col_ref[...], row_ref[0]
    rows = slots // TILES
    masks = [seen(ids_col, ids_row, t * rows, rows, (t + 1) * rows) for t in range(TILES)]
    places, tables = halves(y_ref, rows, cos_ref, sin_ref)

    @pl.when(pl.program_id(0) == 0)
    def _():
        sums_ref[...] = jnp.zeros_like(sums_ref)

    for p in range(width // PAIR):
        columns = [slice(j * width + p * PAIR, j * width + (p + 1) * PAIR) for j in range(3)]
        key, value = (
            jnp.concatenate([turned_ref[place, c] for place in places]) for c in columns[1:]
        )
        d_query, d_key, d_value = [], [], []
        for t, place in enumerate(places):
            here, keys = slice(t * rows, (t + 1) * rows), (t + 1) * rows
            query = two_heads(turned_ref[place, columns[0]] * SCALE)
            d_context = two_heads(back_ref[place, p * PAIR : (p + 1) * PAIR])
            logs = jnp.concatenate(
                [log_ref[2 * p + head : 2 * p + head + 1, here] for head in range(2)], axis=1
            )
            scores = dot(key[:keys], query, 1, 1)
            probs = jnp.where(masks[t], jnp.exp(scores - logs), 0.0)
            d_probs = dot(value[:keys], d_context, 1, 1)
            delta = jnp.sum(probs * d_probs, axis=0, keepdims=True)
            d_scores = (probs * (d_probs - delta)).astype(LOW)
            d_query.append(either(dot(d_scores, key[:keys], 0, 0)) * SCALE)
            d_key.append(dot(d_scores, query, 1, 0))
            d_value.append(dot(probs.astype(LOW), d_context, 1, 0))
        for t, (place, (cosine, sine)) in enumerate(zip(places, tables)):
            here = slice(t * rows, (t + 1) * rows)
            parts = (
                turn(d_query[t], cosine, -sine),
                turn(sum(d[here] for d in d_key[t:]), cosine, -sine),
                sum(d[here] for d in d_value[t:]),
            )
            for c, array in zip(columns, parts):
                low = array.astype(LOW)
                joint_ref[place, c] = low
                sums_ref[:, c] += jnp.sum(low.astype(WIDE), axis=0, keepdims=True)


def by_group(slots, width):
    return pl.BlockSpec((slots, width), lambda g: (g, 0))


def attention_forward(place, normed, head_shift, cosine, sine, ids, blocks):
    groups, slots = ids.shape
    rows, width = normed.shape[0], blocks[0].shape[1] // 4
    return pl.pallas_call(
        forward_kernel,
        grid=(groups,),
        in_specs=[
            pl.BlockSpec(memory_space=pltpu.SMEM),
            row_spec(slots, normed),
            pl.BlockSpec((1, 3 * width), lambda g: (0, 0)),
            by_group(slots, PAIR),
            by_group(slots, PAIR),
            by_group(slots, 1),
            pl.BlockSpec((1, 1, slots), lambda g: (g, 0, 0)),
        ]
        + [ANYWHERE] * len(blocks),
        out_specs=[by_group(slots, 3 * width), by_group(slots, width), by_group(8, slots)],
        out_shape=[
            jax.ShapeDtypeStruct((rows, 3 * width), LOW),
            jax.ShapeDtypeStruct((rows, width), LOW),
            jax.ShapeDtypeStruct((8 * groups, slots), WIDE),
        ],
        scratch_shapes=[pltpu.VMEM((slots, 3 * width), WIDE)]
        + laid(normed.shape[1], 3 * width, blocks),
        compiler_params=pltpu.CompilerParams(vmem_limit_bytes=VMEM_LIMIT),
        cost_estimate=cost(20 * rows * slots * width + 6 * normed.size * width, 2 * normed.size),
    )(place.y.reshape(1), normed, head_shift[None], cosine, sine, ids.reshape(-1, 1), ids[:, None], *blocks)


def attention_backward(place, turned, grad, logs, cosine, sine, ids, blocks):
    groups, slots = ids.shape
    rows, width = grad.shape[0], blocks[0].shape[1] // 4
    return pl.pallas_call(
        backward_kernel,
        grid=(groups,),
        in_specs=[
            pl.BlockSpec(memory_space=pltpu.SMEM),
            by_group(slots, 3 * width),
            row_spec(slots, grad),
            by_group(8, slots),
            by_group(slots, PAIR),
            by_group(slots, PAIR),
            by_group(slots, 1),
            pl.BlockSpec((1, 1, slots), lambda g: (g, 0, 0)),
        ]
        + [ANYWHERE] * len(blocks),
        out_specs=[by_group(slots, 3 * width), pl.BlockSpec((1, 3 * width), lambda g: (0, 0))],
        out_shape=[
            jax.ShapeDtypeStruct((rows, 3 * width), LOW),
            jax.ShapeDtypeStruct((1, 3 * width), WIDE),
        ],
        scratch_shapes=[pltpu.VMEM((slots, width), LOW)] + laid(grad.shape[1], width, blocks),
        compiler_params=pltpu.CompilerParams(vmem_limit_bytes=VMEM_LIMIT),
        cost_estimate=cost(50 * rows * slots * width + 2 * grad.size * width, 2 * grad.size),
    )(place.y.reshape(1), turned, grad, logs, cosine, sine, ids.reshape(-1, 1), ids[:, None], *blocks)


def body(
    dp_size,
    tensor_size,
    tokens,
    cotangent,
    segment_ids,
    joint_weight,
    dense_weight,
    expand_weight,
    shrink_weight,
    head_bias,
    unit_bias,
    row_vectors,
    joint_mean,
    joint_square,
    dense_mean,
    dense_square,
    expand_mean,
    expand_square,
    shrink_mean,
    shrink_square,
    head_mean,
    head_square,
    unit_mean,
    unit_square,
    rows_mean,
    rows_square,
):
    place = Place(dp_size, tensor_size)
    devices = dp_size * tensor_size
    my_rows = tokens.shape[0]
    features = tokens.shape[1]
    group_slots = segment_ids.shape[0]
    shard_rows = joint_weight.shape[0]
    block_rows = 4 * shard_rows
    heads = head_bias.shape[2] // 4
    units = unit_bias.shape[1] // 4
    joint_width, unit_width = heads * HD, units * HD

    def kinds_first(array):
        return array.transpose(1, 0, 2)

    side, core = place.side, place.core
    first, second = place.ring[:2]
    small = SmallGather(
        place,
        jnp.concatenate(
            [
                row_vectors.reshape(-1),
                head_bias.reshape(-1),
                unit_bias.reshape(-1),
                segment_ids.astype(WIDE),
            ]
        ),
    )

    joint_shard = kinds_first(joint_weight)
    quarters = pack(place, joint_shard, dense_weight[None])
    by_core = place.move(quarters[1], core)
    by_side = place.move(quarters[2], side)
    by_both = place.move(quarters[3], side | core)
    small.step(0, 1, quarters[1])
    small.step(core)
    mine = arrange(place, tokens)
    near_quarters = pack(place, expand_weight[None], shrink_weight[None])
    my_ids = lax.dynamic_slice_in_dim(segment_ids, place.y * my_rows, my_rows)
    masked = arrange(place, cotangent * (my_ids > 0).astype(LOW)[:, None])
    blocks = stack(place, (quarters[0], by_core, by_side, by_both), (4 * joint_width,))[0]
    block, joint = blocks[0], Gather(place, *blocks)

    ready = (block, small.rows, mine)
    got = [
        joint.along_first(0),
        joint.along_second(),
        place.move(after(mine, *ready), side),
        place.move(after(mine, *ready), 0, 1),
        place.move(
            after(jnp.concatenate([near_quarters[1], near_quarters[3]]), *ready), core
        ),
        small.step(first, 0, *ready),
    ]
    mine_side, mine_y, by_core = got[2:5]

    ready = tuple(got)
    got = [
        joint.along_first(1, *ready),
        joint.onward(0, *ready),
        place.move(after(mine_side, *ready), 0, 1),
        place.move(
            after(jnp.concatenate([near_quarters[2], by_core[shard_rows:]]), *ready), side
        ),
        small.step(side, 0, *ready),
    ]
    corner, by_side = got[2:4]
    near = join(mine, mine_y, mine_side, corner)
    blocks = stack(
        place, (near_quarters[0], by_core[:shard_rows], by_side), (unit_width, unit_width)
    )
    expand, shrink = (Gather(place, *array) for array in blocks)

    ready = tuple(got) + (blocks[0][0],)
    got = [
        expand.along_first(0, *ready),
        joint.onward(1, *ready),
        expand.along_second(*ready),
        place.move(after(masked, *ready), side),
        place.move(after(masked, *ready), 0, 1),
        small.step(second, 0, *ready),
    ]
    masked_side, masked_y = got[3:5]

    cuts = [row_vectors.size, row_vectors.size + head_bias.size]
    cuts.append(cuts[1] + unit_bias.size)
    rows_small, head_small, unit_small, ids_small = jnp.split(small.whole(), cuts, axis=1)
    row_whole = rows_small.reshape(devices, 4, -1).transpose(1, 0, 2).reshape(4, features)
    head_small = pick(head_small.reshape((dp_size, tensor_size) + head_bias.shape), place.y, 1)
    head_low = lax.dynamic_slice_in_dim(head_small, place.quarter * heads, heads, 3)
    head_shift = head_low.reshape(HD, 3, heads).astype(LOW).astype(WIDE)
    head_shift = head_shift.transpose(1, 2, 0).reshape(-1)
    unit_small = pick(unit_small.reshape((dp_size, tensor_size) + unit_bias.shape), place.y, 1)
    unit_low = lax.dynamic_slice_in_dim(unit_small, place.quarter * units, units, 2)
    unit_shift = unit_low.reshape(HD, units).astype(LOW).astype(WIDE).T.reshape(-1)
    ids_small = ids_small.reshape(dp_size, tensor_size, group_slots)[:, 0]
    distances = (0, place.side, place.core, place.side | place.core)
    ids = jnp.stack([pick(ids_small, place.index ^ d) for d in distances])

    own_vectors = arrange(place, row_whole)
    positions = jax.vmap(doc_positions)(ids)[0].reshape(-1, 1)
    lane = jnp.arange(PAIR) % HD
    half_rot = ROTARY // 2
    frequency = 10000.0 ** (-(lane % half_rot).astype(WIDE) / half_rot)
    angles = positions * frequency
    cosine = jnp.where(lane < ROTARY, jnp.cos(angles), 1.0)
    sine = jnp.sin(angles)
    sine = jnp.where(lane < half_rot, -sine, jnp.where(lane < ROTARY, sine, 0.0))

    ready = tuple(got) + (cosine, sine, own_vectors, head_shift, unit_shift)
    got = [
        expand.along_first(1, *ready),
        shrink.along_second(*ready),
        place.move(after(masked_side, *ready), 0, 1),
        place.move(after(near, *ready), core),
    ]
    normed = norm((mine, mine_y, mine_side, corner), got[3], own_vectors)
    grad_near = join(masked, masked_y, masked_side, got[2])

    ready = tuple(got) + (grad_near, normed)
    got = [
        shrink.along_first(0, *ready),
        expand.onward(0, *ready),
        expand.onward(1, *ready),
        place.move(after(grad_near, *ready), core),
    ]
    joint = joint.whole()
    turned, context, logs = attention_forward(
        place, after(normed, *ready), head_shift, cosine, sine, ids, joint
    )

    ready = tuple(got) + (context,)
    grad_all = join(grad_near, got[3])
    got = [shrink.along_first(1, *ready), shrink.onward(0, *ready)]
    d_joint, joint_sums = attention_backward(
        place, turned, after(grad_all, *ready), logs, cosine, sine, ids, joint
    )
    expand = expand.whole()

    ready = tuple(got) + (d_joint,)
    got = [shrink.onward(1, *ready)]
    shrink = shrink.whole()
    sum_joint = Reduce(place, (after(normed, *ready), d_joint), (grad_all, context))

    ready = tuple(got) + (sum_joint.far,)
    pre, hidden = hidden_units(after(normed, *ready), unit_shift[None], expand)
    sum_shrink = Reduce(place, (after(grad_all, pre), hidden))
    d_pre, unit_sums = d_pre_units(after(grad_all, sum_shrink.far), pre, shrink)
    sum_joint.along(-1, *ready, before=(d_pre,))

    sum_joint.rest()
    ready = (sum_joint.total, d_pre)
    sum_expand = Reduce(place, (after(normed, *ready), d_pre))
    inner_far, inner_near, inner_sums = spread(
        [after(d_joint, sum_expand.far), d_pre],
        [joint, expand],
        ((0, 3 * joint_width), (0, unit_width)),
        normed,
        own_vectors,
    )
    inner = GroupSum(place, inner_far, inner_near, 4)
    sum_joint.along(0, *ready, before=(inner.far,))
    sum_shrink.along(-1, *ready, before=(inner.far,))

    sum_shrink.rest()
    ready = (sum_joint.total, sum_shrink.total, inner.far)
    outer = GroupSum(
        place,
        *spread(
            [after(context, *ready), hidden],
            [joint, shrink],
            ((3 * joint_width, joint_width), (0, unit_width)),
        ),
        2,
    )
    sent = inner.hop(*inner.by_core(*ready))
    before = (outer.far, *sent)
    sum_shrink.along(0, *ready, before=before)
    sum_expand.along(-1, *ready, before=before)

    def returned(reduce, *others):
        summed = after(reduce.total, *others).reshape(4, shard_rows, -1)
        return swap_quarters(place, [pick(summed, place.quarter ^ flip) for flip in FLIPS])

    sum_expand.rest()
    ready = (sum_shrink.total, sum_expand.total, *sent, outer.far)
    d_normed = inner.last_hop(*ready)
    outer_sent = outer.hop(*outer.by_core(*ready))
    g_joint = returned(sum_joint, *ready)
    sum_expand.along(0, *ready, before=(d_normed, *outer_sent))

    ready = (sum_expand.total, d_normed, *outer_sent, *g_joint)
    g_expand = returned(sum_expand, *ready)
    branch = outer.last_hop(*ready)
    g_shrink = returned(sum_shrink, *ready)

    layer_output = mine.astype(WIDE) + branch + own_vectors[2] + own_vectors[3]
    layer_output = arrange(place, layer_output.astype(LOW), True)
    inputs = mine.astype(WIDE)
    centered = inputs - jnp.mean(inputs, axis=-1, keepdims=True)
    inverse = lax.rsqrt(jnp.mean(centered * centered, axis=-1, keepdims=True) + EPS_NORM)
    unit_rows = centered * inverse
    d_unit_rows = d_normed * own_vectors[0]
    d_inputs = inverse * (
        d_unit_rows
        - jnp.mean(d_unit_rows, axis=-1, keepdims=True)
        - unit_rows * jnp.mean(d_unit_rows * unit_rows, axis=-1, keepdims=True)
    )
    input_grad = arrange(place, masked.astype(WIDE) + d_inputs, True)

    own_sums = jnp.concatenate([joint_sums[0], unit_sums[0]])
    row_sums = jnp.concatenate(
        [
            inner_sums[0:1] / own_vectors[0:1],
            inner_sums[1:2],
            jnp.sum(masked, axis=0, dtype=WIDE, keepdims=True),
        ]
    )
    row_sums = arrange(place, row_sums, True).reshape(-1)
    own_sums, row_sums = reduce_small(place, after(own_sums, *ready), row_sums)
    features_here = HD // dp_size
    g_head = own_sums[:, : 3 * joint_width].reshape(4, 3, heads, HD)
    g_head = lax.dynamic_slice_in_dim(g_head, place.index * features_here, features_here, 3)
    g_head = g_head.transpose(3, 1, 0, 2).reshape(head_bias.shape)
    g_unit = own_sums[:, 3 * joint_width :].reshape(4 * units, HD)
    g_unit = lax.dynamic_slice_in_dim(g_unit, place.index * features_here, features_here, 1).T
    row_sums = row_sums.reshape(3, features)
    row_width = row_vectors.shape[1]
    g_rows = lax.dynamic_slice_in_dim(
        row_sums, (place.index * tensor_size + place.y) * row_width, row_width, 1
    )
    g_rows = jnp.concatenate([g_rows, g_rows[2:]])

    def shard_update(pieces, column, weight, moment, square, step_rate):
        news = adam_shard(
            place, pieces, column, weight[None], moment[None], square[None], step_rate
        )
        return [new[0] for new in news]

    joint_new = [
        kinds_first(new)
        for new in adam_shard(
            place,
            g_joint,
            0,
            joint_shard,
            kinds_first(joint_mean),
            kinds_first(joint_square),
            D ** (-0.5),
        )
    ]
    dense_new = shard_update(
        g_joint, 3 * joint_width, dense_weight, dense_mean, dense_square, (D // 32) ** (-0.5)
    )
    shrink_new = shard_update(g_shrink, 0, shrink_weight, shrink_mean, shrink_square, FF ** (-0.5))
    g_expand[0] = after(g_expand[0], joint_new[0], dense_new[0], shrink_new[0])
    expand_new = shard_update(g_expand, 0, expand_weight, expand_mean, expand_square, D ** (-0.5))
    head_new = adam_update(head_bias, g_head, head_mean, head_square, 0.1, 0.0)
    unit_new = adam_update(unit_bias, g_unit, unit_mean, unit_square, 0.1, 0.0)
    rows_new = adam_update(row_vectors, g_rows, rows_mean, rows_square, 0.1, 0.0)
    return (
        layer_output,
        input_grad,
        joint_new[0],
        joint_new[1],
        joint_new[2],
        dense_new[0],
        dense_new[1],
        dense_new[2],
        expand_new[0],
        expand_new[1],
        expand_new[2],
        shrink_new[0],
        shrink_new[1],
        shrink_new[2],
        head_new[0],
        head_new[1],
        head_new[2],
        unit_new[0],
        unit_new[1],
        unit_new[2],
        rows_new[0],
        rows_new[1],
        rows_new[2],
    )


def solution(mesh):
    return jax.shard_map(
        functools.partial(body, mesh.shape["dp"], mesh.shape["tensor"]),
        mesh=mesh,
        in_specs=(
            P(("dp", "tensor"), None),
            P(("dp", "tensor"), None),
            P("dp"),
            P("dp", None, "tensor"),
            P("dp", "tensor"),
            P("dp", "tensor"),
            P("dp", "tensor"),
            P("dp", None, "tensor"),
            P("dp", "tensor"),
            P(None, ("dp", "tensor")),
            P("dp", None, "tensor"),
            P("dp", None, "tensor"),
            P("dp", "tensor"),
            P("dp", "tensor"),
            P("dp", "tensor"),
            P("dp", "tensor"),
            P("dp", "tensor"),
            P("dp", "tensor"),
            P("dp", None, "tensor"),
            P("dp", None, "tensor"),
            P("dp", "tensor"),
            P("dp", "tensor"),
            P(None, ("dp", "tensor")),
            P(None, ("dp", "tensor")),
        ),
        out_specs=(
            P(("dp", "tensor"), None),
            P(("dp", "tensor"), None),
            P("dp", None, "tensor"),
            P("dp", None, "tensor"),
            P("dp", None, "tensor"),
            P("dp", "tensor"),
            P("dp", "tensor"),
            P("dp", "tensor"),
            P("dp", "tensor"),
            P("dp", "tensor"),
            P("dp", "tensor"),
            P("dp", "tensor"),
            P("dp", "tensor"),
            P("dp", "tensor"),
            P("dp", None, "tensor"),
            P("dp", None, "tensor"),
            P("dp", None, "tensor"),
            P("dp", "tensor"),
            P("dp", "tensor"),
            P("dp", "tensor"),
            P(None, ("dp", "tensor")),
            P(None, ("dp", "tensor")),
            P(None, ("dp", "tensor")),
        ),
        check_vma=False,
    )
```

```python
import functools
import math

import jax
import jax.numpy as jnp
from jax import lax
from jax.experimental import pallas as pl
from jax.experimental.pallas import tpu as pltpu
from jax.sharding import PartitionSpec as P

D = 2048
HD = 64
FF = 8192
ROTARY = 32
STEP = 10


EPS_NORM = 1e-05
BETA_ONE = 0.9
BETA_TWO = 0.95
EPS_ADAM = 1e-08
WEIGHT_DECAY = 0.1


def doc_positions(segments):
    row_count = segments.shape[0]
    places = jnp.arange(row_count, dtype=jnp.int32)
    same_doc = segments[:, None] == segments[None, :]
    starts = jnp.min(jnp.where(same_doc, places[None, :], row_count), axis=1)
    allowed = same_doc & (places[None, :] <= places[:, None])
    return ((places - starts).astype(jnp.float32), allowed)


def adam_update(weight, gradient, moment, square, step_rate, decay_rate):
    new_moment = BETA_ONE * moment + (1.0 - BETA_ONE) * gradient
    new_square = BETA_TWO * square + (1.0 - BETA_TWO) * gradient * gradient
    fix_one = 1.0 - BETA_ONE**STEP
    fix_two = 1.0 - BETA_TWO**STEP
    update = new_moment / fix_one / (jnp.sqrt(new_square / fix_two) + EPS_ADAM)
    return (weight - step_rate * (update + decay_rate * weight), new_moment, new_square)


AXES = ("dp", "tensor")
LOW = jnp.bfloat16
WIDE = jnp.float32


def after(array, *others):
    others = [o for o in others if o is not None]
    return lax.optimization_barrier((array, *others))[0] if others else array


def cost(flops, nbytes):
    return pl.CostEstimate(flops=int(flops) >> 10, bytes_accessed=int(nbytes) >> 10, transcendentals=0)


class Place:
    def __init__(self, dp_size, tensor_size):
        count = dp_size.bit_length() - 1
        self.dp_size, self.tensors, self.count = dp_size, tensor_size, count
        self.core, self.side = 1, 1 << (count - 2)
        self.ring = [1 << b for b in range(count - 1, 0, -1) if 1 << b != self.side]
        self.index = lax.axis_index("dp")
        self.y = lax.axis_index("tensor")
        self.quarter = self.bit(self.side) * 2 + self.bit(self.core)
        self.masks = [0]
        for bit in reversed(self.ring):
            self.masks = self.masks + [m | bit for m in self.masks]
        self.last = {}

    def bit(self, mask):
        return (self.index // mask) % 2

    def move(self, array, mask, y=0, lane=None):
        pairs = []
        for dp in range(self.dp_size):
            for oy in range(self.tensors):
                pairs.append((dp * self.tensors + oy, (dp ^ mask) * self.tensors + (oy ^ y)))
        if lane is not None:
            array = after(array, self.last.get(lane))
        got = lax.ppermute(array, AXES, pairs)
        if lane is not None:
            self.last[lane] = got
        return got

    def to_own_order(self, array):
        lead = array.shape[:-1]
        split = array.reshape(lead + (2,) * self.count + (-1,))
        first = len(lead)
        ring_axes = [first + self.count - bit.bit_length() for bit in self.ring]
        for bit, axis in zip(self.ring, ring_axes):
            split = jnp.where(self.bit(bit) == 0, split, jnp.flip(split, axis))
        rest = [first + b for b in range(self.count + 1) if first + b not in ring_axes]
        split = split.transpose(list(range(first)) + ring_axes + rest)
        return split.reshape(array.shape)

    def to_index_order(self, array):
        lead = array.shape[:-1]
        split = array.reshape(lead + (2,) * self.count + (-1,))
        first = len(lead)
        ring_axes = [first + self.count - bit.bit_length() for bit in self.ring]
        rest = [first + b for b in range(self.count + 1) if first + b not in ring_axes]
        order = list(range(first)) + ring_axes + rest
        split = split.transpose([order.index(i) for i in range(len(order))])
        for bit, axis in zip(self.ring, ring_axes):
            split = jnp.where(self.bit(bit) == 0, split, jnp.flip(split, axis))
        return split.reshape(array.shape)


def in_hbm(*arrays):
    return [
        pltpu.with_memory_space_constraint(a, pltpu.HBM) if a.size > 1 << 16 else a for a in arrays
    ]


def pick(array, index, axis=0):
    return lax.dynamic_index_in_dim(array, index, axis, keepdims=False)


def swap_quarters(place, pieces):
    return [
        pieces[0],
        place.move(pieces[1], place.core),
        place.move(pieces[2], place.side),
        place.move(pieces[3], place.side | place.core),
    ]


def arrange_kernel(back, statics, own_ref, array_ref, out_ref):
    width = array_ref.shape[1] // len(statics)
    for r, static in enumerate(statics):
        at = pl.multiple_of((own_ref[0] ^ static) * width, 128)
        here = slice(r * width, (r + 1) * width)
        if back:
            out_ref[:, pl.ds(at, width)] = array_ref[:, here]
        else:
            out_ref[:, here] = array_ref[:, pl.ds(at, width)]


def arrange(place, array, back=False):
    if array.shape[1] // place.dp_size % 128:
        return place.to_index_order(array) if back else place.to_own_order(array)
    ring = sum(place.ring)
    inner = (0, place.core, place.side, place.side | place.core)
    statics = [mask | i for mask in place.masks for i in inner]
    return pl.pallas_call(
        functools.partial(arrange_kernel, back, statics),
        in_specs=[
            pl.BlockSpec(memory_space=pltpu.SMEM),
            pl.BlockSpec(memory_space=pltpu.VMEM),
        ],
        out_specs=pl.BlockSpec(memory_space=pltpu.VMEM),
        out_shape=jax.ShapeDtypeStruct(array.shape, array.dtype),
        compiler_params=pltpu.CompilerParams(vmem_limit_bytes=24 << 20),
        cost_estimate=cost(0, 4 * array.size),
    )((place.index & ring).reshape(1), array)


class Gather:
    def __init__(self, place, block, *halves):
        self.place, self.halves = place, halves
        first, second = place.ring[:2]
        self.both = first | second
        self.first, self.second = first, second
        self.parts = {0: [block], first: [None, None], second: [None], self.both: [None, None]}

    def along_first(self, half, *others):
        got = self.place.move(after(self.halves[half], *others), self.first)
        self.parts[self.first][half] = got
        return got

    def along_second(self, *others):
        got = self.place.move(after(self.parts[0][0], *others), self.second)
        self.parts[self.second][0] = got
        return got

    def onward(self, half, *others):
        got = self.place.move(after(self.parts[self.first][half], *others), self.second)
        self.parts[self.both][half] = got
        return got

    def whole(self):
        for bit in self.place.ring[2:]:
            for mask in list(self.parts):
                self.parts[mask | bit] = [self.place.move(p, bit) for p in self.parts[mask]]
        return [part for m in self.place.masks for part in self.parts[m]]


class Reduce:
    def __init__(self, place, *pairs):
        self.place, self.parts = place, gradient_blocks(place, *pairs)
        for bit in reversed(place.ring[2:]):
            for mask in [m for m in self.parts if m & bit]:
                got = place.move(self.parts.pop(mask), bit)
                total = self.parts[mask ^ bit].astype(WIDE) + got.astype(WIDE)
                self.parts[mask ^ bit] = total.astype(LOW)

    def halves(self, array):
        half = array.shape[0] // 2
        return [array[:half].astype(WIDE), array[half:].astype(WIDE)]

    def send_both(self, *others, before=()):
        first, second = self.place.ring[:2]
        got = self.place.move(after(self.parts[first | second], *others), second)
        got, own = self.halves(after(got, *before)), self.halves(self.parts[first])
        self.sent = [(a + b).astype(LOW) for a, b in zip(got, own)]
        return tuple(self.sent)

    def send_second(self, *others, before=()):
        second = self.place.ring[1]
        got = self.place.move(after(self.parts[second], *others), second)
        got, own = self.halves(after(got, *before)), self.halves(self.parts[0])
        self.sums = [a + b for a, b in zip(got, own)]
        return tuple(self.sums)

    def send_half(self, half, *others, before=()):
        got = self.place.move(after(self.sent[half], *others), self.place.ring[0])
        self.sums[half] = (self.sums[half] + after(got, *before).astype(WIDE)).astype(LOW)
        return (self.sums[half],)


def choose_kernel(quarter_ref, early_ref, late_ref, *outs):
    rows = outs[0].shape[0]
    for quarter in range(4):
        source = early_ref if quarter < 2 else late_ref
        for flip, out in zip(FLIPS, outs):

            @pl.when(quarter_ref[0] ^ quarter == flip)
            def _():
                out[...] = source[(quarter % 2) * rows : (quarter % 2 + 1) * rows, :]


def choose(place, halves):
    rows, width = halves[0].shape[0] // 2, halves[0].shape[1]
    return pl.pallas_call(
        choose_kernel,
        in_specs=[pl.BlockSpec(memory_space=pltpu.SMEM)]
        + [pl.BlockSpec(memory_space=pltpu.VMEM)] * 2,
        out_specs=[pl.BlockSpec(memory_space=pltpu.VMEM)] * 4,
        out_shape=[jax.ShapeDtypeStruct((rows, width), LOW)] * 4,
        cost_estimate=cost(0, 16 * rows * width),
    )(place.quarter.reshape(1), *halves)


def cores_kernel(near_ref, got_ref, first_ref, second_ref, side_ref, y_ref):
    step = pl.program_id(0)
    cut = first_ref.shape[1]

    def write(out, part):
        total = near_ref[part, :].astype(WIDE) + got_ref[part, :].astype(WIDE)
        out[0] = total.astype(LOW)

    early, late = pl.ds(0, cut), pl.ds(cut, near_ref.shape[0] - cut)
    pl.when(step < 2)(lambda: write(first_ref, early))
    pl.when(step >= 2)(lambda: write(side_ref, early))
    pl.when(step % 2 == 0)(lambda: write(second_ref, late))
    pl.when(step % 2 == 1)(lambda: write(y_ref, late))


def add_cores(near, got, cut):
    rows, features = near.shape[0] // 4, near.shape[1]
    block = pl.BlockSpec((rows, features), lambda i: (i, 0))
    early = (1, cut, features)
    late = (1, rows - cut, features)
    return pl.pallas_call(
        cores_kernel,
        grid=(4,),
        in_specs=[block, block],
        out_specs=[
            pl.BlockSpec(early, lambda i: (jnp.minimum(i, 1), 0, 0)),
            pl.BlockSpec(late, lambda i: (i // 2, 0, 0)),
            pl.BlockSpec(early, lambda i: (jnp.maximum(i - 2, 0), 0, 0)),
            pl.BlockSpec(late, lambda i: (i // 2, 0, 0)),
        ],
        out_shape=[
            jax.ShapeDtypeStruct((2,) + shape[1:], LOW) for shape in (early, late, early, late)
        ],
        compiler_params=pltpu.CompilerParams(vmem_limit_bytes=32 << 20),
        cost_estimate=cost(0, 24 * rows * features),
    )(near, got)


class GroupSum:
    def __init__(self, place, far, near):
        self.place, self.far, self.near = place, far, near

    def by_core(self, *others):
        got = self.place.move(after(self.far, *others), self.place.core)
        self.first, self.second, *self.sent = add_cores(self.near, got, self.near.shape[0] // 16)
        return self.sent

    def hop(self, *others):
        place, (first, second) = self.place, self.sent
        got_side = place.move(after(first, *others), place.side)
        got_y = place.move(after(second, *others), 0, 1)
        self.first = self.first.astype(WIDE) + got_side.astype(WIDE)
        self.second = self.second.astype(WIDE) + got_y.astype(WIDE)
        self.sent = [self.first[1].astype(LOW), self.second[1].astype(LOW)]
        return self.sent

    def last_hop(self, *others):
        place, (first, second) = self.place, self.sent
        self.got = [
            place.move(after(first, *others), 0, 1),
            place.move(after(second, *others), place.side),
        ]
        return jnp.concatenate(
            [a[0] + b.astype(WIDE) for a, b in zip((self.first, self.second), self.got)]
        )


class SmallGather:
    def __init__(self, place, vector):
        self.place, self.rows, self.bits = place, vector[None], []

    def step(self, mask, y=0, *others):
        got = self.place.move(after(self.rows, *others), mask, y)
        self.rows = jnp.concatenate([self.rows, got])
        self.bits.append(2 * mask + y)
        return self.rows

    def whole(self):
        place = self.place
        for b in range(place.count):
            if 2 << b not in self.bits:
                self.step(1 << b)
        length = self.rows.shape[1]
        split = self.rows.reshape((2,) * len(self.bits) + (length,))
        axes = []
        for b in [2 << b for b in range(place.count - 1, -1, -1)] + [1]:
            axis = len(self.bits) - 1 - self.bits.index(b)
            own = place.y if b == 1 else place.bit(b // 2)
            split = jnp.where(own == 0, split, jnp.flip(split, axis))
            axes.append(axis)
        return split.transpose(axes + [len(axes)]).reshape(-1, length)


class SmallReduce:
    def __init__(self, place, own, shared):
        self.place, self.width = place, own.size
        slot = place.y * 4 + place.quarter
        padded = jnp.zeros((4 * place.tensors, own.size), WIDE)
        padded = lax.dynamic_update_slice_in_dim(padded, own[None], slot, 0)
        self.vector = jnp.concatenate([padded.reshape(-1), shared])

    def step(self, *moves):
        self.vector = self.vector + sum(self.place.move(self.vector, *move) for move in moves)

    def results(self):
        count = 4 * self.place.tensors * self.width
        own = self.vector[:count].reshape(self.place.tensors, 4, self.width)
        return pick(own, self.place.y), self.vector[count:]


FLIPS = (0, 1, 2, 3)


def pack_kernel(quarter_ref, *refs):
    shards, outs = refs[: len(refs) - 4], refs[len(refs) - 4 :]
    for flip, out in zip(FLIPS, outs):
        quarter = quarter_ref[0] ^ flip
        column = 0
        for shard in shards:
            width = shard.shape[2] // 4
            for kind in range(shard.shape[0]):
                at = pl.multiple_of(quarter * width, 128)
                out[:, column : column + width] = shard[kind, :, pl.ds(at, width)].astype(LOW)
                column += width


def pack(place, *shards):
    rows = shards[0].shape[1]
    width = sum(s.shape[0] * s.shape[2] for s in shards) // 4
    return pl.pallas_call(
        pack_kernel,
        in_specs=[pl.BlockSpec(memory_space=pltpu.SMEM)]
        + [pl.BlockSpec(memory_space=pltpu.VMEM)] * len(shards),
        out_specs=[pl.BlockSpec(memory_space=pltpu.VMEM)] * 4,
        out_shape=[jax.ShapeDtypeStruct((rows, width), LOW)] * 4,
        compiler_params=pltpu.CompilerParams(vmem_limit_bytes=24 << 20),
        cost_estimate=cost(0, 24 * rows * width),
    )(place.quarter.reshape(1), *shards)


def stack_kernel(count, quarter_ref, *refs):
    pieces, outs = refs[:count], refs[count:]
    third = len(outs) // 3
    outs, halves = outs[:third], (outs[third : 2 * third], outs[2 * third :])
    rows = sum(piece.shape[0] for piece in pieces) // 4
    flip = 0
    for piece in pieces:
        for part in range(piece.shape[0] // rows):
            at = pl.multiple_of((quarter_ref[0] ^ flip) * rows, 16)
            column = 0
            for out in outs:
                width = out.shape[1]
                out[pl.ds(at, rows), :] = piece[
                    part * rows : (part + 1) * rows, column : column + width
                ]
                column += width
            flip += 1
    for out, early, late in zip(outs, *halves):
        early[...] = out[: 2 * rows]
        late[...] = out[2 * rows :]


def stack(place, pieces, widths):
    rows = sum(piece.shape[0] for piece in pieces)
    outs = pl.pallas_call(
        functools.partial(stack_kernel, len(pieces)),
        in_specs=[pl.BlockSpec(memory_space=pltpu.SMEM)]
        + [pl.BlockSpec(memory_space=pltpu.VMEM)] * len(pieces),
        out_specs=[pl.BlockSpec(memory_space=pltpu.VMEM)] * (3 * len(widths)),
        out_shape=[
            jax.ShapeDtypeStruct((r, w), LOW) for r in (rows, rows // 2, rows // 2) for w in widths
        ],
        compiler_params=pltpu.CompilerParams(vmem_limit_bytes=24 << 20),
        cost_estimate=cost(0, 4 * rows * sum(widths)),
    )(place.quarter.reshape(1), *pieces)
    return list(zip(outs[: len(widths)], outs[len(widths) : 2 * len(widths)], outs[-len(widths) :]))


def adam_kernel(step_rate, column, quarter_ref, near_ref, core_ref, side_ref, both_ref, *refs):
    weight, moment, square, new_weight, new_moment, new_square = refs
    distance = pl.program_id(0) ^ quarter_ref[0]
    for flip, piece in zip(FLIPS, (near_ref, core_ref, side_ref, both_ref)):

        @pl.when(distance == flip)
        def _():
            width = weight.shape[2]
            for kind in range(weight.shape[0]):
                start = column + kind * width
                results = adam_update(
                    weight[kind],
                    piece[:, start : start + width].astype(WIDE),
                    moment[kind],
                    square[kind],
                    step_rate,
                    WEIGHT_DECAY,
                )
                new_weight[kind], new_moment[kind], new_square[kind] = results


def adam_shard(place, pieces, column, weight, moment, square, step_rate):
    kinds, rows, width = weight.shape
    block = pl.BlockSpec((kinds, rows, width // 4), lambda q: (0, 0, q))
    return pl.pallas_call(
        functools.partial(adam_kernel, step_rate, column),
        grid=(4,),
        in_specs=[pl.BlockSpec(memory_space=pltpu.SMEM)]
        + [pl.BlockSpec(pieces[0].shape, lambda q: (0, 0))] * 4
        + [block] * 3,
        out_specs=[block] * 3,
        out_shape=[jax.ShapeDtypeStruct(weight.shape, WIDE)] * 3,
        compiler_params=pltpu.CompilerParams(vmem_limit_bytes=32 << 20),
        cost_estimate=pl.CostEstimate(
            flops=20 * weight.size, bytes_accessed=26 * weight.size, transcendentals=0
        ),
    )(*in_hbm(place.quarter.reshape(1), *pieces, weight, moment, square))


def join_kernel(starts, *refs):
    arrays, out = refs[:-1], refs[-1]
    step = pl.program_id(0)
    for array, start, end in zip(arrays, starts, starts[1:]):

        @pl.when((step >= start) & (step < end))
        def _():
            out[...] = array[...]


def join(*arrays):
    tile = arrays[0].shape[0] // 2
    starts = [0]
    for array in arrays:
        starts.append(starts[-1] + array.shape[0] // tile)
    width = arrays[0].shape[1]

    def spec(start, end):
        return pl.BlockSpec((tile, width), lambda i: (jnp.clip(i - start, 0, end - start - 1), 0))

    return pl.pallas_call(
        functools.partial(join_kernel, starts),
        grid=(starts[-1],),
        in_specs=[spec(*ends) for ends in zip(starts, starts[1:])],
        out_specs=pl.BlockSpec((tile, width), lambda i: (i, 0)),
        out_shape=jax.ShapeDtypeStruct((starts[-1] * tile, width), arrays[0].dtype),
        compiler_params=pltpu.CompilerParams(vmem_limit_bytes=32 << 20),
        cost_estimate=cost(0, 4 * starts[-1] * tile * width),
    )(*arrays)


def norm_kernel(count, *refs):
    pieces, far_ref, vectors_ref, normed_ref = refs[:count], *refs[count:]

    def write(ref):
        rows = ref[...].astype(WIDE)
        centered = rows - jnp.mean(rows, axis=-1, keepdims=True)
        inverse = lax.rsqrt(jnp.mean(centered * centered, axis=-1, keepdims=True) + EPS_NORM)
        normed_ref[...] = (centered * inverse * vectors_ref[0:1] + vectors_ref[1:2]).astype(LOW)

    step = pl.program_id(0)
    for i, piece in enumerate(pieces):
        pl.when(step == i)(functools.partial(write, piece))
    pl.when(step >= count)(functools.partial(write, far_ref))


def norm(pieces, far, vectors):
    rows, features = pieces[0].shape
    count = len(pieces)
    return pl.pallas_call(
        functools.partial(norm_kernel, count),
        grid=(2 * count,),
        in_specs=[pl.BlockSpec((rows, features), lambda i: (0, 0))] * count
        + [
            pl.BlockSpec((rows, features), lambda i: (jnp.maximum(i - count, 0), 0)),
            pl.BlockSpec(vectors.shape, lambda i: (0, 0)),
        ],
        out_specs=pl.BlockSpec((rows, features), lambda i: (i, 0)),
        out_shape=jax.ShapeDtypeStruct((2 * count * rows, features), LOW),
        compiler_params=pltpu.CompilerParams(vmem_limit_bytes=32 << 20),
        cost_estimate=cost(0, 8 * count * rows * features),
    )(*pieces, far, vectors)


VMEM_LIMIT = 40 << 20


def dot(left, right, left_axis, right_axis):
    return lax.dot_general(
        left, right, (((left_axis,), (right_axis,)), ((), ())), preferred_element_type=WIDE
    )


def lay(block_lists, cuts, weights_ref, arrived):
    @pl.when(pl.program_id(0) == 0)
    def _():
        copies, column = [], 0
        for blocks, (start, width) in zip(block_lists, cuts):
            at = 0
            for block in blocks:
                depth = block.shape[0]
                copy = pltpu.make_async_copy(
                    block.at[:, pl.ds(start, width)],
                    weights_ref.at[pl.ds(at, depth), pl.ds(column, width)],
                    arrived.at[len(copies)],
                )
                copy.start()
                copies.append(copy)
                at += depth
            column += width
        for copy in copies:
            copy.wait()


def laid(features, width, *block_lists):
    count = sum(len(blocks) for blocks in block_lists)
    return [pltpu.VMEM((features, width), LOW), pltpu.SemaphoreType.DMA((count,))]


ANYWHERE = pl.BlockSpec(memory_space=pl.ANY)


def whole_spec(array):
    return pl.BlockSpec(array.shape, lambda i: (0, 0))


def row_spec(rows, array):
    return pl.BlockSpec((rows, array.shape[1]), lambda i: (i, 0))


GELU_A, GELU_B = (2 / math.pi) ** 0.5, 0.044715


def hidden_kernel(rows_ref, shift_ref, *refs):
    blocks, (slope_ref, hidden_ref, weights_ref, arrived) = refs[:-4], refs[-4:]
    lay([blocks], [(0, slope_ref.shape[1])], weights_ref, arrived)
    pre = dot(rows_ref[...], weights_ref[...], 1, 0) + shift_ref[...]
    square = pre * pre
    bend = jnp.tanh(GELU_A * (pre + GELU_B * (square * pre)))
    raised = 0.5 * (1.0 + bend)
    hidden_ref[...] = (pre * raised).astype(LOW)
    slope = raised + 0.5 * pre * (1.0 - bend * bend) * (GELU_A * (1.0 + 3.0 * GELU_B * square))
    slope_ref[...] = slope.astype(LOW)


def hidden_units(rows, shift, blocks):
    count, features = rows.shape
    width = blocks[0].shape[1]
    tile = count // 4
    return pl.pallas_call(
        hidden_kernel,
        grid=(4,),
        in_specs=[row_spec(tile, rows), whole_spec(shift)] + [ANYWHERE] * len(blocks),
        out_specs=[pl.BlockSpec((tile, width), lambda i: (i, 0))] * 2,
        out_shape=[jax.ShapeDtypeStruct((count, width), LOW)] * 2,
        scratch_shapes=laid(features, width, blocks),
        compiler_params=pltpu.CompilerParams(vmem_limit_bytes=VMEM_LIMIT),
        cost_estimate=cost(2 * rows.size * width, 2 * rows.size + 6 * count * width),
    )(rows, shift, *blocks)


def d_pre_kernel(rows_ref, slope_ref, *refs):
    blocks, (d_pre_ref, sums_ref, weights_ref, arrived) = refs[:-4], refs[-4:]

    @pl.when(pl.program_id(0) == 0)
    def _():
        sums_ref[...] = jnp.zeros_like(sums_ref)

    lay([blocks], [(0, slope_ref.shape[1])], weights_ref, arrived)
    d_hidden = dot(rows_ref[...], weights_ref[...], 1, 0)
    low = (d_hidden * slope_ref[...].astype(WIDE)).astype(LOW)
    d_pre_ref[...] = low
    sums_ref[...] += jnp.sum(low.astype(WIDE), axis=0, keepdims=True)


def d_pre_units(rows, slope, blocks):
    count, width = slope.shape
    tile = count // 4
    return pl.pallas_call(
        d_pre_kernel,
        grid=(4,),
        in_specs=[row_spec(tile, rows), row_spec(tile, slope)] + [ANYWHERE] * len(blocks),
        out_specs=[
            pl.BlockSpec((tile, width), lambda i: (i, 0)),
            pl.BlockSpec((1, width), lambda i: (0, 0)),
        ],
        out_shape=[
            jax.ShapeDtypeStruct((count, width), LOW),
            jax.ShapeDtypeStruct((1, width), WIDE),
        ],
        scratch_shapes=laid(rows.shape[1], width, blocks),
        compiler_params=pltpu.CompilerParams(vmem_limit_bytes=VMEM_LIMIT),
        cost_estimate=cost(2 * rows.size * width, 2 * rows.size + 6 * count * width),
    )(rows, slope, *blocks)


def gradient_kernel(pairs, *refs):
    operands, outs = refs[: 2 * pairs], refs[2 * pairs :]

    def write(out):
        column = 0
        for i in range(pairs):
            part = dot(operands[2 * i][...], operands[2 * i + 1][...], 0, 0).astype(LOW)
            out[:, column : column + part.shape[1]] = part
            column += part.shape[1]

    for step, out in enumerate(outs):
        pl.when(pl.program_id(0) == step)(functools.partial(write, out))


def gradient_blocks(place, *pairs):
    count, features = pairs[0][0].shape
    steps = len(place.masks)
    rows = features // steps
    width = sum(right.shape[1] for _, right in pairs)
    specs = []
    for _, right in pairs:
        specs += [pl.BlockSpec((count, rows), lambda i: (0, i)), whole_spec(right)]
    outs = pl.pallas_call(
        functools.partial(gradient_kernel, len(pairs)),
        grid=(steps,),
        in_specs=specs,
        out_specs=[pl.BlockSpec((rows, width), lambda i: (0, 0))] * steps,
        out_shape=[jax.ShapeDtypeStruct((rows, width), LOW)] * steps,
        compiler_params=pltpu.CompilerParams(vmem_limit_bytes=VMEM_LIMIT),
        cost_estimate=cost(2 * count * features * width, 2 * count * (features + width)),
    )(*[array for pair in pairs for array in pair])
    return dict(zip(place.masks, outs))


def spread_kernel(cuts, counts, summed, *refs):
    if summed:
        (normed_ref, vectors_ref), refs = refs[:2], refs[2:]
        sums_ref, refs = refs[-3], refs[:-3] + refs[-2:]
    lefts, rest = refs[: len(cuts)], refs[len(cuts) :]
    block_lists = []
    for count in counts:
        block_lists.append(rest[:count])
        rest = rest[count:]
    far_ref, near_ref, weights_ref, arrived = rest
    lay(block_lists, cuts, weights_ref, arrived)
    left = jnp.concatenate([ref[...] for ref in lefts], axis=1)

    def write(out):
        total = dot(left, weights_ref[...], 1, 1)
        out[...] = total.astype(LOW)
        if summed:
            unit = normed_ref[...].astype(WIDE) - vectors_ref[1:2]
            sums_ref[0:1] += jnp.sum(total * unit, axis=0, keepdims=True)
            sums_ref[1:2] += jnp.sum(total, axis=0, keepdims=True)

    if summed:

        @pl.when(pl.program_id(0) == 0)
        def _():
            sums_ref[...] = jnp.zeros_like(sums_ref)

    pl.when(pl.program_id(0) < 2)(lambda: write(far_ref))
    pl.when(pl.program_id(0) >= 2)(lambda: write(near_ref))


def spread(lefts, block_lists, cuts, *unit):
    count = lefts[0].shape[0]
    tile = count // 4
    features = sum(b.shape[0] for b in block_lists[0])
    depth = sum(width for _, width in cuts)
    return pl.pallas_call(
        functools.partial(spread_kernel, cuts, [len(b) for b in block_lists], bool(unit)),
        grid=(4,),
        in_specs=[
            pl.BlockSpec((tile, rows.shape[1]), lambda i: ((i + 2) % 4, 0)) for rows in unit[:1]
        ]
        + [whole_spec(vectors) for vectors in unit[1:]]
        + [pl.BlockSpec((tile, left.shape[1]), lambda i: ((i + 2) % 4, 0)) for left in lefts]
        + [ANYWHERE] * sum(len(blocks) for blocks in block_lists),
        out_specs=[
            pl.BlockSpec((tile, features), lambda i: (jnp.minimum(i, 1), 0)),
            pl.BlockSpec((tile, features), lambda i: (jnp.maximum(i - 2, 0), 0)),
        ]
        + [pl.BlockSpec((2, features), lambda i: (0, 0)) for _ in unit[:1]],
        out_shape=[jax.ShapeDtypeStruct((count // 2, features), LOW)] * 2
        + [jax.ShapeDtypeStruct((2, features), WIDE) for _ in unit[:1]],
        scratch_shapes=laid(features, depth, *block_lists),
        compiler_params=pltpu.CompilerParams(vmem_limit_bytes=VMEM_LIMIT),
        cost_estimate=cost(2 * count * features * depth, 2 * count * (features + depth)),
    )(*unit, *lefts, *[b for blocks in block_lists for b in blocks])


PAIR = 2 * HD
SCALE = HD ** (-0.5)
TILES = 2


def turn(pair, cosine, sine):
    half = ROTARY // 2
    lane = lax.broadcasted_iota(jnp.int32, pair.shape, 1) % HD
    partner = jnp.where(lane < half, pltpu.roll(pair, PAIR - half, 1), pltpu.roll(pair, half, 1))
    return pair * cosine + partner * sine


def two_heads(pair):
    lane = lax.broadcasted_iota(jnp.int32, pair.shape, 1) // HD
    zero = jnp.zeros_like(pair)
    return jnp.concatenate([jnp.where(lane == head, pair, zero) for head in range(2)])


def either(stacked):
    rows = stacked.shape[0] // 2
    lane = lax.broadcasted_iota(jnp.int32, (rows, PAIR), 1) // HD
    return jnp.where(lane == 0, stacked[:rows], stacked[rows:])


def seen(ids_col, ids_row, first, rows, width):
    key = lax.broadcasted_iota(jnp.int32, (width, rows), 0)
    query = lax.broadcasted_iota(jnp.int32, (width, rows), 1) + first
    mask = (ids_col[:width] == ids_row[:, first : first + rows]) & (key <= query)
    return jnp.concatenate([mask, mask], axis=1)


def halves(y_ref, rows, cos_ref, sin_ref):
    places = [pl.ds(pl.multiple_of((y_ref[0] ^ t) * rows, 128), rows) for t in range(TILES)]
    cuts = [slice(t * rows, (t + 1) * rows) for t in range(TILES)]
    return places, [(cos_ref[cut], sin_ref[cut]) for cut in cuts]


def forward_kernel(y_ref, rows_ref, shift_ref, cos_ref, sin_ref, col_ref, row_ref, *refs):
    blocks, outs, (joint_ref, weights_ref, arrived) = refs[:-6], refs[-6:-3], refs[-3:]
    turned_ref, context_ref, log_ref = outs
    slots, width = context_ref.shape
    lay([blocks], [(0, 3 * width)], weights_ref, arrived)
    joint_ref[...] = dot(rows_ref[...], weights_ref[...], 1, 0)
    ids_col, ids_row = col_ref[...], row_ref[0]
    rows = slots // TILES
    masks = [seen(ids_col, ids_row, t * rows, rows, (t + 1) * rows) for t in range(TILES)]
    places, tables = halves(y_ref, rows, cos_ref, sin_ref)
    log_ref[...] = jnp.zeros_like(log_ref)
    for p in range(width // PAIR):
        columns = [slice(j * width + p * PAIR, j * width + (p + 1) * PAIR) for j in range(3)]
        query, key, value = [], [], []
        for place, table in zip(places, tables):
            parts = [joint_ref[place, c] + shift_ref[:, c] for c in columns]
            query.append(turn(parts[0], *table).astype(LOW))
            key.append(turn(parts[1], *table).astype(LOW))
            value.append(parts[2].astype(LOW))
            for c, array in zip(columns, (query, key, value)):
                turned_ref[place, c] = array[-1]
        key, value = jnp.concatenate(key), jnp.concatenate(value)
        for t in range(TILES):
            keys = (t + 1) * rows
            scores = dot(key[:keys], two_heads(query[t] * SCALE), 1, 1)
            scores = jnp.where(masks[t], scores, -1e30)
            top = jnp.max(scores, axis=0, keepdims=True)
            raised = jnp.exp(scores - top)
            total = jnp.sum(raised, axis=0, keepdims=True)
            probs = (raised * (1.0 / total)).astype(LOW)
            out = dot(probs, value[:keys], 0, 0)
            log_total = top + jnp.log(total)
            for head in range(2):
                log_ref[2 * p + head : 2 * p + head + 1, t * rows : (t + 1) * rows] = log_total[
                    :, head * rows : (head + 1) * rows
                ]
            context_ref[places[t], p * PAIR : (p + 1) * PAIR] = either(out).astype(LOW)


def backward_kernel(y_ref, turned_ref, rows_ref, log_ref, cos_ref, sin_ref, col_ref, row_ref, *refs):
    blocks, outs, (back_ref, weights_ref, arrived) = refs[:-5], refs[-5:-3], refs[-3:]
    joint_ref, sums_ref = outs
    slots, width = back_ref.shape
    lay([blocks], [(3 * width, width)], weights_ref, arrived)
    back_ref[...] = dot(rows_ref[...], weights_ref[...], 1, 0).astype(LOW)
    ids_col, ids_row = col_ref[...], row_ref[0]
    rows = slots // TILES
    masks = [seen(ids_col, ids_row, t * rows, rows, (t + 1) * rows) for t in range(TILES)]
    places, tables = halves(y_ref, rows, cos_ref, sin_ref)

    @pl.when(pl.program_id(0) == 0)
    def _():
        sums_ref[...] = jnp.zeros_like(sums_ref)

    for p in range(width // PAIR):
        columns = [slice(j * width + p * PAIR, j * width + (p + 1) * PAIR) for j in range(3)]
        key, value = (
            jnp.concatenate([turned_ref[place, c] for place in places]) for c in columns[1:]
        )
        d_query, d_key, d_value = [], [], []
        for t, place in enumerate(places):
            here, keys = slice(t * rows, (t + 1) * rows), (t + 1) * rows
            query = two_heads(turned_ref[place, columns[0]] * SCALE)
            d_context = two_heads(back_ref[place, p * PAIR : (p + 1) * PAIR])
            logs = jnp.concatenate(
                [log_ref[2 * p + head : 2 * p + head + 1, here] for head in range(2)], axis=1
            )
            scores = dot(key[:keys], query, 1, 1)
            probs = jnp.where(masks[t], jnp.exp(scores - logs), 0.0)
            d_probs = dot(value[:keys], d_context, 1, 1)
            delta = jnp.sum(probs * d_probs, axis=0, keepdims=True)
            d_scores = (probs * (d_probs - delta)).astype(LOW)
            d_query.append(either(dot(d_scores, key[:keys], 0, 0)) * SCALE)
            d_key.append(dot(d_scores, query, 1, 0))
            d_value.append(dot(probs.astype(LOW), d_context, 1, 0))
        for t, (place, (cosine, sine)) in enumerate(zip(places, tables)):
            here = slice(t * rows, (t + 1) * rows)
            parts = (
                turn(d_query[t], cosine, -sine),
                turn(sum(d[here] for d in d_key[t:]), cosine, -sine),
                sum(d[here] for d in d_value[t:]),
            )
            for c, array in zip(columns, parts):
                low = array.astype(LOW)
                joint_ref[place, c] = low
                sums_ref[:, c] += jnp.sum(low.astype(WIDE), axis=0, keepdims=True)


def by_group(slots, width):
    return pl.BlockSpec((slots, width), lambda g: (g, 0))


def attention_forward(place, normed, head_shift, cosine, sine, ids, blocks):
    groups, slots = ids.shape
    rows, width = normed.shape[0], blocks[0].shape[1] // 4
    return pl.pallas_call(
        forward_kernel,
        grid=(groups,),
        in_specs=[
            pl.BlockSpec(memory_space=pltpu.SMEM),
            row_spec(slots, normed),
            pl.BlockSpec((1, 3 * width), lambda g: (0, 0)),
            by_group(slots, PAIR),
            by_group(slots, PAIR),
            by_group(slots, 1),
            pl.BlockSpec((1, 1, slots), lambda g: (g, 0, 0)),
        ]
        + [ANYWHERE] * len(blocks),
        out_specs=[by_group(slots, 3 * width), by_group(slots, width), by_group(8, slots)],
        out_shape=[
            jax.ShapeDtypeStruct((rows, 3 * width), LOW),
            jax.ShapeDtypeStruct((rows, width), LOW),
            jax.ShapeDtypeStruct((8 * groups, slots), WIDE),
        ],
        scratch_shapes=[pltpu.VMEM((slots, 3 * width), WIDE)]
        + laid(normed.shape[1], 3 * width, blocks),
        compiler_params=pltpu.CompilerParams(vmem_limit_bytes=VMEM_LIMIT),
        cost_estimate=cost(20 * rows * slots * width + 6 * normed.size * width, 2 * normed.size),
    )(place.y.reshape(1), normed, head_shift[None], cosine, sine, ids.reshape(-1, 1), ids[:, None], *blocks)


def attention_backward(place, turned, grad, logs, cosine, sine, ids, blocks):
    groups, slots = ids.shape
    rows, width = grad.shape[0], blocks[0].shape[1] // 4
    return pl.pallas_call(
        backward_kernel,
        grid=(groups,),
        in_specs=[
            pl.BlockSpec(memory_space=pltpu.SMEM),
            by_group(slots, 3 * width),
            row_spec(slots, grad),
            by_group(8, slots),
            by_group(slots, PAIR),
            by_group(slots, PAIR),
            by_group(slots, 1),
            pl.BlockSpec((1, 1, slots), lambda g: (g, 0, 0)),
        ]
        + [ANYWHERE] * len(blocks),
        out_specs=[by_group(slots, 3 * width), pl.BlockSpec((1, 3 * width), lambda g: (0, 0))],
        out_shape=[
            jax.ShapeDtypeStruct((rows, 3 * width), LOW),
            jax.ShapeDtypeStruct((1, 3 * width), WIDE),
        ],
        scratch_shapes=[pltpu.VMEM((slots, width), LOW)] + laid(grad.shape[1], width, blocks),
        compiler_params=pltpu.CompilerParams(vmem_limit_bytes=VMEM_LIMIT),
        cost_estimate=cost(50 * rows * slots * width + 2 * grad.size * width, 2 * grad.size),
    )(place.y.reshape(1), turned, grad, logs, cosine, sine, ids.reshape(-1, 1), ids[:, None], *blocks)


def body(
    dp_size,
    tensor_size,
    tokens,
    cotangent,
    segment_ids,
    joint_weight,
    dense_weight,
    expand_weight,
    shrink_weight,
    head_bias,
    unit_bias,
    row_vectors,
    joint_mean,
    joint_square,
    dense_mean,
    dense_square,
    expand_mean,
    expand_square,
    shrink_mean,
    shrink_square,
    head_mean,
    head_square,
    unit_mean,
    unit_square,
    rows_mean,
    rows_square,
):
    place = Place(dp_size, tensor_size)
    devices = dp_size * tensor_size
    my_rows = tokens.shape[0]
    features = tokens.shape[1]
    group_slots = segment_ids.shape[0]
    shard_rows = joint_weight.shape[0]
    block_rows = 4 * shard_rows
    heads = head_bias.shape[2] // 4
    units = unit_bias.shape[1] // 4
    joint_width, unit_width = heads * HD, units * HD

    def kinds_first(array):
        return array.transpose(1, 0, 2)

    side, core = place.side, place.core
    first, second = place.ring[:2]
    small = SmallGather(
        place,
        jnp.concatenate(
            [
                row_vectors.reshape(-1),
                head_bias.reshape(-1),
                unit_bias.reshape(-1),
                segment_ids.astype(WIDE),
            ]
        ),
    )

    joint_shard = kinds_first(joint_weight)
    quarters = pack(place, joint_shard, dense_weight[None])
    by_core = place.move(quarters[1], core)
    by_side = place.move(quarters[2], side)
    by_both = place.move(quarters[3], side | core)
    small.step(0, 1, by_core)
    small.step(core)
    small.step(second)
    mine = arrange(place, tokens)
    near_quarters = pack(place, expand_weight[None], shrink_weight[None])
    my_ids = lax.dynamic_slice_in_dim(segment_ids, place.y * my_rows, my_rows)
    masked = arrange(place, cotangent * (my_ids > 0).astype(LOW)[:, None])
    blocks = stack(place, (quarters[0], by_core, by_side, by_both), (4 * joint_width,))[0]
    block, joint = blocks[0], Gather(place, *blocks)

    ready = (block, small.rows, mine)
    got = [
        joint.along_first(0),
        joint.along_second(),
        place.move(after(mine, *ready), side),
        place.move(after(mine, *ready), 0, 1),
        place.move(
            after(jnp.concatenate([near_quarters[1], near_quarters[3]]), *ready), core
        ),
    ]
    mine_side, mine_y, by_core = got[2:5]

    ready = tuple(got)
    got = [
        joint.along_first(1, *ready),
        joint.onward(0, *ready),
        place.move(after(mine_side, *ready), 0, 1),
        place.move(
            after(jnp.concatenate([near_quarters[2], by_core[shard_rows:]]), *ready), side
        ),
        small.step(first, 0, *ready),
    ]
    corner, by_side = got[2:4]
    near = join(mine, mine_y, mine_side, corner)
    blocks = stack(
        place, (near_quarters[0], by_core[:shard_rows], by_side), (unit_width, unit_width)
    )
    expand, shrink = (Gather(place, *array) for array in blocks)

    ready = tuple(got) + (blocks[0][0],)
    got = [
        expand.along_first(0, *ready),
        joint.onward(1, *ready),
        place.move(after(masked, *ready), side),
        place.move(after(masked, *ready), 0, 1),
        small.step(side, 0, *ready),
    ]
    masked_side, masked_y = got[2:4]

    cuts = [row_vectors.size, row_vectors.size + head_bias.size]
    cuts.append(cuts[1] + unit_bias.size)
    rows_small, head_small, unit_small, ids_small = jnp.split(small.whole(), cuts, axis=1)
    row_whole = rows_small.reshape(devices, 4, -1).transpose(1, 0, 2).reshape(4, features)
    head_small = pick(head_small.reshape((dp_size, tensor_size) + head_bias.shape), place.y, 1)
    head_low = lax.dynamic_slice_in_dim(head_small, place.quarter * heads, heads, 3)
    head_shift = head_low.reshape(HD, 3, heads).astype(LOW).astype(WIDE)
    head_shift = head_shift.transpose(1, 2, 0).reshape(-1)
    unit_small = pick(unit_small.reshape((dp_size, tensor_size) + unit_bias.shape), place.y, 1)
    unit_low = lax.dynamic_slice_in_dim(unit_small, place.quarter * units, units, 2)
    unit_shift = unit_low.reshape(HD, units).astype(LOW).astype(WIDE).T.reshape(-1)
    ids_small = ids_small.reshape(dp_size, tensor_size, group_slots)[:, 0]
    distances = (0, place.side, place.core, place.side | place.core)
    ids = jnp.stack([pick(ids_small, place.index ^ d) for d in distances])

    own_vectors = arrange(place, row_whole)
    positions = jax.vmap(doc_positions)(ids)[0].reshape(-1, 1)
    lane = jnp.arange(PAIR) % HD
    half_rot = ROTARY // 2
    frequency = 10000.0 ** (-(lane % half_rot).astype(WIDE) / half_rot)
    angles = positions * frequency
    cosine = jnp.where(lane < ROTARY, jnp.cos(angles), 1.0)
    sine = jnp.sin(angles)
    sine = jnp.where(lane < half_rot, -sine, jnp.where(lane < ROTARY, sine, 0.0))

    ready = tuple(got) + (cosine, sine, own_vectors, head_shift, unit_shift)
    got = [
        expand.along_first(1, *ready),
        expand.along_second(*ready),
        place.move(after(masked_side, *ready), 0, 1),
        place.move(after(near, *ready), core),
    ]
    normed = norm((mine, mine_y, mine_side, corner), got[3], own_vectors)
    grad_near = join(after(masked, normed), masked_y, masked_side, got[2])

    ready = tuple(got) + (grad_near, normed)
    got = [
        shrink.along_first(0, *ready),
        expand.onward(0, *ready),
        expand.onward(1, *ready),
        place.move(after(grad_near, *ready), core),
    ]
    joint = joint.whole()
    turned, context, logs = attention_forward(
        place, after(normed, *ready), head_shift, cosine, sine, ids, joint
    )

    ready = tuple(got) + (context,)
    grad_all = join(grad_near, got[3])
    got = [
        shrink.along_first(1, *ready),
        shrink.onward(0, *ready),
        shrink.along_second(*ready),
    ]
    d_joint, joint_sums = attention_backward(
        place, turned, after(grad_all, *ready), logs, cosine, sine, ids, joint
    )
    expand = expand.whole()

    ready = tuple(got) + (d_joint,)
    got = [shrink.onward(1, *ready)]
    shrink = shrink.whole()
    sum_joint = Reduce(place, (after(normed, *ready), d_joint), (grad_all, context))

    def returned(reduce, *others):
        return list(choose(place, [after(half, *others) for half in reduce.sums]))

    ready = tuple(got) + tuple(sum_joint.parts.values())
    slope, hidden = hidden_units(after(normed, *ready), unit_shift[None], expand)
    got = sum_joint.send_both(*ready, before=(hidden,))

    ready = got + (hidden,)
    sum_shrink = Reduce(place, (after(grad_all, *ready), hidden))
    d_pre, unit_sums = d_pre_units(after(grad_all, *sum_shrink.parts.values()), slope, shrink)
    got = sum_joint.send_second(*ready, before=(d_pre,))
    got += sum_joint.send_half(0, *ready, before=(d_pre,))

    ready = got + (d_pre,)
    outer = GroupSum(
        place,
        *spread(
            [after(context, *ready), hidden],
            [joint, shrink],
            ((3 * joint_width, joint_width), (0, unit_width)),
        ),
    )
    got = sum_shrink.send_both(*ready, before=(outer.far,))
    got += sum_joint.send_half(1, *ready, before=(outer.far,))

    ready = got + (outer.far,)
    sum_expand = Reduce(place, (after(normed, *ready), d_pre))
    before = tuple(sum_expand.parts.values())
    got = sum_shrink.send_second(*ready, before=before)
    got += sum_shrink.send_half(0, *ready, before=before)
    outer_sent = outer.by_core(*ready)
    g_joint = returned(sum_joint, *ready)
    g_joint[1] = place.move(g_joint[1], core)
    g_joint[2] = place.move(g_joint[2], side)

    ready = got + before + tuple(outer_sent) + tuple(g_joint[1:3])
    inner_far, inner_near, inner_sums = spread(
        [after(d_joint, *ready), d_pre],
        [joint, expand],
        ((0, 3 * joint_width), (0, unit_width)),
        normed,
        own_vectors,
    )
    inner = GroupSum(place, inner_far, inner_near)
    got = sum_expand.send_both(*ready, before=(inner.far,))
    got += sum_shrink.send_half(1, *ready, before=(inner.far,))
    outer_sent = outer.hop(*ready)
    g_joint[3] = place.move(after(g_joint[3], *ready), side | core)

    ready = got + (inner.far, g_joint[3]) + tuple(outer_sent)
    own_sums = jnp.concatenate([joint_sums[0], unit_sums[0]])
    row_sums = jnp.concatenate(
        [
            inner_sums[0:1] / own_vectors[0:1],
            inner_sums[1:2],
            jnp.sum(masked, axis=0, dtype=WIDE, keepdims=True),
        ]
    )
    sums = SmallReduce(place, own_sums, arrange(place, row_sums, True).reshape(-1))
    sent = inner.by_core(*ready)
    got = sum_expand.send_second(*ready) + sum_expand.send_half(0, *ready)
    branch = outer.last_hop(*ready)
    g_shrink = returned(sum_shrink, *ready)

    ready = got + tuple(sent) + (branch,)
    got = sum_expand.send_half(1, *ready)
    sent = inner.hop(*ready)
    for flip, mask in ((1, core), (2, side), (3, side | core)):
        g_shrink[flip] = place.move(after(g_shrink[flip], *ready), mask)

    ready = got + tuple(sent) + tuple(g_shrink[1:])
    g_expand = returned(sum_expand, *ready)
    for flip, mask in ((1, core), (2, side), (3, side | core)):
        g_expand[flip] = place.move(g_expand[flip], mask)
    d_normed = inner.last_hop(*ready)
    g_joint[0] = after(g_joint[0], *ready)

    def shard_update(pieces, column, weight, moment, square, step_rate):
        news = adam_shard(
            place, pieces, column, weight[None], moment[None], square[None], step_rate
        )
        return [new[0] for new in news]

    joint_new = adam_shard(
        place,
        g_joint,
        0,
        joint_shard,
        kinds_first(joint_mean),
        kinds_first(joint_square),
        D ** (-0.5),
    )
    dense_new = shard_update(
        g_joint, 3 * joint_width, dense_weight, dense_mean, dense_square, (D // 32) ** (-0.5)
    )

    sums.vector = after(sums.vector, joint_new[0], dense_new[0], *g_expand[1:])
    sums.step((core, 0), (0, 1), (core, 1))
    shrink_new = shard_update(g_shrink, 0, shrink_weight, shrink_mean, shrink_square, FF ** (-0.5))
    sums.vector = after(sums.vector, shrink_new[0])
    sums.step((side, 0), (second, 0), (side | second, 0))
    g_expand[0] = after(g_expand[0], shrink_new[0])
    expand_new = shard_update(g_expand, 0, expand_weight, expand_mean, expand_square, D ** (-0.5))
    sums.vector = after(sums.vector, expand_new[0])
    for bit in place.ring:
        if bit != second:
            sums.step((bit, 0))
    own_sums, row_sums = sums.results()

    layer_output = mine.astype(WIDE) + branch + own_vectors[2] + own_vectors[3]
    layer_output = arrange(place, layer_output.astype(LOW), True)
    inputs = mine.astype(WIDE)
    centered = inputs - jnp.mean(inputs, axis=-1, keepdims=True)
    inverse = lax.rsqrt(jnp.mean(centered * centered, axis=-1, keepdims=True) + EPS_NORM)
    unit_rows = centered * inverse
    d_unit_rows = d_normed * own_vectors[0]
    d_inputs = inverse * (
        d_unit_rows
        - jnp.mean(d_unit_rows, axis=-1, keepdims=True)
        - unit_rows * jnp.mean(d_unit_rows * unit_rows, axis=-1, keepdims=True)
    )
    input_grad = arrange(place, masked.astype(WIDE) + d_inputs, True)

    features_here = HD // dp_size
    g_head = own_sums[:, : 3 * joint_width].reshape(4, 3, heads, HD)
    g_head = lax.dynamic_slice_in_dim(g_head, place.index * features_here, features_here, 3)
    g_head = g_head.transpose(3, 1, 0, 2).reshape(head_bias.shape)
    g_unit = own_sums[:, 3 * joint_width :].reshape(4 * units, HD)
    g_unit = lax.dynamic_slice_in_dim(g_unit, place.index * features_here, features_here, 1).T
    row_sums = row_sums.reshape(3, features)
    row_width = row_vectors.shape[1]
    g_rows = lax.dynamic_slice_in_dim(
        row_sums, (place.index * tensor_size + place.y) * row_width, row_width, 1
    )
    g_rows = jnp.concatenate([g_rows, g_rows[2:]])

    joint_new = [kinds_first(new) for new in joint_new]
    head_new = adam_update(head_bias, g_head, head_mean, head_square, 0.1, 0.0)
    unit_new = adam_update(unit_bias, g_unit, unit_mean, unit_square, 0.1, 0.0)
    rows_new = adam_update(row_vectors, g_rows, rows_mean, rows_square, 0.1, 0.0)
    return (
        layer_output,
        input_grad,
        joint_new[0],
        joint_new[1],
        joint_new[2],
        dense_new[0],
        dense_new[1],
        dense_new[2],
        expand_new[0],
        expand_new[1],
        expand_new[2],
        shrink_new[0],
        shrink_new[1],
        shrink_new[2],
        head_new[0],
        head_new[1],
        head_new[2],
        unit_new[0],
        unit_new[1],
        unit_new[2],
        rows_new[0],
        rows_new[1],
        rows_new[2],
    )


def solution(mesh):
    return jax.shard_map(
        functools.partial(body, mesh.shape["dp"], mesh.shape["tensor"]),
        mesh=mesh,
        in_specs=(
            P(("dp", "tensor"), None),
            P(("dp", "tensor"), None),
            P("dp"),
            P("dp", None, "tensor"),
            P("dp", "tensor"),
            P("dp", "tensor"),
            P("dp", "tensor"),
            P("dp", None, "tensor"),
            P("dp", "tensor"),
            P(None, ("dp", "tensor")),
            P("dp", None, "tensor"),
            P("dp", None, "tensor"),
            P("dp", "tensor"),
            P("dp", "tensor"),
            P("dp", "tensor"),
            P("dp", "tensor"),
            P("dp", "tensor"),
            P("dp", "tensor"),
            P("dp", None, "tensor"),
            P("dp", None, "tensor"),
            P("dp", "tensor"),
            P("dp", "tensor"),
            P(None, ("dp", "tensor")),
            P(None, ("dp", "tensor")),
        ),
        out_specs=(
            P(("dp", "tensor"), None),
            P(("dp", "tensor"), None),
            P("dp", None, "tensor"),
            P("dp", None, "tensor"),
            P("dp", None, "tensor"),
            P("dp", "tensor"),
            P("dp", "tensor"),
            P("dp", "tensor"),
            P("dp", "tensor"),
            P("dp", "tensor"),
            P("dp", "tensor"),
            P("dp", "tensor"),
            P("dp", "tensor"),
            P("dp", "tensor"),
            P("dp", None, "tensor"),
            P("dp", None, "tensor"),
            P("dp", None, "tensor"),
            P("dp", "tensor"),
            P("dp", "tensor"),
            P("dp", "tensor"),
            P(None, ("dp", "tensor")),
            P(None, ("dp", "tensor")),
            P(None, ("dp", "tensor")),
        ),
        check_vma=False,
    )
```

```python
import functools
import math

import jax
import jax.numpy as jnp
from jax import lax
from jax.experimental import pallas as pl
from jax.experimental.pallas import tpu as pltpu
from jax.sharding import PartitionSpec as P

D = 2048
HD = 64
FF = 8192
ROTARY = 32
STEP = 10


EPS_NORM = 1e-05
BETA_ONE = 0.9
BETA_TWO = 0.95
EPS_ADAM = 1e-08
WEIGHT_DECAY = 0.1


def doc_positions(segments):
    row_count = segments.shape[0]
    places = jnp.arange(row_count, dtype=jnp.int32)
    same_doc = segments[:, None] == segments[None, :]
    starts = jnp.min(jnp.where(same_doc, places[None, :], row_count), axis=1)
    allowed = same_doc & (places[None, :] <= places[:, None])
    return ((places - starts).astype(jnp.float32), allowed)


def adam_update(weight, gradient, moment, square, step_rate, decay_rate):
    new_moment = BETA_ONE * moment + (1.0 - BETA_ONE) * gradient
    new_square = BETA_TWO * square + (1.0 - BETA_TWO) * gradient * gradient
    fix_one = 1.0 - BETA_ONE**STEP
    fix_two = 1.0 - BETA_TWO**STEP
    update = new_moment / fix_one / (jnp.sqrt(new_square / fix_two) + EPS_ADAM)
    return (weight - step_rate * (update + decay_rate * weight), new_moment, new_square)


AXES = ("dp", "tensor")
LOW = jnp.bfloat16
WIDE = jnp.float32


def after(array, *others):
    others = [o for o in others if o is not None]
    return lax.optimization_barrier((array, *others))[0] if others else array


def cost(flops, nbytes):
    return pl.CostEstimate(flops=int(flops) >> 10, bytes_accessed=int(nbytes) >> 10, transcendentals=0)


class Place:
    def __init__(self, dp_size, tensor_size):
        count = dp_size.bit_length() - 1
        self.dp_size, self.tensors, self.count = dp_size, tensor_size, count
        self.core, self.side = 1, 1 << (count - 2)
        self.ring = [1 << b for b in range(count - 1, 0, -1) if 1 << b != self.side]
        self.index = lax.axis_index("dp")
        self.y = lax.axis_index("tensor")
        self.quarter = self.bit(self.side) * 2 + self.bit(self.core)
        self.masks = [0]
        for bit in reversed(self.ring):
            self.masks = self.masks + [m | bit for m in self.masks]
        self.last = {}

    def bit(self, mask):
        return (self.index // mask) % 2

    def move(self, array, mask, y=0, lane=None):
        pairs = []
        for dp in range(self.dp_size):
            for oy in range(self.tensors):
                pairs.append((dp * self.tensors + oy, (dp ^ mask) * self.tensors + (oy ^ y)))
        if lane is not None:
            array = after(array, self.last.get(lane))
        got = lax.ppermute(array, AXES, pairs)
        if lane is not None:
            self.last[lane] = got
        return got

    def to_own_order(self, array):
        lead = array.shape[:-1]
        split = array.reshape(lead + (2,) * self.count + (-1,))
        first = len(lead)
        ring_axes = [first + self.count - bit.bit_length() for bit in self.ring]
        for bit, axis in zip(self.ring, ring_axes):
            split = jnp.where(self.bit(bit) == 0, split, jnp.flip(split, axis))
        rest = [first + b for b in range(self.count + 1) if first + b not in ring_axes]
        split = split.transpose(list(range(first)) + ring_axes + rest)
        return split.reshape(array.shape)

    def to_index_order(self, array):
        lead = array.shape[:-1]
        split = array.reshape(lead + (2,) * self.count + (-1,))
        first = len(lead)
        ring_axes = [first + self.count - bit.bit_length() for bit in self.ring]
        rest = [first + b for b in range(self.count + 1) if first + b not in ring_axes]
        order = list(range(first)) + ring_axes + rest
        split = split.transpose([order.index(i) for i in range(len(order))])
        for bit, axis in zip(self.ring, ring_axes):
            split = jnp.where(self.bit(bit) == 0, split, jnp.flip(split, axis))
        return split.reshape(array.shape)


def as_hbm(shapes):
    if not isinstance(shapes, list):
        return as_hbm([shapes])[0]
    return [pltpu.HBM(s.shape, s.dtype) if s.size > 1 << 16 else s for s in shapes]


def in_hbm(*arrays):
    return [
        pltpu.with_memory_space_constraint(a, pltpu.HBM) if a.size > 1 << 16 else a for a in arrays
    ]


def pick(array, index, axis=0):
    return lax.dynamic_index_in_dim(array, index, axis, keepdims=False)


def swap_quarters(place, pieces):
    return [
        pieces[0],
        place.move(pieces[1], place.core),
        place.move(pieces[2], place.side),
        place.move(pieces[3], place.side | place.core),
    ]


def arrange_kernel(back, statics, own_ref, array_ref, out_ref):
    width = array_ref.shape[1] // len(statics)
    for r, static in enumerate(statics):
        at = pl.multiple_of((own_ref[0] ^ static) * width, 128)
        here = slice(r * width, (r + 1) * width)
        if back:
            out_ref[:, pl.ds(at, width)] = array_ref[:, here]
        else:
            out_ref[:, here] = array_ref[:, pl.ds(at, width)]


def arrange(place, array, back=False):
    if array.shape[1] // place.dp_size % 128:
        return place.to_index_order(array) if back else place.to_own_order(array)
    ring = sum(place.ring)
    inner = (0, place.core, place.side, place.side | place.core)
    statics = [mask | i for mask in place.masks for i in inner]
    return pl.pallas_call(
        functools.partial(arrange_kernel, back, statics),
        in_specs=[
            pl.BlockSpec(memory_space=pltpu.SMEM),
            pl.BlockSpec(memory_space=pltpu.VMEM),
        ],
        out_specs=pl.BlockSpec(memory_space=pltpu.VMEM),
        out_shape=jax.ShapeDtypeStruct(array.shape, array.dtype),
        compiler_params=pltpu.CompilerParams(vmem_limit_bytes=24 << 20),
        cost_estimate=cost(0, 4 * array.size),
    )((place.index & ring).reshape(1), array)


class Gather:
    def __init__(self, place, block, *halves):
        self.place, self.halves = place, halves
        first, second = place.ring[:2]
        self.both = first | second
        self.first, self.second = first, second
        self.parts = {0: [block], first: [None, None], second: [None], self.both: [None, None]}

    def along_first(self, half, *others):
        got = self.place.move(after(self.halves[half], *others), self.first)
        self.parts[self.first][half] = got
        return got

    def along_second(self, *others):
        got = self.place.move(after(self.parts[0][0], *others), self.second)
        self.parts[self.second][0] = got
        return got

    def onward(self, half, *others):
        got = self.place.move(after(self.parts[self.first][half], *others), self.second)
        self.parts[self.both][half] = got
        return got

    def whole(self):
        for bit in self.place.ring[2:]:
            for mask in list(self.parts):
                self.parts[mask | bit] = [self.place.move(p, bit) for p in self.parts[mask]]
        return [part for m in self.place.masks for part in self.parts[m]]


class Reduce:
    def __init__(self, place, *pairs):
        self.place, self.parts = place, gradient_blocks(place, *pairs)
        for bit in reversed(place.ring[2:]):
            for mask in [m for m in self.parts if m & bit]:
                got = place.move(self.parts.pop(mask), bit)
                total = self.parts[mask ^ bit].astype(WIDE) + got.astype(WIDE)
                self.parts[mask ^ bit] = total.astype(LOW)

    def halves(self, array):
        half = array.shape[0] // 2
        return [array[:half].astype(WIDE), array[half:].astype(WIDE)]

    def send_both(self, *others, before=()):
        first, second = self.place.ring[:2]
        got = self.place.move(after(self.parts[first | second], *others), second)
        got, own = self.halves(after(got, *before)), self.halves(self.parts[first])
        self.sent = [(a + b).astype(LOW) for a, b in zip(got, own)]
        return tuple(self.sent)

    def send_second(self, *others, before=()):
        second = self.place.ring[1]
        got = after(self.place.move(after(self.parts[second], *others), second), *before)
        self.sums = [a + b for a, b in zip(self.halves(got), self.halves(self.parts[0]))]
        return (got,)

    def send_half(self, half, *others, before=()):
        got = self.place.move(after(self.sent[half], *others), self.place.ring[0])
        self.sums[half] = (self.sums[half] + after(got, *before).astype(WIDE)).astype(LOW)
        return (self.sums[half],)


def choose_kernel(quarter_ref, early_ref, late_ref, *outs):
    rows = outs[0].shape[0]
    for quarter in range(4):
        source = early_ref if quarter < 2 else late_ref
        for flip, out in zip(FLIPS, outs):

            @pl.when(quarter_ref[0] ^ quarter == flip)
            def _():
                out[...] = source[(quarter % 2) * rows : (quarter % 2 + 1) * rows, :]


def choose(place, halves):
    rows, width = halves[0].shape[0] // 2, halves[0].shape[1]
    return pl.pallas_call(
        choose_kernel,
        in_specs=[pl.BlockSpec(memory_space=pltpu.SMEM)]
        + [pl.BlockSpec(memory_space=pltpu.VMEM)] * 2,
        out_specs=[pl.BlockSpec(memory_space=pltpu.VMEM)] * 4,
        out_shape=[jax.ShapeDtypeStruct((rows, width), LOW)] * 4,
        cost_estimate=cost(0, 16 * rows * width),
    )(place.quarter.reshape(1), *halves)


def cores_kernel(near_ref, got_ref, first_ref, second_ref, side_ref, y_ref):
    step = pl.program_id(0)
    cut = first_ref.shape[1]

    def write(out, part):
        total = near_ref[part, :].astype(WIDE) + got_ref[part, :].astype(WIDE)
        out[0] = total.astype(LOW)

    early, late = pl.ds(0, cut), pl.ds(cut, near_ref.shape[0] - cut)
    pl.when(step < 2)(lambda: write(first_ref, early))
    pl.when(step >= 2)(lambda: write(side_ref, early))
    pl.when(step % 2 == 0)(lambda: write(second_ref, late))
    pl.when(step % 2 == 1)(lambda: write(y_ref, late))


def add_cores(near, got, cut):
    rows, features = near.shape[0] // 4, near.shape[1]
    block = pl.BlockSpec((rows, features), lambda i: (i, 0))
    early = (1, cut, features)
    late = (1, rows - cut, features)
    return pl.pallas_call(
        cores_kernel,
        grid=(4,),
        in_specs=[block, block],
        out_specs=[
            pl.BlockSpec(early, lambda i: (jnp.minimum(i, 1), 0, 0)),
            pl.BlockSpec(late, lambda i: (i // 2, 0, 0)),
            pl.BlockSpec(early, lambda i: (jnp.maximum(i - 2, 0), 0, 0)),
            pl.BlockSpec(late, lambda i: (i // 2, 0, 0)),
        ],
        out_shape=as_hbm([
            jax.ShapeDtypeStruct((2,) + shape[1:], LOW) for shape in (early, late, early, late)
        ]),
        compiler_params=pltpu.CompilerParams(vmem_limit_bytes=32 << 20),
        cost_estimate=cost(0, 24 * rows * features),
    )(*in_hbm(near, got))


class GroupSum:
    def __init__(self, place, far, near):
        self.place, self.far, self.near = place, far, near

    def by_core(self, *others):
        got = self.place.move(after(self.far, *others), self.place.core)
        self.first, self.second, *self.sent = add_cores(self.near, got, self.near.shape[0] // 16)
        return self.sent

    def hop(self, *others):
        place, (first, second) = self.place, self.sent
        got_side = place.move(after(first, *others), place.side)
        got_y = place.move(after(second, *others), 0, 1)
        self.first = self.first.astype(WIDE) + got_side.astype(WIDE)
        self.second = self.second.astype(WIDE) + got_y.astype(WIDE)
        self.sent = [self.first[1].astype(LOW), self.second[1].astype(LOW)]
        return self.sent

    def last_hop(self, *others):
        place, (first, second) = self.place, self.sent
        self.got = [
            place.move(after(first, *others), 0, 1),
            place.move(after(second, *others), place.side),
        ]
        return jnp.concatenate(
            [a[0] + b.astype(WIDE) for a, b in zip((self.first, self.second), self.got)]
        )


class SmallGather:
    def __init__(self, place, vector):
        self.place, self.rows, self.bits = place, vector[None], []

    def step(self, mask, y=0, *others):
        got = self.place.move(after(self.rows, *others), mask, y)
        self.rows = jnp.concatenate([self.rows, got])
        self.bits.append(2 * mask + y)
        return self.rows

    def whole(self):
        place = self.place
        for b in range(place.count):
            if 2 << b not in self.bits:
                self.step(1 << b)
        length = self.rows.shape[1]
        split = self.rows.reshape((2,) * len(self.bits) + (length,))
        axes = []
        for b in [2 << b for b in range(place.count - 1, -1, -1)] + [1]:
            axis = len(self.bits) - 1 - self.bits.index(b)
            own = place.y if b == 1 else place.bit(b // 2)
            split = jnp.where(own == 0, split, jnp.flip(split, axis))
            axes.append(axis)
        return split.transpose(axes + [len(axes)]).reshape(-1, length)


class SmallReduce:
    def __init__(self, place, own, shared):
        self.place, self.width = place, own.size
        slot = place.y * 4 + place.quarter
        padded = jnp.zeros((4 * place.tensors, own.size), WIDE)
        padded = lax.dynamic_update_slice_in_dim(padded, own[None], slot, 0)
        self.vector = jnp.concatenate([padded.reshape(-1), shared])

    def step(self, *moves):
        self.vector = self.vector + sum(self.place.move(self.vector, *move) for move in moves)

    def results(self):
        count = 4 * self.place.tensors * self.width
        own = self.vector[:count].reshape(self.place.tensors, 4, self.width)
        return pick(own, self.place.y), self.vector[count:]


FLIPS = (0, 1, 2, 3)


def pack_kernel(quarter_ref, *refs):
    shards, outs = refs[: len(refs) - 4], refs[len(refs) - 4 :]
    for flip, out in zip(FLIPS, outs):
        quarter = quarter_ref[0] ^ flip
        column = 0
        for shard in shards:
            width = shard.shape[2] // 4
            for kind in range(shard.shape[0]):
                at = pl.multiple_of(quarter * width, 128)
                out[:, column : column + width] = shard[kind, :, pl.ds(at, width)].astype(LOW)
                column += width


def pack(place, *shards):
    rows = shards[0].shape[1]
    width = sum(s.shape[0] * s.shape[2] for s in shards) // 4
    return pl.pallas_call(
        pack_kernel,
        in_specs=[pl.BlockSpec(memory_space=pltpu.SMEM)]
        + [pl.BlockSpec(memory_space=pltpu.VMEM)] * len(shards),
        out_specs=[pl.BlockSpec(memory_space=pltpu.VMEM)] * 4,
        out_shape=[jax.ShapeDtypeStruct((rows, width), LOW)] * 4,
        compiler_params=pltpu.CompilerParams(vmem_limit_bytes=24 << 20),
        cost_estimate=cost(0, 24 * rows * width),
    )(place.quarter.reshape(1), *shards)


def stack_kernel(count, quarter_ref, *refs):
    pieces, outs = refs[:count], refs[count:]
    third = len(outs) // 3
    outs, halves = outs[:third], (outs[third : 2 * third], outs[2 * third :])
    rows = sum(piece.shape[0] for piece in pieces) // 4
    flip = 0
    for piece in pieces:
        for part in range(piece.shape[0] // rows):
            at = pl.multiple_of((quarter_ref[0] ^ flip) * rows, 16)
            column = 0
            for out in outs:
                width = out.shape[1]
                out[pl.ds(at, rows), :] = piece[
                    part * rows : (part + 1) * rows, column : column + width
                ]
                column += width
            flip += 1
    for out, early, late in zip(outs, *halves):
        early[...] = out[: 2 * rows]
        late[...] = out[2 * rows :]


def stack(place, pieces, widths):
    rows = sum(piece.shape[0] for piece in pieces)
    outs = pl.pallas_call(
        functools.partial(stack_kernel, len(pieces)),
        in_specs=[pl.BlockSpec(memory_space=pltpu.SMEM)]
        + [pl.BlockSpec(memory_space=pltpu.VMEM)] * len(pieces),
        out_specs=[pl.BlockSpec(memory_space=pltpu.VMEM)] * (3 * len(widths)),
        out_shape=[
            jax.ShapeDtypeStruct((r, w), LOW) for r in (rows, rows // 2, rows // 2) for w in widths
        ],
        compiler_params=pltpu.CompilerParams(vmem_limit_bytes=24 << 20),
        cost_estimate=cost(0, 4 * rows * sum(widths)),
    )(place.quarter.reshape(1), *pieces)
    return list(zip(outs[: len(widths)], outs[len(widths) : 2 * len(widths)], outs[-len(widths) :]))


def adam_kernel(step_rate, column, quarter_ref, near_ref, core_ref, side_ref, both_ref, *refs):
    weight, moment, square, new_weight, new_moment, new_square = refs
    distance = pl.program_id(0) ^ quarter_ref[0]
    for flip, piece in zip(FLIPS, (near_ref, core_ref, side_ref, both_ref)):

        @pl.when(distance == flip)
        def _():
            width = weight.shape[2]
            for kind in range(weight.shape[0]):
                start = column + kind * width
                results = adam_update(
                    weight[kind],
                    piece[:, start : start + width].astype(WIDE),
                    moment[kind],
                    square[kind],
                    step_rate,
                    WEIGHT_DECAY,
                )
                new_weight[kind], new_moment[kind], new_square[kind] = results


def adam_shard(place, pieces, column, weight, moment, square, step_rate):
    kinds, rows, width = weight.shape
    block = pl.BlockSpec((kinds, rows, width // 4), lambda q: (0, 0, q))
    return pl.pallas_call(
        functools.partial(adam_kernel, step_rate, column),
        grid=(4,),
        in_specs=[pl.BlockSpec(memory_space=pltpu.SMEM)]
        + [pl.BlockSpec(pieces[0].shape, lambda q: (0, 0))] * 4
        + [block] * 3,
        out_specs=[block] * 3,
        out_shape=[jax.ShapeDtypeStruct(weight.shape, WIDE)] * 3,
        compiler_params=pltpu.CompilerParams(vmem_limit_bytes=32 << 20),
        cost_estimate=pl.CostEstimate(
            flops=20 * weight.size, bytes_accessed=26 * weight.size, transcendentals=0
        ),
    )(*in_hbm(place.quarter.reshape(1), *pieces, weight, moment, square))


def join_kernel(starts, *refs):
    arrays, out = refs[:-1], refs[-1]
    step = pl.program_id(0)
    for array, start, end in zip(arrays, starts, starts[1:]):

        @pl.when((step >= start) & (step < end))
        def _():
            out[...] = array[...]


def join(*arrays):
    tile = arrays[0].shape[0] // 2
    starts = [0]
    for array in arrays:
        starts.append(starts[-1] + array.shape[0] // tile)
    width = arrays[0].shape[1]

    def spec(start, end):
        return pl.BlockSpec((tile, width), lambda i: (jnp.clip(i - start, 0, end - start - 1), 0))

    return pl.pallas_call(
        functools.partial(join_kernel, starts),
        grid=(starts[-1],),
        in_specs=[spec(*ends) for ends in zip(starts, starts[1:])],
        out_specs=pl.BlockSpec((tile, width), lambda i: (i, 0)),
        out_shape=as_hbm(jax.ShapeDtypeStruct((starts[-1] * tile, width), arrays[0].dtype)),
        compiler_params=pltpu.CompilerParams(vmem_limit_bytes=32 << 20),
        cost_estimate=cost(0, 4 * starts[-1] * tile * width),
    )(*in_hbm(*arrays))


def norm_kernel(count, *refs):
    pieces, far_ref, vectors_ref, normed_ref = refs[:count], *refs[count:]

    def write(ref):
        rows = ref[...].astype(WIDE)
        centered = rows - jnp.mean(rows, axis=-1, keepdims=True)
        inverse = lax.rsqrt(jnp.mean(centered * centered, axis=-1, keepdims=True) + EPS_NORM)
        normed_ref[...] = (centered * inverse * vectors_ref[0:1] + vectors_ref[1:2]).astype(LOW)

    step = pl.program_id(0)
    for i, piece in enumerate(pieces):
        pl.when(step == i)(functools.partial(write, piece))
    pl.when(step >= count)(functools.partial(write, far_ref))


def norm(pieces, far, vectors):
    rows, features = pieces[0].shape
    count = len(pieces)
    return pl.pallas_call(
        functools.partial(norm_kernel, count),
        grid=(2 * count,),
        in_specs=[pl.BlockSpec((rows, features), lambda i: (0, 0))] * count
        + [
            pl.BlockSpec((rows, features), lambda i: (jnp.maximum(i - count, 0), 0)),
            pl.BlockSpec(vectors.shape, lambda i: (0, 0)),
        ],
        out_specs=pl.BlockSpec((rows, features), lambda i: (i, 0)),
        out_shape=as_hbm(jax.ShapeDtypeStruct((2 * count * rows, features), LOW)),
        compiler_params=pltpu.CompilerParams(vmem_limit_bytes=32 << 20),
        cost_estimate=cost(0, 8 * count * rows * features),
    )(*in_hbm(*pieces, far, vectors))


VMEM_LIMIT = 40 << 20


def dot(left, right, left_axis, right_axis):
    return lax.dot_general(
        left, right, (((left_axis,), (right_axis,)), ((), ())), preferred_element_type=WIDE
    )


def lay(block_lists, cuts, weights_ref, arrived):
    @pl.when(pl.program_id(0) == 0)
    def _():
        copies, column = [], 0
        for blocks, (start, width) in zip(block_lists, cuts):
            at = 0
            for block in blocks:
                depth = block.shape[0]
                copy = pltpu.make_async_copy(
                    block.at[:, pl.ds(start, width)],
                    weights_ref.at[pl.ds(at, depth), pl.ds(column, width)],
                    arrived.at[len(copies)],
                )
                copy.start()
                copies.append(copy)
                at += depth
            column += width
        for copy in copies:
            copy.wait()


def laid(features, width, *block_lists):
    count = sum(len(blocks) for blocks in block_lists)
    return [pltpu.VMEM((features, width), LOW), pltpu.SemaphoreType.DMA((count,))]


ANYWHERE = pl.BlockSpec(memory_space=pl.ANY)


def whole_spec(array):
    return pl.BlockSpec(array.shape, lambda i: (0, 0))


def row_spec(rows, array):
    return pl.BlockSpec((rows, array.shape[1]), lambda i: (i, 0))


GELU_A, GELU_B = (2 / math.pi) ** 0.5, 0.044715


def hidden_kernel(rows_ref, shift_ref, *refs):
    blocks, (slope_ref, hidden_ref, weights_ref, arrived) = refs[:-4], refs[-4:]
    lay([blocks], [(0, slope_ref.shape[1])], weights_ref, arrived)
    pre = dot(rows_ref[...], weights_ref[...], 1, 0) + shift_ref[...]
    square = pre * pre
    bend = jnp.tanh(GELU_A * (pre + GELU_B * (square * pre)))
    raised = 0.5 * (1.0 + bend)
    hidden_ref[...] = (pre * raised).astype(LOW)
    slope = raised + 0.5 * pre * (1.0 - bend * bend) * (GELU_A * (1.0 + 3.0 * GELU_B * square))
    slope_ref[...] = slope.astype(LOW)


def hidden_units(rows, shift, blocks):
    count, features = rows.shape
    width = blocks[0].shape[1]
    tile = count // 4
    return pl.pallas_call(
        hidden_kernel,
        grid=(4,),
        in_specs=[row_spec(tile, rows), whole_spec(shift)] + [ANYWHERE] * len(blocks),
        out_specs=[pl.BlockSpec((tile, width), lambda i: (i, 0))] * 2,
        out_shape=as_hbm([jax.ShapeDtypeStruct((count, width), LOW)] * 2),
        scratch_shapes=laid(features, width, blocks),
        compiler_params=pltpu.CompilerParams(vmem_limit_bytes=VMEM_LIMIT),
        cost_estimate=cost(2 * rows.size * width, 2 * rows.size + 6 * count * width),
    )(*in_hbm(rows, shift, *blocks))


def d_pre_kernel(rows_ref, slope_ref, *refs):
    blocks, (d_pre_ref, sums_ref, weights_ref, arrived) = refs[:-4], refs[-4:]

    @pl.when(pl.program_id(0) == 0)
    def _():
        sums_ref[...] = jnp.zeros_like(sums_ref)

    lay([blocks], [(0, slope_ref.shape[1])], weights_ref, arrived)
    d_hidden = dot(rows_ref[...], weights_ref[...], 1, 0)
    low = (d_hidden * slope_ref[...].astype(WIDE)).astype(LOW)
    d_pre_ref[...] = low
    sums_ref[...] += jnp.sum(low.astype(WIDE), axis=0, keepdims=True)


def d_pre_units(rows, slope, blocks):
    count, width = slope.shape
    tile = count // 4
    return pl.pallas_call(
        d_pre_kernel,
        grid=(4,),
        in_specs=[row_spec(tile, rows), row_spec(tile, slope)] + [ANYWHERE] * len(blocks),
        out_specs=[
            pl.BlockSpec((tile, width), lambda i: (i, 0)),
            pl.BlockSpec((1, width), lambda i: (0, 0)),
        ],
        out_shape=as_hbm([
            jax.ShapeDtypeStruct((count, width), LOW),
            jax.ShapeDtypeStruct((1, width), WIDE),
        ]),
        scratch_shapes=laid(rows.shape[1], width, blocks),
        compiler_params=pltpu.CompilerParams(vmem_limit_bytes=VMEM_LIMIT),
        cost_estimate=cost(2 * rows.size * width, 2 * rows.size + 6 * count * width),
    )(*in_hbm(rows, slope, *blocks))


def gradient_kernel(pairs, *refs):
    operands, outs = refs[: 2 * pairs], refs[2 * pairs :]

    def write(out):
        column = 0
        for i in range(pairs):
            part = dot(operands[2 * i][...], operands[2 * i + 1][...], 0, 0).astype(LOW)
            out[:, column : column + part.shape[1]] = part
            column += part.shape[1]

    for step, out in enumerate(outs):
        pl.when(pl.program_id(0) == step)(functools.partial(write, out))


def gradient_blocks(place, *pairs):
    count, features = pairs[0][0].shape
    steps = len(place.masks)
    rows = features // steps
    width = sum(right.shape[1] for _, right in pairs)
    specs = []
    for _, right in pairs:
        specs += [pl.BlockSpec((count, rows), lambda i: (0, i)), whole_spec(right)]
    outs = pl.pallas_call(
        functools.partial(gradient_kernel, len(pairs)),
        grid=(steps,),
        in_specs=specs,
        out_specs=[pl.BlockSpec((rows, width), lambda i: (0, 0))] * steps,
        out_shape=as_hbm([jax.ShapeDtypeStruct((rows, width), LOW)] * steps),
        compiler_params=pltpu.CompilerParams(vmem_limit_bytes=VMEM_LIMIT),
        cost_estimate=cost(2 * count * features * width, 2 * count * (features + width)),
    )(*in_hbm(*[array for pair in pairs for array in pair]))
    return dict(zip(place.masks, outs))


def spread_kernel(cuts, counts, summed, *refs):
    if summed:
        (normed_ref, vectors_ref), refs = refs[:2], refs[2:]
        sums_ref, refs = refs[-3], refs[:-3] + refs[-2:]
    lefts, rest = refs[: len(cuts)], refs[len(cuts) :]
    block_lists = []
    for count in counts:
        block_lists.append(rest[:count])
        rest = rest[count:]
    far_ref, near_ref, weights_ref, arrived = rest
    lay(block_lists, cuts, weights_ref, arrived)
    left = jnp.concatenate([ref[...] for ref in lefts], axis=1)

    def write(out):
        total = dot(left, weights_ref[...], 1, 1)
        out[...] = total.astype(LOW)
        if summed:
            unit = normed_ref[...].astype(WIDE) - vectors_ref[1:2]
            sums_ref[0:1] += jnp.sum(total * unit, axis=0, keepdims=True)
            sums_ref[1:2] += jnp.sum(total, axis=0, keepdims=True)

    if summed:

        @pl.when(pl.program_id(0) == 0)
        def _():
            sums_ref[...] = jnp.zeros_like(sums_ref)

    pl.when(pl.program_id(0) < 2)(lambda: write(far_ref))
    pl.when(pl.program_id(0) >= 2)(lambda: write(near_ref))


def spread(lefts, block_lists, cuts, *unit):
    count = lefts[0].shape[0]
    tile = count // 4
    features = sum(b.shape[0] for b in block_lists[0])
    depth = sum(width for _, width in cuts)
    return pl.pallas_call(
        functools.partial(spread_kernel, cuts, [len(b) for b in block_lists], bool(unit)),
        grid=(4,),
        in_specs=[
            pl.BlockSpec((tile, rows.shape[1]), lambda i: ((i + 2) % 4, 0)) for rows in unit[:1]
        ]
        + [whole_spec(vectors) for vectors in unit[1:]]
        + [pl.BlockSpec((tile, left.shape[1]), lambda i: ((i + 2) % 4, 0)) for left in lefts]
        + [ANYWHERE] * sum(len(blocks) for blocks in block_lists),
        out_specs=[
            pl.BlockSpec((tile, features), lambda i: (jnp.minimum(i, 1), 0)),
            pl.BlockSpec((tile, features), lambda i: (jnp.maximum(i - 2, 0), 0)),
        ]
        + [pl.BlockSpec((2, features), lambda i: (0, 0)) for _ in unit[:1]],
        out_shape=as_hbm([jax.ShapeDtypeStruct((count // 2, features), LOW)] * 2
        + [jax.ShapeDtypeStruct((2, features), WIDE) for _ in unit[:1]]),
        scratch_shapes=laid(features, depth, *block_lists),
        compiler_params=pltpu.CompilerParams(vmem_limit_bytes=VMEM_LIMIT),
        cost_estimate=cost(2 * count * features * depth, 2 * count * (features + depth)),
    )(*in_hbm(*unit, *lefts, *[b for blocks in block_lists for b in blocks]))


PAIR = 2 * HD
SCALE = HD ** (-0.5)
TILES = 2


def turn(pair, cosine, sine):
    half = ROTARY // 2
    lane = lax.broadcasted_iota(jnp.int32, pair.shape, 1) % HD
    partner = jnp.where(lane < half, pltpu.roll(pair, PAIR - half, 1), pltpu.roll(pair, half, 1))
    return pair * cosine + partner * sine


def two_heads(pair):
    lane = lax.broadcasted_iota(jnp.int32, pair.shape, 1) // HD
    zero = jnp.zeros_like(pair)
    return jnp.concatenate([jnp.where(lane == head, pair, zero) for head in range(2)])


def either(stacked):
    rows = stacked.shape[0] // 2
    lane = lax.broadcasted_iota(jnp.int32, (rows, PAIR), 1) // HD
    return jnp.where(lane == 0, stacked[:rows], stacked[rows:])


def seen(ids_col, ids_row, first, rows, width):
    key = lax.broadcasted_iota(jnp.int32, (width, rows), 0)
    query = lax.broadcasted_iota(jnp.int32, (width, rows), 1) + first
    mask = (ids_col[:width] == ids_row[:, first : first + rows]) & (key <= query)
    return jnp.concatenate([mask, mask], axis=1)


def halves(y_ref, rows, cos_ref, sin_ref):
    places = [pl.ds(pl.multiple_of((y_ref[0] ^ t) * rows, 128), rows) for t in range(TILES)]
    cuts = [slice(t * rows, (t + 1) * rows) for t in range(TILES)]
    return places, [(cos_ref[cut], sin_ref[cut]) for cut in cuts]


def forward_kernel(y_ref, rows_ref, shift_ref, cos_ref, sin_ref, col_ref, row_ref, *refs):
    blocks, outs, (joint_ref, weights_ref, arrived) = refs[:-6], refs[-6:-3], refs[-3:]
    turned_ref, context_ref, log_ref = outs
    slots, width = context_ref.shape
    lay([blocks], [(0, 3 * width)], weights_ref, arrived)
    joint_ref[...] = dot(rows_ref[...], weights_ref[...], 1, 0)
    ids_col, ids_row = col_ref[...], row_ref[0]
    rows = slots // TILES
    masks = [seen(ids_col, ids_row, t * rows, rows, (t + 1) * rows) for t in range(TILES)]
    places, tables = halves(y_ref, rows, cos_ref, sin_ref)
    log_ref[...] = jnp.zeros_like(log_ref)
    for p in range(width // PAIR):
        columns = [slice(j * width + p * PAIR, j * width + (p + 1) * PAIR) for j in range(3)]
        query, key, value = [], [], []
        for place, table in zip(places, tables):
            parts = [joint_ref[place, c] + shift_ref[:, c] for c in columns]
            query.append(turn(parts[0], *table).astype(LOW))
            key.append(turn(parts[1], *table).astype(LOW))
            value.append(parts[2].astype(LOW))
            for c, array in zip(columns, (query, key, value)):
                turned_ref[place, c] = array[-1]
        key, value = jnp.concatenate(key), jnp.concatenate(value)
        for t in range(TILES):
            keys = (t + 1) * rows
            scores = dot(key[:keys], two_heads(query[t] * SCALE), 1, 1)
            scores = jnp.where(masks[t], scores, -1e30)
            top = jnp.max(scores, axis=0, keepdims=True)
            raised = jnp.exp(scores - top)
            total = jnp.sum(raised, axis=0, keepdims=True)
            probs = (raised * (1.0 / total)).astype(LOW)
            out = dot(probs, value[:keys], 0, 0)
            log_total = top + jnp.log(total)
            for head in range(2):
                log_ref[2 * p + head : 2 * p + head + 1, t * rows : (t + 1) * rows] = log_total[
                    :, head * rows : (head + 1) * rows
                ]
            context_ref[places[t], p * PAIR : (p + 1) * PAIR] = either(out).astype(LOW)


def backward_kernel(y_ref, turned_ref, rows_ref, log_ref, cos_ref, sin_ref, col_ref, row_ref, *refs):
    blocks, outs, (back_ref, weights_ref, arrived) = refs[:-5], refs[-5:-3], refs[-3:]
    joint_ref, sums_ref = outs
    slots, width = back_ref.shape
    lay([blocks], [(3 * width, width)], weights_ref, arrived)
    back_ref[...] = dot(rows_ref[...], weights_ref[...], 1, 0).astype(LOW)
    ids_col, ids_row = col_ref[...], row_ref[0]
    rows = slots // TILES
    masks = [seen(ids_col, ids_row, t * rows, rows, (t + 1) * rows) for t in range(TILES)]
    places, tables = halves(y_ref, rows, cos_ref, sin_ref)

    @pl.when(pl.program_id(0) == 0)
    def _():
        sums_ref[...] = jnp.zeros_like(sums_ref)

    for p in range(width // PAIR):
        columns = [slice(j * width + p * PAIR, j * width + (p + 1) * PAIR) for j in range(3)]
        key, value = (
            jnp.concatenate([turned_ref[place, c] for place in places]) for c in columns[1:]
        )
        d_query, d_key, d_value = [], [], []
        for t, place in enumerate(places):
            here, keys = slice(t * rows, (t + 1) * rows), (t + 1) * rows
            query = two_heads(turned_ref[place, columns[0]] * SCALE)
            d_context = two_heads(back_ref[place, p * PAIR : (p + 1) * PAIR])
            logs = jnp.concatenate(
                [log_ref[2 * p + head : 2 * p + head + 1, here] for head in range(2)], axis=1
            )
            scores = dot(key[:keys], query, 1, 1)
            probs = jnp.where(masks[t], jnp.exp(scores - logs), 0.0)
            d_probs = dot(value[:keys], d_context, 1, 1)
            delta = jnp.sum(probs * d_probs, axis=0, keepdims=True)
            d_scores = (probs * (d_probs - delta)).astype(LOW)
            d_query.append(either(dot(d_scores, key[:keys], 0, 0)) * SCALE)
            d_key.append(dot(d_scores, query, 1, 0))
            d_value.append(dot(probs.astype(LOW), d_context, 1, 0))
        for t, (place, (cosine, sine)) in enumerate(zip(places, tables)):
            here = slice(t * rows, (t + 1) * rows)
            parts = (
                turn(d_query[t], cosine, -sine),
                turn(sum(d[here] for d in d_key[t:]), cosine, -sine),
                sum(d[here] for d in d_value[t:]),
            )
            for c, array in zip(columns, parts):
                low = array.astype(LOW)
                joint_ref[place, c] = low
                sums_ref[:, c] += jnp.sum(low.astype(WIDE), axis=0, keepdims=True)


def by_group(slots, width):
    return pl.BlockSpec((slots, width), lambda g: (g, 0))


def attention_forward(place, normed, head_shift, cosine, sine, ids, blocks):
    groups, slots = ids.shape
    rows, width = normed.shape[0], blocks[0].shape[1] // 4
    return pl.pallas_call(
        forward_kernel,
        grid=(groups,),
        in_specs=[
            pl.BlockSpec(memory_space=pltpu.SMEM),
            row_spec(slots, normed),
            pl.BlockSpec((1, 3 * width), lambda g: (0, 0)),
            by_group(slots, PAIR),
            by_group(slots, PAIR),
            by_group(slots, 1),
            pl.BlockSpec((1, 1, slots), lambda g: (g, 0, 0)),
        ]
        + [ANYWHERE] * len(blocks),
        out_specs=[by_group(slots, 3 * width), by_group(slots, width), by_group(8, slots)],
        out_shape=as_hbm([
            jax.ShapeDtypeStruct((rows, 3 * width), LOW),
            jax.ShapeDtypeStruct((rows, width), LOW),
            jax.ShapeDtypeStruct((8 * groups, slots), WIDE),
        ]),
        scratch_shapes=[pltpu.VMEM((slots, 3 * width), WIDE)]
        + laid(normed.shape[1], 3 * width, blocks),
        compiler_params=pltpu.CompilerParams(vmem_limit_bytes=VMEM_LIMIT),
        cost_estimate=cost(20 * rows * slots * width + 6 * normed.size * width, 2 * normed.size),
    )(*in_hbm(place.y.reshape(1), normed, head_shift[None], cosine, sine, ids.reshape(-1, 1), ids[:, None], *blocks))


def attention_backward(place, turned, grad, logs, cosine, sine, ids, blocks):
    groups, slots = ids.shape
    rows, width = grad.shape[0], blocks[0].shape[1] // 4
    return pl.pallas_call(
        backward_kernel,
        grid=(groups,),
        in_specs=[
            pl.BlockSpec(memory_space=pltpu.SMEM),
            by_group(slots, 3 * width),
            row_spec(slots, grad),
            by_group(8, slots),
            by_group(slots, PAIR),
            by_group(slots, PAIR),
            by_group(slots, 1),
            pl.BlockSpec((1, 1, slots), lambda g: (g, 0, 0)),
        ]
        + [ANYWHERE] * len(blocks),
        out_specs=[by_group(slots, 3 * width), pl.BlockSpec((1, 3 * width), lambda g: (0, 0))],
        out_shape=as_hbm([
            jax.ShapeDtypeStruct((rows, 3 * width), LOW),
            jax.ShapeDtypeStruct((1, 3 * width), WIDE),
        ]),
        scratch_shapes=[pltpu.VMEM((slots, width), LOW)] + laid(grad.shape[1], width, blocks),
        compiler_params=pltpu.CompilerParams(vmem_limit_bytes=VMEM_LIMIT),
        cost_estimate=cost(50 * rows * slots * width + 2 * grad.size * width, 2 * grad.size),
    )(*in_hbm(place.y.reshape(1), turned, grad, logs, cosine, sine, ids.reshape(-1, 1), ids[:, None], *blocks))


def body(
    dp_size,
    tensor_size,
    tokens,
    cotangent,
    segment_ids,
    joint_weight,
    dense_weight,
    expand_weight,
    shrink_weight,
    head_bias,
    unit_bias,
    row_vectors,
    joint_mean,
    joint_square,
    dense_mean,
    dense_square,
    expand_mean,
    expand_square,
    shrink_mean,
    shrink_square,
    head_mean,
    head_square,
    unit_mean,
    unit_square,
    rows_mean,
    rows_square,
):
    place = Place(dp_size, tensor_size)
    devices = dp_size * tensor_size
    my_rows = tokens.shape[0]
    features = tokens.shape[1]
    group_slots = segment_ids.shape[0]
    shard_rows = joint_weight.shape[0]
    block_rows = 4 * shard_rows
    heads = head_bias.shape[2] // 4
    units = unit_bias.shape[1] // 4
    joint_width, unit_width = heads * HD, units * HD

    def kinds_first(array):
        return array.transpose(1, 0, 2)

    side, core = place.side, place.core
    first, second = place.ring[:2]
    small = SmallGather(
        place,
        jnp.concatenate(
            [
                row_vectors.reshape(-1),
                head_bias.reshape(-1),
                unit_bias.reshape(-1),
                segment_ids.astype(WIDE),
            ]
        ),
    )

    joint_shard = kinds_first(joint_weight)
    quarters = pack(place, joint_shard, dense_weight[None])
    by_core = place.move(quarters[1], core)
    by_side = place.move(quarters[2], side)
    by_both = place.move(quarters[3], side | core)
    small.step(0, 1, by_core)
    small.step(core)
    small.step(second)
    mine = arrange(place, tokens)
    near_quarters = pack(place, expand_weight[None], shrink_weight[None])
    my_ids = lax.dynamic_slice_in_dim(segment_ids, place.y * my_rows, my_rows)
    masked = arrange(place, cotangent * (my_ids > 0).astype(LOW)[:, None])
    blocks = stack(place, (quarters[0], by_core, by_side, by_both), (4 * joint_width,))[0]
    block, joint = blocks[0], Gather(place, *blocks)

    ready = (block, small.rows, mine)
    got = [
        joint.along_first(0),
        joint.along_second(),
        place.move(after(mine, *ready), side),
        place.move(after(mine, *ready), 0, 1),
        place.move(
            after(jnp.concatenate([near_quarters[1], near_quarters[3]]), *ready), core
        ),
    ]
    mine_side, mine_y, by_core = got[2:5]

    ready = tuple(got)
    got = [
        joint.along_first(1, *ready),
        joint.onward(0, *ready),
        place.move(after(mine_side, *ready), 0, 1),
        place.move(
            after(jnp.concatenate([near_quarters[2], by_core[shard_rows:]]), *ready), side
        ),
        small.step(first, 0, *ready),
    ]
    corner, by_side = got[2:4]
    near = join(mine, mine_y, mine_side, corner)
    blocks = stack(
        place, (near_quarters[0], by_core[:shard_rows], by_side), (unit_width, unit_width)
    )
    expand, shrink = (Gather(place, *array) for array in blocks)

    ready = tuple(got) + (blocks[0][0],)
    got = [
        expand.along_first(0, *ready),
        joint.onward(1, *ready),
        place.move(after(masked, *ready), side),
        place.move(after(masked, *ready), 0, 1),
        small.step(side, 0, *ready),
    ]
    masked_side, masked_y = got[2:4]

    cuts = [row_vectors.size, row_vectors.size + head_bias.size]
    cuts.append(cuts[1] + unit_bias.size)
    rows_small, head_small, unit_small, ids_small = jnp.split(small.whole(), cuts, axis=1)
    row_whole = rows_small.reshape(devices, 4, -1).transpose(1, 0, 2).reshape(4, features)
    head_small = pick(head_small.reshape((dp_size, tensor_size) + head_bias.shape), place.y, 1)
    head_low = lax.dynamic_slice_in_dim(head_small, place.quarter * heads, heads, 3)
    head_shift = head_low.reshape(HD, 3, heads).astype(LOW).astype(WIDE)
    head_shift = head_shift.transpose(1, 2, 0).reshape(-1)
    unit_small = pick(unit_small.reshape((dp_size, tensor_size) + unit_bias.shape), place.y, 1)
    unit_low = lax.dynamic_slice_in_dim(unit_small, place.quarter * units, units, 2)
    unit_shift = unit_low.reshape(HD, units).astype(LOW).astype(WIDE).T.reshape(-1)
    ids_small = ids_small.reshape(dp_size, tensor_size, group_slots)[:, 0]
    distances = (0, place.side, place.core, place.side | place.core)
    ids = jnp.stack([pick(ids_small, place.index ^ d) for d in distances])

    own_vectors = arrange(place, row_whole)
    positions = jax.vmap(doc_positions)(ids)[0].reshape(-1, 1)
    lane = jnp.arange(PAIR) % HD
    half_rot = ROTARY // 2
    frequency = 10000.0 ** (-(lane % half_rot).astype(WIDE) / half_rot)
    angles = positions * frequency
    cosine = jnp.where(lane < ROTARY, jnp.cos(angles), 1.0)
    sine = jnp.sin(angles)
    sine = jnp.where(lane < half_rot, -sine, jnp.where(lane < ROTARY, sine, 0.0))

    ready = tuple(got) + (cosine, sine, own_vectors, head_shift, unit_shift)
    got = [
        expand.along_first(1, *ready),
        expand.along_second(*ready),
        place.move(after(masked_side, *ready), 0, 1),
        place.move(after(near, *ready), core),
    ]
    normed = norm((mine, mine_y, mine_side, corner), got[3], own_vectors)

    ready = tuple(got) + (normed,)
    masked_corner = got[2]
    got = [
        shrink.along_first(0, *ready),
        expand.onward(0, *ready),
        expand.onward(1, *ready),
    ]
    joint = joint.whole()
    turned, context, logs = attention_forward(
        place, after(normed, *ready), head_shift, cosine, sine, ids, joint
    )

    ready = tuple(got) + (context,)
    grad_near = join(after(masked, *ready), masked_y, masked_side, masked_corner)
    got = [
        shrink.along_first(1, *ready),
        shrink.onward(0, *ready),
        shrink.along_second(*ready),
        place.move(grad_near, core),
    ]
    grad_all = join(grad_near, got[3])
    d_joint, joint_sums = attention_backward(
        place, turned, grad_all, logs, cosine, sine, ids, joint
    )
    expand = expand.whole()

    ready = tuple(got) + (d_joint,)
    got = [shrink.onward(1, *ready)]
    shrink = shrink.whole()
    sum_joint = Reduce(place, (after(normed, *ready), d_joint), (grad_all, context))

    def returned(reduce, *others):
        return list(choose(place, [after(half, *others) for half in reduce.sums]))

    ready = tuple(got) + tuple(sum_joint.parts.values())
    slope, hidden = hidden_units(after(normed, *ready), unit_shift[None], expand)
    got = sum_joint.send_both(*ready, before=(hidden,))

    ready = got + (hidden,)
    sum_shrink = Reduce(place, (after(grad_all, *ready), hidden))
    d_pre, unit_sums = d_pre_units(after(grad_all, *sum_shrink.parts.values()), slope, shrink)
    got = sum_joint.send_second(*ready, before=(d_pre,))
    got += sum_joint.send_half(0, *ready, before=(d_pre,))

    ready = got + (d_pre,)
    outer = GroupSum(
        place,
        *spread(
            [after(context, *ready), hidden],
            [joint, shrink],
            ((3 * joint_width, joint_width), (0, unit_width)),
        ),
    )
    got = sum_shrink.send_both(*ready, before=(outer.far,))
    got += sum_joint.send_half(1, *ready, before=(outer.far,))

    ready = got + (outer.far,)
    sum_expand = Reduce(place, (after(normed, *ready), d_pre))
    before = tuple(sum_expand.parts.values())
    got = sum_shrink.send_second(*ready, before=before)
    got += sum_shrink.send_half(0, *ready, before=before)
    outer_sent = outer.by_core(*ready)
    g_joint = returned(sum_joint, *ready)
    g_joint[1] = place.move(g_joint[1], core)
    g_joint[2] = place.move(g_joint[2], side)

    ready = got + before + tuple(outer_sent) + tuple(g_joint[1:3])
    inner_far, inner_near, inner_sums = spread(
        [after(d_joint, *ready), d_pre],
        [joint, expand],
        ((0, 3 * joint_width), (0, unit_width)),
        normed,
        own_vectors,
    )
    inner = GroupSum(place, inner_far, inner_near)
    got = sum_expand.send_both(*ready, before=(inner.far,))
    got += sum_shrink.send_half(1, *ready, before=(inner.far,))
    outer_sent = outer.hop(*ready)
    g_joint[3] = place.move(after(g_joint[3], *ready), side | core)

    ready = got + (inner.far, g_joint[3]) + tuple(outer_sent)
    own_sums = jnp.concatenate([joint_sums[0], unit_sums[0]])
    row_sums = jnp.concatenate(
        [
            inner_sums[0:1] / own_vectors[0:1],
            inner_sums[1:2],
            jnp.sum(masked, axis=0, dtype=WIDE, keepdims=True),
        ]
    )
    sums = SmallReduce(place, own_sums, arrange(place, row_sums, True).reshape(-1))
    sent = inner.by_core(*ready)
    got = sum_expand.send_second(*ready) + sum_expand.send_half(0, *ready)
    branch = outer.last_hop(*ready)
    g_shrink = returned(sum_shrink, *ready)

    ready = got + tuple(sent) + (branch,)
    got = sum_expand.send_half(1, *ready)
    sent = inner.hop(*ready)
    for flip, mask in ((1, core), (2, side), (3, side | core)):
        g_shrink[flip] = place.move(after(g_shrink[flip], *ready), mask)

    ready = got + tuple(sent) + tuple(g_shrink[1:])
    g_expand = returned(sum_expand, *ready)
    for flip, mask in ((1, core), (2, side), (3, side | core)):
        g_expand[flip] = place.move(g_expand[flip], mask)
    d_normed = inner.last_hop(*ready)
    g_joint[0] = after(g_joint[0], *ready)

    def shard_update(pieces, column, weight, moment, square, step_rate):
        news = adam_shard(
            place, pieces, column, weight[None], moment[None], square[None], step_rate
        )
        return [new[0] for new in news]

    joint_new = adam_shard(
        place,
        g_joint,
        0,
        joint_shard,
        kinds_first(joint_mean),
        kinds_first(joint_square),
        D ** (-0.5),
    )
    dense_new = shard_update(
        g_joint, 3 * joint_width, dense_weight, dense_mean, dense_square, (D // 32) ** (-0.5)
    )

    g_shrink[0] = after(g_shrink[0], joint_new[0], dense_new[0])
    shrink_new = shard_update(g_shrink, 0, shrink_weight, shrink_mean, shrink_square, FF ** (-0.5))

    sums.vector = after(sums.vector, shrink_new[0], *g_expand[1:])
    sums.step((core, 0), (0, 1), (core, 1))
    expand_new = shard_update(g_expand, 0, expand_weight, expand_mean, expand_square, D ** (-0.5))
    sums.vector = after(sums.vector, expand_new[0])
    sums.step((side, 0), (second, 0), (side | second, 0))
    for bit in place.ring:
        if bit != second:
            sums.step((bit, 0))
    own_sums, row_sums = sums.results()

    layer_output = mine.astype(WIDE) + branch + own_vectors[2] + own_vectors[3]
    layer_output = arrange(place, layer_output.astype(LOW), True)
    inputs = mine.astype(WIDE)
    centered = inputs - jnp.mean(inputs, axis=-1, keepdims=True)
    inverse = lax.rsqrt(jnp.mean(centered * centered, axis=-1, keepdims=True) + EPS_NORM)
    unit_rows = centered * inverse
    d_unit_rows = d_normed * own_vectors[0]
    d_inputs = inverse * (
        d_unit_rows
        - jnp.mean(d_unit_rows, axis=-1, keepdims=True)
        - unit_rows * jnp.mean(d_unit_rows * unit_rows, axis=-1, keepdims=True)
    )
    input_grad = arrange(place, masked.astype(WIDE) + d_inputs, True)

    features_here = HD // dp_size
    g_head = own_sums[:, : 3 * joint_width].reshape(4, 3, heads, HD)
    g_head = lax.dynamic_slice_in_dim(g_head, place.index * features_here, features_here, 3)
    g_head = g_head.transpose(3, 1, 0, 2).reshape(head_bias.shape)
    g_unit = own_sums[:, 3 * joint_width :].reshape(4 * units, HD)
    g_unit = lax.dynamic_slice_in_dim(g_unit, place.index * features_here, features_here, 1).T
    row_sums = row_sums.reshape(3, features)
    row_width = row_vectors.shape[1]
    g_rows = lax.dynamic_slice_in_dim(
        row_sums, (place.index * tensor_size + place.y) * row_width, row_width, 1
    )
    g_rows = jnp.concatenate([g_rows, g_rows[2:]])

    joint_new = [kinds_first(new) for new in joint_new]
    head_new = adam_update(head_bias, g_head, head_mean, head_square, 0.1, 0.0)
    unit_new = adam_update(unit_bias, g_unit, unit_mean, unit_square, 0.1, 0.0)
    rows_new = adam_update(row_vectors, g_rows, rows_mean, rows_square, 0.1, 0.0)
    return (
        layer_output,
        input_grad,
        joint_new[0],
        joint_new[1],
        joint_new[2],
        dense_new[0],
        dense_new[1],
        dense_new[2],
        expand_new[0],
        expand_new[1],
        expand_new[2],
        shrink_new[0],
        shrink_new[1],
        shrink_new[2],
        head_new[0],
        head_new[1],
        head_new[2],
        unit_new[0],
        unit_new[1],
        unit_new[2],
        rows_new[0],
        rows_new[1],
        rows_new[2],
    )


def solution(mesh):
    return jax.shard_map(
        functools.partial(body, mesh.shape["dp"], mesh.shape["tensor"]),
        mesh=mesh,
        in_specs=(
            P(("dp", "tensor"), None),
            P(("dp", "tensor"), None),
            P("dp"),
            P("dp", None, "tensor"),
            P("dp", "tensor"),
            P("dp", "tensor"),
            P("dp", "tensor"),
            P("dp", None, "tensor"),
            P("dp", "tensor"),
            P(None, ("dp", "tensor")),
            P("dp", None, "tensor"),
            P("dp", None, "tensor"),
            P("dp", "tensor"),
            P("dp", "tensor"),
            P("dp", "tensor"),
            P("dp", "tensor"),
            P("dp", "tensor"),
            P("dp", "tensor"),
            P("dp", None, "tensor"),
            P("dp", None, "tensor"),
            P("dp", "tensor"),
            P("dp", "tensor"),
            P(None, ("dp", "tensor")),
            P(None, ("dp", "tensor")),
        ),
        out_specs=(
            P(("dp", "tensor"), None),
            P(("dp", "tensor"), None),
            P("dp", None, "tensor"),
            P("dp", None, "tensor"),
            P("dp", None, "tensor"),
            P("dp", "tensor"),
            P("dp", "tensor"),
            P("dp", "tensor"),
            P("dp", "tensor"),
            P("dp", "tensor"),
            P("dp", "tensor"),
            P("dp", "tensor"),
            P("dp", "tensor"),
            P("dp", "tensor"),
            P("dp", None, "tensor"),
            P("dp", None, "tensor"),
            P("dp", None, "tensor"),
            P("dp", "tensor"),
            P("dp", "tensor"),
            P("dp", "tensor"),
            P(None, ("dp", "tensor")),
            P(None, ("dp", "tensor")),
            P(None, ("dp", "tensor")),
        ),
        check_vma=False,
    )
```

```python
import functools
import math

import jax
import jax.numpy as jnp
from jax import lax
from jax.experimental import pallas as pl
from jax.experimental.pallas import tpu as pltpu
from jax.sharding import PartitionSpec as P

D = 2048
HD = 64
FF = 8192
ROTARY = 32
STEP = 10


EPS_NORM = 1e-05
BETA_ONE = 0.9
BETA_TWO = 0.95
EPS_ADAM = 1e-08
WEIGHT_DECAY = 0.1


def doc_positions(segments):
    row_count = segments.shape[0]
    places = jnp.arange(row_count, dtype=jnp.int32)
    same_doc = segments[:, None] == segments[None, :]
    starts = jnp.min(jnp.where(same_doc, places[None, :], row_count), axis=1)
    allowed = same_doc & (places[None, :] <= places[:, None])
    return ((places - starts).astype(jnp.float32), allowed)


def adam_update(weight, gradient, moment, square, step_rate, decay_rate):
    new_moment = BETA_ONE * moment + (1.0 - BETA_ONE) * gradient
    new_square = BETA_TWO * square + (1.0 - BETA_TWO) * gradient * gradient
    fix_one = 1.0 - BETA_ONE**STEP
    fix_two = 1.0 - BETA_TWO**STEP
    update = new_moment / fix_one / (jnp.sqrt(new_square / fix_two) + EPS_ADAM)
    return (weight - step_rate * (update + decay_rate * weight), new_moment, new_square)


AXES = ("dp", "tensor")
LOW = jnp.bfloat16
WIDE = jnp.float32


def after(array, *others):
    others = [o for o in others if o is not None]
    return lax.optimization_barrier((array, *others))[0] if others else array


def cost(flops, nbytes):
    return pl.CostEstimate(flops=int(flops) >> 10, bytes_accessed=int(nbytes) >> 10, transcendentals=0)


class Place:
    def __init__(self, dp_size, tensor_size):
        count = dp_size.bit_length() - 1
        self.dp_size, self.tensors, self.count = dp_size, tensor_size, count
        self.core, self.side = 1, 1 << (count - 2)
        self.ring = [1 << b for b in range(count - 1, 0, -1) if 1 << b != self.side]
        self.index = lax.axis_index("dp")
        self.y = lax.axis_index("tensor")
        self.quarter = self.bit(self.side) * 2 + self.bit(self.core)
        self.masks = [0]
        for bit in reversed(self.ring):
            self.masks = self.masks + [m | bit for m in self.masks]
        self.last = {}

    def bit(self, mask):
        return (self.index // mask) % 2

    def move(self, array, mask, y=0, lane=None):
        pairs = []
        for dp in range(self.dp_size):
            for oy in range(self.tensors):
                pairs.append((dp * self.tensors + oy, (dp ^ mask) * self.tensors + (oy ^ y)))
        if lane is not None:
            array = after(array, self.last.get(lane))
        got = lax.ppermute(array, AXES, pairs)
        if lane is not None:
            self.last[lane] = got
        return got

    def to_own_order(self, array):
        lead = array.shape[:-1]
        split = array.reshape(lead + (2,) * self.count + (-1,))
        first = len(lead)
        ring_axes = [first + self.count - bit.bit_length() for bit in self.ring]
        for bit, axis in zip(self.ring, ring_axes):
            split = jnp.where(self.bit(bit) == 0, split, jnp.flip(split, axis))
        rest = [first + b for b in range(self.count + 1) if first + b not in ring_axes]
        split = split.transpose(list(range(first)) + ring_axes + rest)
        return split.reshape(array.shape)

    def to_index_order(self, array):
        lead = array.shape[:-1]
        split = array.reshape(lead + (2,) * self.count + (-1,))
        first = len(lead)
        ring_axes = [first + self.count - bit.bit_length() for bit in self.ring]
        rest = [first + b for b in range(self.count + 1) if first + b not in ring_axes]
        order = list(range(first)) + ring_axes + rest
        split = split.transpose([order.index(i) for i in range(len(order))])
        for bit, axis in zip(self.ring, ring_axes):
            split = jnp.where(self.bit(bit) == 0, split, jnp.flip(split, axis))
        return split.reshape(array.shape)


def as_hbm(shapes):
    if not isinstance(shapes, list):
        return as_hbm([shapes])[0]
    return [pltpu.HBM(s.shape, s.dtype) if s.size > 1 << 16 else s for s in shapes]


def in_hbm(*arrays):
    return [
        pltpu.with_memory_space_constraint(a, pltpu.HBM) if a.size > 1 << 16 else a for a in arrays
    ]


def pick(array, index, axis=0):
    return lax.dynamic_index_in_dim(array, index, axis, keepdims=False)


def swap_quarters(place, pieces):
    return [
        pieces[0],
        place.move(pieces[1], place.core),
        place.move(pieces[2], place.side),
        place.move(pieces[3], place.side | place.core),
    ]


def arrange_kernel(back, statics, own_ref, array_ref, out_ref):
    width = array_ref.shape[1] // len(statics)
    for r, static in enumerate(statics):
        at = pl.multiple_of((own_ref[0] ^ static) * width, 128)
        here = slice(r * width, (r + 1) * width)
        if back:
            out_ref[:, pl.ds(at, width)] = array_ref[:, here]
        else:
            out_ref[:, here] = array_ref[:, pl.ds(at, width)]


def arrange(place, array, back=False):
    if array.shape[1] // place.dp_size % 128:
        return place.to_index_order(array) if back else place.to_own_order(array)
    ring = sum(place.ring)
    inner = (0, place.core, place.side, place.side | place.core)
    statics = [mask | i for mask in place.masks for i in inner]
    return pl.pallas_call(
        functools.partial(arrange_kernel, back, statics),
        in_specs=[
            pl.BlockSpec(memory_space=pltpu.SMEM),
            pl.BlockSpec(memory_space=pltpu.VMEM),
        ],
        out_specs=pl.BlockSpec(memory_space=pltpu.VMEM),
        out_shape=jax.ShapeDtypeStruct(array.shape, array.dtype),
        compiler_params=pltpu.CompilerParams(vmem_limit_bytes=24 << 20),
        cost_estimate=cost(0, 4 * array.size),
    )((place.index & ring).reshape(1), array)


class Gather:
    def __init__(self, place, block, *halves):
        self.place, self.halves = place, halves
        first, second = place.ring[:2]
        self.both = first | second
        self.first, self.second = first, second
        self.parts = {0: [block], first: [None, None], second: [None], self.both: [None, None]}

    def along_first(self, half, *others):
        got = self.place.move(after(self.halves[half], *others), self.first)
        self.parts[self.first][half] = got
        return got

    def along_second(self, *others):
        got = self.place.move(after(self.parts[0][0], *others), self.second)
        self.parts[self.second][0] = got
        return got

    def onward(self, half, *others):
        got = self.place.move(after(self.parts[self.first][half], *others), self.second)
        self.parts[self.both][half] = got
        return got

    def whole(self):
        for bit in self.place.ring[2:]:
            for mask in list(self.parts):
                self.parts[mask | bit] = [self.place.move(p, bit) for p in self.parts[mask]]
        return [part for m in self.place.masks for part in self.parts[m]]


class Reduce:
    def __init__(self, place, *pairs):
        self.place, self.parts = place, gradient_blocks(place, *pairs)
        for bit in reversed(place.ring[2:]):
            for mask in [m for m in self.parts if m & bit]:
                got = place.move(self.parts.pop(mask), bit)
                total = self.parts[mask ^ bit].astype(WIDE) + got.astype(WIDE)
                self.parts[mask ^ bit] = total.astype(LOW)

    def halves(self, array):
        half = array.shape[0] // 2
        return [array[:half].astype(WIDE), array[half:].astype(WIDE)]

    def send_both(self, *others, before=()):
        first, second = self.place.ring[:2]
        got = self.place.move(after(self.parts[first | second], *others), second)
        got, own = self.halves(after(got, *before)), self.halves(self.parts[first])
        self.sent = [(a + b).astype(LOW) for a, b in zip(got, own)]
        return tuple(self.sent)

    def send_second(self, *others, before=()):
        second = self.place.ring[1]
        got = after(self.place.move(after(self.parts[second], *others), second), *before)
        self.sums = [a + b for a, b in zip(self.halves(got), self.halves(self.parts[0]))]
        return (got,)

    def send_half(self, half, *others, before=()):
        got = self.place.move(after(self.sent[half], *others), self.place.ring[0])
        self.sums[half] = (self.sums[half] + after(got, *before).astype(WIDE)).astype(LOW)
        return (self.sums[half],)


def choose_kernel(quarter_ref, early_ref, late_ref, *outs):
    rows = outs[0].shape[0]
    for quarter in range(4):
        source = early_ref if quarter < 2 else late_ref
        for flip, out in zip(FLIPS, outs):

            @pl.when(quarter_ref[0] ^ quarter == flip)
            def _():
                out[...] = source[(quarter % 2) * rows : (quarter % 2 + 1) * rows, :]


def choose(place, halves):
    rows, width = halves[0].shape[0] // 2, halves[0].shape[1]
    return pl.pallas_call(
        choose_kernel,
        in_specs=[pl.BlockSpec(memory_space=pltpu.SMEM)]
        + [pl.BlockSpec(memory_space=pltpu.VMEM)] * 2,
        out_specs=[pl.BlockSpec(memory_space=pltpu.VMEM)] * 4,
        out_shape=[jax.ShapeDtypeStruct((rows, width), LOW)] * 4,
        cost_estimate=cost(0, 16 * rows * width),
    )(place.quarter.reshape(1), *halves)


def cores_kernel(near_ref, got_ref, first_ref, second_ref, side_ref, y_ref):
    step = pl.program_id(0)
    cut = first_ref.shape[1]

    def write(out, part):
        total = near_ref[part, :].astype(WIDE) + got_ref[part, :].astype(WIDE)
        out[0] = total.astype(LOW)

    early, late = pl.ds(0, cut), pl.ds(cut, near_ref.shape[0] - cut)
    pl.when(step < 2)(lambda: write(first_ref, early))
    pl.when(step >= 2)(lambda: write(side_ref, early))
    pl.when(step % 2 == 0)(lambda: write(second_ref, late))
    pl.when(step % 2 == 1)(lambda: write(y_ref, late))


def add_cores(near, got, cut):
    rows, features = near.shape[0] // 4, near.shape[1]
    block = pl.BlockSpec((rows, features), lambda i: (i, 0))
    early = (1, cut, features)
    late = (1, rows - cut, features)
    return pl.pallas_call(
        cores_kernel,
        grid=(4,),
        in_specs=[block, block],
        out_specs=[
            pl.BlockSpec(early, lambda i: (jnp.minimum(i, 1), 0, 0)),
            pl.BlockSpec(late, lambda i: (i // 2, 0, 0)),
            pl.BlockSpec(early, lambda i: (jnp.maximum(i - 2, 0), 0, 0)),
            pl.BlockSpec(late, lambda i: (i // 2, 0, 0)),
        ],
        out_shape=as_hbm([
            jax.ShapeDtypeStruct((2,) + shape[1:], LOW) for shape in (early, late, early, late)
        ]),
        compiler_params=pltpu.CompilerParams(vmem_limit_bytes=32 << 20),
        cost_estimate=cost(0, 24 * rows * features),
    )(*in_hbm(near, got))


class GroupSum:
    def __init__(self, place, far, near):
        self.place, self.far, self.near = place, far, near

    def by_core(self, *others):
        got = self.place.move(after(self.far, *others), self.place.core)
        self.first, self.second, *self.sent = add_cores(self.near, got, self.near.shape[0] // 64 * 5)
        return self.sent

    def hop(self, *others):
        place, (first, second) = self.place, self.sent
        got_side = place.move(after(first, *others), place.side)
        got_y = place.move(after(second, *others), 0, 1)
        self.first = self.first.astype(WIDE) + got_side.astype(WIDE)
        self.second = self.second.astype(WIDE) + got_y.astype(WIDE)
        self.sent = [self.first[1].astype(LOW), self.second[1].astype(LOW)]
        return self.sent

    def last_hop(self, *others):
        place, (first, second) = self.place, self.sent
        self.got = [
            place.move(after(first, *others), 0, 1),
            place.move(after(second, *others), place.side),
        ]
        return jnp.concatenate(
            [a[0] + b.astype(WIDE) for a, b in zip((self.first, self.second), self.got)]
        )


class SmallGather:
    def __init__(self, place, vector):
        self.place, self.rows, self.bits = place, vector[None], []

    def step(self, mask, y=0, *others):
        got = self.place.move(after(self.rows, *others), mask, y)
        self.rows = jnp.concatenate([self.rows, got])
        self.bits.append(2 * mask + y)
        return self.rows

    def whole(self):
        place = self.place
        for b in range(place.count):
            if 2 << b not in self.bits:
                self.step(1 << b)
        length = self.rows.shape[1]
        split = self.rows.reshape((2,) * len(self.bits) + (length,))
        axes = []
        for b in [2 << b for b in range(place.count - 1, -1, -1)] + [1]:
            axis = len(self.bits) - 1 - self.bits.index(b)
            own = place.y if b == 1 else place.bit(b // 2)
            split = jnp.where(own == 0, split, jnp.flip(split, axis))
            axes.append(axis)
        return split.transpose(axes + [len(axes)]).reshape(-1, length)


class SmallReduce:
    def __init__(self, place, own, shared):
        self.place, self.width = place, own.size
        slot = place.y * 4 + place.quarter
        padded = jnp.zeros((4 * place.tensors, own.size), WIDE)
        padded = lax.dynamic_update_slice_in_dim(padded, own[None], slot, 0)
        self.vector = jnp.concatenate([padded.reshape(-1), shared])

    def step(self, *moves):
        self.vector = self.vector + sum(self.place.move(self.vector, *move) for move in moves)

    def results(self):
        count = 4 * self.place.tensors * self.width
        own = self.vector[:count].reshape(self.place.tensors, 4, self.width)
        return pick(own, self.place.y), self.vector[count:]


FLIPS = (0, 1, 2, 3)


def pack_kernel(quarter_ref, *refs):
    shards, outs = refs[: len(refs) - 4], refs[len(refs) - 4 :]
    for flip, out in zip(FLIPS, outs):
        quarter = quarter_ref[0] ^ flip
        column = 0
        for shard in shards:
            width = shard.shape[2] // 4
            for kind in range(shard.shape[0]):
                at = pl.multiple_of(quarter * width, 128)
                out[:, column : column + width] = shard[kind, :, pl.ds(at, width)].astype(LOW)
                column += width


def pack(place, *shards):
    rows = shards[0].shape[1]
    width = sum(s.shape[0] * s.shape[2] for s in shards) // 4
    return pl.pallas_call(
        pack_kernel,
        in_specs=[pl.BlockSpec(memory_space=pltpu.SMEM)]
        + [pl.BlockSpec(memory_space=pltpu.VMEM)] * len(shards),
        out_specs=[pl.BlockSpec(memory_space=pltpu.VMEM)] * 4,
        out_shape=[jax.ShapeDtypeStruct((rows, width), LOW)] * 4,
        compiler_params=pltpu.CompilerParams(vmem_limit_bytes=24 << 20),
        cost_estimate=cost(0, 24 * rows * width),
    )(place.quarter.reshape(1), *shards)


def stack_kernel(count, quarter_ref, *refs):
    pieces, outs = refs[:count], refs[count:]
    third = len(outs) // 3
    outs, halves = outs[:third], (outs[third : 2 * third], outs[2 * third :])
    rows = sum(piece.shape[0] for piece in pieces) // 4
    flip = 0
    for piece in pieces:
        for part in range(piece.shape[0] // rows):
            at = pl.multiple_of((quarter_ref[0] ^ flip) * rows, 16)
            column = 0
            for out in outs:
                width = out.shape[1]
                out[pl.ds(at, rows), :] = piece[
                    part * rows : (part + 1) * rows, column : column + width
                ]
                column += width
            flip += 1
    for out, early, late in zip(outs, *halves):
        early[...] = out[: 2 * rows]
        late[...] = out[2 * rows :]


def stack(place, pieces, widths):
    rows = sum(piece.shape[0] for piece in pieces)
    outs = pl.pallas_call(
        functools.partial(stack_kernel, len(pieces)),
        in_specs=[pl.BlockSpec(memory_space=pltpu.SMEM)]
        + [pl.BlockSpec(memory_space=pltpu.VMEM)] * len(pieces),
        out_specs=[pl.BlockSpec(memory_space=pltpu.VMEM)] * (3 * len(widths)),
        out_shape=[
            jax.ShapeDtypeStruct((r, w), LOW) for r in (rows, rows // 2, rows // 2) for w in widths
        ],
        compiler_params=pltpu.CompilerParams(vmem_limit_bytes=24 << 20),
        cost_estimate=cost(0, 4 * rows * sum(widths)),
    )(place.quarter.reshape(1), *pieces)
    return list(zip(outs[: len(widths)], outs[len(widths) : 2 * len(widths)], outs[-len(widths) :]))


def adam_kernel(step_rate, column, quarter_ref, near_ref, core_ref, side_ref, both_ref, *refs):
    weight, moment, square, new_weight, new_moment, new_square = refs
    distance = pl.program_id(0) ^ quarter_ref[0]
    for flip, piece in zip(FLIPS, (near_ref, core_ref, side_ref, both_ref)):

        @pl.when(distance == flip)
        def _():
            width = weight.shape[2]
            for kind in range(weight.shape[0]):
                start = column + kind * width
                results = adam_update(
                    weight[kind],
                    piece[:, start : start + width].astype(WIDE),
                    moment[kind],
                    square[kind],
                    step_rate,
                    WEIGHT_DECAY,
                )
                new_weight[kind], new_moment[kind], new_square[kind] = results


def adam_shard(place, pieces, column, weight, moment, square, step_rate):
    kinds, rows, width = weight.shape
    block = pl.BlockSpec((kinds, rows, width // 4), lambda q: (0, 0, q))
    return pl.pallas_call(
        functools.partial(adam_kernel, step_rate, column),
        grid=(4,),
        in_specs=[pl.BlockSpec(memory_space=pltpu.SMEM)]
        + [pl.BlockSpec(pieces[0].shape, lambda q: (0, 0))] * 4
        + [block] * 3,
        out_specs=[block] * 3,
        out_shape=[jax.ShapeDtypeStruct(weight.shape, WIDE)] * 3,
        compiler_params=pltpu.CompilerParams(vmem_limit_bytes=32 << 20),
        cost_estimate=pl.CostEstimate(
            flops=20 * weight.size, bytes_accessed=26 * weight.size, transcendentals=0
        ),
    )(*in_hbm(place.quarter.reshape(1), *pieces, weight, moment, square))


def join_kernel(starts, *refs):
    arrays, out = refs[:-1], refs[-1]
    step = pl.program_id(0)
    for array, start, end in zip(arrays, starts, starts[1:]):

        @pl.when((step >= start) & (step < end))
        def _():
            out[...] = array[...]


def join(*arrays):
    tile = arrays[0].shape[0] // 2
    starts = [0]
    for array in arrays:
        starts.append(starts[-1] + array.shape[0] // tile)
    width = arrays[0].shape[1]

    def spec(start, end):
        return pl.BlockSpec((tile, width), lambda i: (jnp.clip(i - start, 0, end - start - 1), 0))

    return pl.pallas_call(
        functools.partial(join_kernel, starts),
        grid=(starts[-1],),
        in_specs=[spec(*ends) for ends in zip(starts, starts[1:])],
        out_specs=pl.BlockSpec((tile, width), lambda i: (i, 0)),
        out_shape=as_hbm(jax.ShapeDtypeStruct((starts[-1] * tile, width), arrays[0].dtype)),
        compiler_params=pltpu.CompilerParams(vmem_limit_bytes=32 << 20),
        cost_estimate=cost(0, 4 * starts[-1] * tile * width),
    )(*in_hbm(*arrays))


def norm_kernel(count, *refs):
    pieces, far_ref, vectors_ref, normed_ref = refs[:count], *refs[count:]

    def write(ref):
        rows = ref[...].astype(WIDE)
        centered = rows - jnp.mean(rows, axis=-1, keepdims=True)
        inverse = lax.rsqrt(jnp.mean(centered * centered, axis=-1, keepdims=True) + EPS_NORM)
        normed_ref[...] = (centered * inverse * vectors_ref[0:1] + vectors_ref[1:2]).astype(LOW)

    step = pl.program_id(0)
    for i, piece in enumerate(pieces):
        pl.when(step == i)(functools.partial(write, piece))
    pl.when(step >= count)(functools.partial(write, far_ref))


def norm(pieces, far, vectors):
    rows, features = pieces[0].shape
    count = len(pieces)
    return pl.pallas_call(
        functools.partial(norm_kernel, count),
        grid=(2 * count,),
        in_specs=[pl.BlockSpec((rows, features), lambda i: (0, 0))] * count
        + [
            pl.BlockSpec((rows, features), lambda i: (jnp.maximum(i - count, 0), 0)),
            pl.BlockSpec(vectors.shape, lambda i: (0, 0)),
        ],
        out_specs=pl.BlockSpec((rows, features), lambda i: (i, 0)),
        out_shape=as_hbm(jax.ShapeDtypeStruct((2 * count * rows, features), LOW)),
        compiler_params=pltpu.CompilerParams(vmem_limit_bytes=32 << 20),
        cost_estimate=cost(0, 8 * count * rows * features),
    )(*in_hbm(*pieces, far, vectors))


VMEM_LIMIT = 40 << 20


def dot(left, right, left_axis, right_axis):
    return lax.dot_general(
        left, right, (((left_axis,), (right_axis,)), ((), ())), preferred_element_type=WIDE
    )


def lay(block_lists, cuts, weights_ref, arrived):
    @pl.when(pl.program_id(0) == 0)
    def _():
        copies, column = [], 0
        for blocks, (start, width) in zip(block_lists, cuts):
            at = 0
            for block in blocks:
                depth = block.shape[0]
                copy = pltpu.make_async_copy(
                    block.at[:, pl.ds(start, width)],
                    weights_ref.at[pl.ds(at, depth), pl.ds(column, width)],
                    arrived.at[len(copies)],
                )
                copy.start()
                copies.append(copy)
                at += depth
            column += width
        for copy in copies:
            copy.wait()


def laid(features, width, *block_lists):
    count = sum(len(blocks) for blocks in block_lists)
    return [pltpu.VMEM((features, width), LOW), pltpu.SemaphoreType.DMA((count,))]


ANYWHERE = pl.BlockSpec(memory_space=pl.ANY)


def whole_spec(array):
    return pl.BlockSpec(array.shape, lambda i: (0, 0))


def row_spec(rows, array):
    return pl.BlockSpec((rows, array.shape[1]), lambda i: (i, 0))


GELU_A, GELU_B = (2 / math.pi) ** 0.5, 0.044715


def hidden_kernel(rows_ref, shift_ref, *refs):
    blocks, (slope_ref, hidden_ref, weights_ref, arrived) = refs[:-4], refs[-4:]
    lay([blocks], [(0, slope_ref.shape[1])], weights_ref, arrived)
    pre = dot(rows_ref[...], weights_ref[...], 1, 0) + shift_ref[...]
    square = pre * pre
    bend = jnp.tanh(GELU_A * (pre + GELU_B * (square * pre)))
    raised = 0.5 * (1.0 + bend)
    hidden_ref[...] = (pre * raised).astype(LOW)
    slope = raised + 0.5 * pre * (1.0 - bend * bend) * (GELU_A * (1.0 + 3.0 * GELU_B * square))
    slope_ref[...] = slope.astype(LOW)


def hidden_units(rows, shift, blocks):
    count, features = rows.shape
    width = blocks[0].shape[1]
    tile = count // 4
    return pl.pallas_call(
        hidden_kernel,
        grid=(4,),
        in_specs=[row_spec(tile, rows), whole_spec(shift)] + [ANYWHERE] * len(blocks),
        out_specs=[pl.BlockSpec((tile, width), lambda i: (i, 0))] * 2,
        out_shape=as_hbm([jax.ShapeDtypeStruct((count, width), LOW)] * 2),
        scratch_shapes=laid(features, width, blocks),
        compiler_params=pltpu.CompilerParams(vmem_limit_bytes=VMEM_LIMIT),
        cost_estimate=cost(2 * rows.size * width, 2 * rows.size + 6 * count * width),
    )(*in_hbm(rows, shift, *blocks))


def d_pre_kernel(rows_ref, slope_ref, *refs):
    blocks, (d_pre_ref, sums_ref, weights_ref, arrived) = refs[:-4], refs[-4:]

    @pl.when(pl.program_id(0) == 0)
    def _():
        sums_ref[...] = jnp.zeros_like(sums_ref)

    lay([blocks], [(0, slope_ref.shape[1])], weights_ref, arrived)
    d_hidden = dot(rows_ref[...], weights_ref[...], 1, 0)
    low = (d_hidden * slope_ref[...].astype(WIDE)).astype(LOW)
    d_pre_ref[...] = low
    sums_ref[...] += jnp.sum(low.astype(WIDE), axis=0, keepdims=True)


def d_pre_units(rows, slope, blocks):
    count, width = slope.shape
    tile = count // 4
    return pl.pallas_call(
        d_pre_kernel,
        grid=(4,),
        in_specs=[row_spec(tile, rows), row_spec(tile, slope)] + [ANYWHERE] * len(blocks),
        out_specs=[
            pl.BlockSpec((tile, width), lambda i: (i, 0)),
            pl.BlockSpec((1, width), lambda i: (0, 0)),
        ],
        out_shape=as_hbm([
            jax.ShapeDtypeStruct((count, width), LOW),
            jax.ShapeDtypeStruct((1, width), WIDE),
        ]),
        scratch_shapes=laid(rows.shape[1], width, blocks),
        compiler_params=pltpu.CompilerParams(vmem_limit_bytes=VMEM_LIMIT),
        cost_estimate=cost(2 * rows.size * width, 2 * rows.size + 6 * count * width),
    )(*in_hbm(rows, slope, *blocks))


def gradient_kernel(pairs, *refs):
    operands, outs = refs[: 2 * pairs], refs[2 * pairs :]

    def write(out):
        column = 0
        for i in range(pairs):
            part = dot(operands[2 * i][...], operands[2 * i + 1][...], 0, 0).astype(LOW)
            out[:, column : column + part.shape[1]] = part
            column += part.shape[1]

    for step, out in enumerate(outs):
        pl.when(pl.program_id(0) == step)(functools.partial(write, out))


def gradient_blocks(place, *pairs):
    count, features = pairs[0][0].shape
    steps = len(place.masks)
    rows = features // steps
    width = sum(right.shape[1] for _, right in pairs)
    specs = []
    for _, right in pairs:
        specs += [pl.BlockSpec((count, rows), lambda i: (0, i)), whole_spec(right)]
    outs = pl.pallas_call(
        functools.partial(gradient_kernel, len(pairs)),
        grid=(steps,),
        in_specs=specs,
        out_specs=[pl.BlockSpec((rows, width), lambda i: (0, 0))] * steps,
        out_shape=as_hbm([jax.ShapeDtypeStruct((rows, width), LOW)] * steps),
        compiler_params=pltpu.CompilerParams(vmem_limit_bytes=VMEM_LIMIT),
        cost_estimate=cost(2 * count * features * width, 2 * count * (features + width)),
    )(*in_hbm(*[array for pair in pairs for array in pair]))
    return dict(zip(place.masks, outs))


def spread_kernel(cuts, counts, summed, *refs):
    if summed:
        (normed_ref, vectors_ref), refs = refs[:2], refs[2:]
        sums_ref, refs = refs[-3], refs[:-3] + refs[-2:]
    lefts, rest = refs[: len(cuts)], refs[len(cuts) :]
    block_lists = []
    for count in counts:
        block_lists.append(rest[:count])
        rest = rest[count:]
    far_ref, near_ref, weights_ref, arrived = rest
    lay(block_lists, cuts, weights_ref, arrived)
    left = jnp.concatenate([ref[...] for ref in lefts], axis=1)

    def write(out):
        total = dot(left, weights_ref[...], 1, 1)
        out[...] = total.astype(LOW)
        if summed:
            unit = normed_ref[...].astype(WIDE) - vectors_ref[1:2]
            sums_ref[0:1] += jnp.sum(total * unit, axis=0, keepdims=True)
            sums_ref[1:2] += jnp.sum(total, axis=0, keepdims=True)

    if summed:

        @pl.when(pl.program_id(0) == 0)
        def _():
            sums_ref[...] = jnp.zeros_like(sums_ref)

    pl.when(pl.program_id(0) < 2)(lambda: write(far_ref))
    pl.when(pl.program_id(0) >= 2)(lambda: write(near_ref))


def spread(lefts, block_lists, cuts, *unit):
    count = lefts[0].shape[0]
    tile = count // 4
    features = sum(b.shape[0] for b in block_lists[0])
    depth = sum(width for _, width in cuts)
    return pl.pallas_call(
        functools.partial(spread_kernel, cuts, [len(b) for b in block_lists], bool(unit)),
        grid=(4,),
        in_specs=[
            pl.BlockSpec((tile, rows.shape[1]), lambda i: ((i + 2) % 4, 0)) for rows in unit[:1]
        ]
        + [whole_spec(vectors) for vectors in unit[1:]]
        + [pl.BlockSpec((tile, left.shape[1]), lambda i: ((i + 2) % 4, 0)) for left in lefts]
        + [ANYWHERE] * sum(len(blocks) for blocks in block_lists),
        out_specs=[
            pl.BlockSpec((tile, features), lambda i: (jnp.minimum(i, 1), 0)),
            pl.BlockSpec((tile, features), lambda i: (jnp.maximum(i - 2, 0), 0)),
        ]
        + [pl.BlockSpec((2, features), lambda i: (0, 0)) for _ in unit[:1]],
        out_shape=as_hbm([jax.ShapeDtypeStruct((count // 2, features), LOW)] * 2
        + [jax.ShapeDtypeStruct((2, features), WIDE) for _ in unit[:1]]),
        scratch_shapes=laid(features, depth, *block_lists),
        compiler_params=pltpu.CompilerParams(vmem_limit_bytes=VMEM_LIMIT),
        cost_estimate=cost(2 * count * features * depth, 2 * count * (features + depth)),
    )(*in_hbm(*unit, *lefts, *[b for blocks in block_lists for b in blocks]))


PAIR = 2 * HD
SCALE = HD ** (-0.5)
TILES = 2


def turn(pair, cosine, sine):
    half = ROTARY // 2
    lane = lax.broadcasted_iota(jnp.int32, pair.shape, 1) % HD
    partner = jnp.where(lane < half, pltpu.roll(pair, PAIR - half, 1), pltpu.roll(pair, half, 1))
    return pair * cosine + partner * sine


def two_heads(pair):
    lane = lax.broadcasted_iota(jnp.int32, pair.shape, 1) // HD
    zero = jnp.zeros_like(pair)
    return jnp.concatenate([jnp.where(lane == head, pair, zero) for head in range(2)])


def either(stacked):
    rows = stacked.shape[0] // 2
    lane = lax.broadcasted_iota(jnp.int32, (rows, PAIR), 1) // HD
    return jnp.where(lane == 0, stacked[:rows], stacked[rows:])


def seen(ids_col, ids_row, first, rows, width):
    key = lax.broadcasted_iota(jnp.int32, (width, rows), 0)
    query = lax.broadcasted_iota(jnp.int32, (width, rows), 1) + first
    mask = (ids_col[:width] == ids_row[:, first : first + rows]) & (key <= query)
    return jnp.concatenate([mask, mask], axis=1)


def halves(y_ref, rows, cos_ref, sin_ref):
    places = [pl.ds(pl.multiple_of((y_ref[0] ^ t) * rows, 128), rows) for t in range(TILES)]
    cuts = [slice(t * rows, (t + 1) * rows) for t in range(TILES)]
    return places, [(cos_ref[cut], sin_ref[cut]) for cut in cuts]


def forward_kernel(y_ref, rows_ref, shift_ref, cos_ref, sin_ref, col_ref, row_ref, *refs):
    blocks, outs, (joint_ref, weights_ref, arrived) = refs[:-6], refs[-6:-3], refs[-3:]
    turned_ref, context_ref, log_ref = outs
    slots, width = context_ref.shape
    lay([blocks], [(0, 3 * width)], weights_ref, arrived)
    joint_ref[...] = dot(rows_ref[...], weights_ref[...], 1, 0)
    ids_col, ids_row = col_ref[...], row_ref[0]
    rows = slots // TILES
    masks = [seen(ids_col, ids_row, t * rows, rows, (t + 1) * rows) for t in range(TILES)]
    places, tables = halves(y_ref, rows, cos_ref, sin_ref)
    log_ref[...] = jnp.zeros_like(log_ref)
    for p in range(width // PAIR):
        columns = [slice(j * width + p * PAIR, j * width + (p + 1) * PAIR) for j in range(3)]
        query, key, value = [], [], []
        for place, table in zip(places, tables):
            parts = [joint_ref[place, c] + shift_ref[:, c] for c in columns]
            query.append(turn(parts[0], *table).astype(LOW))
            key.append(turn(parts[1], *table).astype(LOW))
            value.append(parts[2].astype(LOW))
            for c, array in zip(columns, (query, key, value)):
                turned_ref[place, c] = array[-1]
        key, value = jnp.concatenate(key), jnp.concatenate(value)
        for t in range(TILES):
            keys = (t + 1) * rows
            scores = dot(key[:keys], two_heads(query[t] * SCALE), 1, 1)
            scores = jnp.where(masks[t], scores, -1e30)
            top = jnp.max(scores, axis=0, keepdims=True)
            raised = jnp.exp(scores - top)
            total = jnp.sum(raised, axis=0, keepdims=True)
            probs = (raised * (1.0 / total)).astype(LOW)
            out = dot(probs, value[:keys], 0, 0)
            log_total = top + jnp.log(total)
            for head in range(2):
                log_ref[2 * p + head : 2 * p + head + 1, t * rows : (t + 1) * rows] = log_total[
                    :, head * rows : (head + 1) * rows
                ]
            context_ref[places[t], p * PAIR : (p + 1) * PAIR] = either(out).astype(LOW)


def backward_kernel(y_ref, turned_ref, rows_ref, log_ref, cos_ref, sin_ref, col_ref, row_ref, *refs):
    blocks, outs, (back_ref, weights_ref, arrived) = refs[:-5], refs[-5:-3], refs[-3:]
    joint_ref, sums_ref = outs
    slots, width = back_ref.shape
    lay([blocks], [(3 * width, width)], weights_ref, arrived)
    back_ref[...] = dot(rows_ref[...], weights_ref[...], 1, 0).astype(LOW)
    ids_col, ids_row = col_ref[...], row_ref[0]
    rows = slots // TILES
    masks = [seen(ids_col, ids_row, t * rows, rows, (t + 1) * rows) for t in range(TILES)]
    places, tables = halves(y_ref, rows, cos_ref, sin_ref)

    @pl.when(pl.program_id(0) == 0)
    def _():
        sums_ref[...] = jnp.zeros_like(sums_ref)

    for p in range(width // PAIR):
        columns = [slice(j * width + p * PAIR, j * width + (p + 1) * PAIR) for j in range(3)]
        key, value = (
            jnp.concatenate([turned_ref[place, c] for place in places]) for c in columns[1:]
        )
        d_query, d_key, d_value = [], [], []
        for t, place in enumerate(places):
            here, keys = slice(t * rows, (t + 1) * rows), (t + 1) * rows
            query = two_heads(turned_ref[place, columns[0]] * SCALE)
            d_context = two_heads(back_ref[place, p * PAIR : (p + 1) * PAIR])
            logs = jnp.concatenate(
                [log_ref[2 * p + head : 2 * p + head + 1, here] for head in range(2)], axis=1
            )
            scores = dot(key[:keys], query, 1, 1)
            probs = jnp.where(masks[t], jnp.exp(scores - logs), 0.0)
            d_probs = dot(value[:keys], d_context, 1, 1)
            delta = jnp.sum(probs * d_probs, axis=0, keepdims=True)
            d_scores = (probs * (d_probs - delta)).astype(LOW)
            d_query.append(either(dot(d_scores, key[:keys], 0, 0)) * SCALE)
            d_key.append(dot(d_scores, query, 1, 0))
            d_value.append(dot(probs.astype(LOW), d_context, 1, 0))
        for t, (place, (cosine, sine)) in enumerate(zip(places, tables)):
            here = slice(t * rows, (t + 1) * rows)
            parts = (
                turn(d_query[t], cosine, -sine),
                turn(sum(d[here] for d in d_key[t:]), cosine, -sine),
                sum(d[here] for d in d_value[t:]),
            )
            for c, array in zip(columns, parts):
                low = array.astype(LOW)
                joint_ref[place, c] = low
                sums_ref[:, c] += jnp.sum(low.astype(WIDE), axis=0, keepdims=True)


def by_group(slots, width):
    return pl.BlockSpec((slots, width), lambda g: (g, 0))


def attention_forward(place, normed, head_shift, cosine, sine, ids, blocks):
    groups, slots = ids.shape
    rows, width = normed.shape[0], blocks[0].shape[1] // 4
    return pl.pallas_call(
        forward_kernel,
        grid=(groups,),
        in_specs=[
            pl.BlockSpec(memory_space=pltpu.SMEM),
            row_spec(slots, normed),
            pl.BlockSpec((1, 3 * width), lambda g: (0, 0)),
            by_group(slots, PAIR),
            by_group(slots, PAIR),
            by_group(slots, 1),
            pl.BlockSpec((1, 1, slots), lambda g: (g, 0, 0)),
        ]
        + [ANYWHERE] * len(blocks),
        out_specs=[by_group(slots, 3 * width), by_group(slots, width), by_group(8, slots)],
        out_shape=as_hbm([
            jax.ShapeDtypeStruct((rows, 3 * width), LOW),
            jax.ShapeDtypeStruct((rows, width), LOW),
            jax.ShapeDtypeStruct((8 * groups, slots), WIDE),
        ]),
        scratch_shapes=[pltpu.VMEM((slots, 3 * width), WIDE)]
        + laid(normed.shape[1], 3 * width, blocks),
        compiler_params=pltpu.CompilerParams(vmem_limit_bytes=VMEM_LIMIT),
        cost_estimate=cost(20 * rows * slots * width + 6 * normed.size * width, 2 * normed.size),
    )(*in_hbm(place.y.reshape(1), normed, head_shift[None], cosine, sine, ids.reshape(-1, 1), ids[:, None], *blocks))


def attention_backward(place, turned, grad, logs, cosine, sine, ids, blocks):
    groups, slots = ids.shape
    rows, width = grad.shape[0], blocks[0].shape[1] // 4
    return pl.pallas_call(
        backward_kernel,
        grid=(groups,),
        in_specs=[
            pl.BlockSpec(memory_space=pltpu.SMEM),
            by_group(slots, 3 * width),
            row_spec(slots, grad),
            by_group(8, slots),
            by_group(slots, PAIR),
            by_group(slots, PAIR),
            by_group(slots, 1),
            pl.BlockSpec((1, 1, slots), lambda g: (g, 0, 0)),
        ]
        + [ANYWHERE] * len(blocks),
        out_specs=[by_group(slots, 3 * width), pl.BlockSpec((1, 3 * width), lambda g: (0, 0))],
        out_shape=as_hbm([
            jax.ShapeDtypeStruct((rows, 3 * width), LOW),
            jax.ShapeDtypeStruct((1, 3 * width), WIDE),
        ]),
        scratch_shapes=[pltpu.VMEM((slots, width), LOW)] + laid(grad.shape[1], width, blocks),
        compiler_params=pltpu.CompilerParams(vmem_limit_bytes=VMEM_LIMIT),
        cost_estimate=cost(50 * rows * slots * width + 2 * grad.size * width, 2 * grad.size),
    )(*in_hbm(place.y.reshape(1), turned, grad, logs, cosine, sine, ids.reshape(-1, 1), ids[:, None], *blocks))


def body(
    dp_size,
    tensor_size,
    tokens,
    cotangent,
    segment_ids,
    joint_weight,
    dense_weight,
    expand_weight,
    shrink_weight,
    head_bias,
    unit_bias,
    row_vectors,
    joint_mean,
    joint_square,
    dense_mean,
    dense_square,
    expand_mean,
    expand_square,
    shrink_mean,
    shrink_square,
    head_mean,
    head_square,
    unit_mean,
    unit_square,
    rows_mean,
    rows_square,
):
    place = Place(dp_size, tensor_size)
    devices = dp_size * tensor_size
    my_rows = tokens.shape[0]
    features = tokens.shape[1]
    group_slots = segment_ids.shape[0]
    shard_rows = joint_weight.shape[0]
    block_rows = 4 * shard_rows
    heads = head_bias.shape[2] // 4
    units = unit_bias.shape[1] // 4
    joint_width, unit_width = heads * HD, units * HD

    def kinds_first(array):
        return array.transpose(1, 0, 2)

    side, core = place.side, place.core
    first, second = place.ring[:2]
    small = SmallGather(
        place,
        jnp.concatenate(
            [
                row_vectors.reshape(-1),
                head_bias.reshape(-1),
                unit_bias.reshape(-1),
                segment_ids.astype(WIDE),
            ]
        ),
    )

    joint_shard = kinds_first(joint_weight)
    quarters = pack(place, joint_shard, dense_weight[None])
    by_core = place.move(quarters[1], core)
    by_side = place.move(quarters[2], side)
    by_both = place.move(quarters[3], side | core)
    small.step(0, 1, by_side)
    small.step(core)
    small.step(second)
    mine = arrange(place, tokens)
    near_quarters = pack(place, expand_weight[None], shrink_weight[None])
    my_ids = lax.dynamic_slice_in_dim(segment_ids, place.y * my_rows, my_rows)
    masked = arrange(place, cotangent * (my_ids > 0).astype(LOW)[:, None])
    blocks = stack(place, (quarters[0], by_core, by_side, by_both), (4 * joint_width,))[0]
    block, joint = blocks[0], Gather(place, *blocks)

    ready = (block, small.rows, mine)
    got = [
        joint.along_first(0),
        joint.along_second(),
        place.move(after(mine, *ready), side),
        place.move(after(mine, *ready), 0, 1),
        place.move(
            after(jnp.concatenate([near_quarters[1], near_quarters[3]]), *ready), core
        ),
    ]
    mine_side, mine_y, by_core = got[2:5]

    ready = tuple(got)
    got = [
        joint.along_first(1, *ready),
        joint.onward(0, *ready),
        place.move(after(mine_side, *ready), 0, 1),
        place.move(
            after(jnp.concatenate([near_quarters[2], by_core[shard_rows:]]), *ready), side
        ),
        small.step(first, 0, *ready),
    ]
    corner, by_side = got[2:4]
    near = join(mine, mine_y, mine_side, corner)
    blocks = stack(
        place, (near_quarters[0], by_core[:shard_rows], by_side), (unit_width, unit_width)
    )
    expand, shrink = (Gather(place, *array) for array in blocks)

    ready = tuple(got) + (blocks[0][0],)
    got = [
        expand.along_first(0, *ready),
        joint.onward(1, *ready),
        place.move(after(masked, *ready), side),
        place.move(after(masked, *ready), 0, 1),
        small.step(side, 0, *ready),
    ]
    masked_side, masked_y = got[2:4]

    cuts = [row_vectors.size, row_vectors.size + head_bias.size]
    cuts.append(cuts[1] + unit_bias.size)
    rows_small, head_small, unit_small, ids_small = jnp.split(small.whole(), cuts, axis=1)
    row_whole = rows_small.reshape(devices, 4, -1).transpose(1, 0, 2).reshape(4, features)
    head_small = pick(head_small.reshape((dp_size, tensor_size) + head_bias.shape), place.y, 1)
    head_low = lax.dynamic_slice_in_dim(head_small, place.quarter * heads, heads, 3)
    head_shift = head_low.reshape(HD, 3, heads).astype(LOW).astype(WIDE)
    head_shift = head_shift.transpose(1, 2, 0).reshape(-1)
    unit_small = pick(unit_small.reshape((dp_size, tensor_size) + unit_bias.shape), place.y, 1)
    unit_low = lax.dynamic_slice_in_dim(unit_small, place.quarter * units, units, 2)
    unit_shift = unit_low.reshape(HD, units).astype(LOW).astype(WIDE).T.reshape(-1)
    ids_small = ids_small.reshape(dp_size, tensor_size, group_slots)[:, 0]
    distances = (0, place.side, place.core, place.side | place.core)
    ids = jnp.stack([pick(ids_small, place.index ^ d) for d in distances])

    own_vectors = arrange(place, row_whole)
    positions = jax.vmap(doc_positions)(ids)[0].reshape(-1, 1)
    lane = jnp.arange(PAIR) % HD
    half_rot = ROTARY // 2
    frequency = 10000.0 ** (-(lane % half_rot).astype(WIDE) / half_rot)
    angles = positions * frequency
    cosine = jnp.where(lane < ROTARY, jnp.cos(angles), 1.0)
    sine = jnp.sin(angles)
    sine = jnp.where(lane < half_rot, -sine, jnp.where(lane < ROTARY, sine, 0.0))

    ready = tuple(got) + (cosine, sine, own_vectors, head_shift, unit_shift)
    got = [
        expand.along_first(1, *ready),
        expand.along_second(*ready),
        place.move(after(masked_side, *ready), 0, 1),
        place.move(after(near, *ready), core),
    ]
    normed = norm((mine, mine_y, mine_side, corner), got[3], own_vectors)

    ready = tuple(got) + (normed,)
    masked_corner = got[2]
    got = [
        shrink.along_first(0, *ready),
        expand.onward(0, *ready),
        expand.onward(1, *ready),
    ]
    joint = joint.whole()
    turned, context, logs = attention_forward(
        place, after(normed, *ready), head_shift, cosine, sine, ids, joint
    )

    ready = tuple(got) + (context,)
    grad_near = join(after(masked, *ready), masked_y, masked_side, masked_corner)
    got = [
        shrink.along_first(1, *ready),
        shrink.onward(0, *ready),
        shrink.along_second(*ready),
        place.move(grad_near, core),
    ]
    grad_all = join(grad_near, got[3])
    d_joint, joint_sums = attention_backward(
        place, turned, grad_all, logs, cosine, sine, ids, joint
    )
    expand = expand.whole()

    ready = tuple(got) + (d_joint,)
    got = [shrink.onward(1, *ready)]
    shrink = shrink.whole()
    sum_joint = Reduce(place, (after(normed, *ready), d_joint), (grad_all, context))

    def returned(reduce, *others):
        return list(choose(place, [after(half, *others) for half in reduce.sums]))

    ready = tuple(got) + tuple(sum_joint.parts.values())
    slope, hidden = hidden_units(after(normed, *ready), unit_shift[None], expand)
    got = sum_joint.send_both(*ready, before=(hidden,))

    ready = got + (hidden,)
    sum_shrink = Reduce(place, (after(grad_all, *ready), hidden))
    d_pre, unit_sums = d_pre_units(after(grad_all, *sum_shrink.parts.values()), slope, shrink)
    got = sum_joint.send_second(*ready, before=(d_pre,))
    got += sum_joint.send_half(0, *ready, before=(d_pre,))

    ready = got + (d_pre,)
    outer = GroupSum(
        place,
        *spread(
            [after(context, *ready), hidden],
            [joint, shrink],
            ((3 * joint_width, joint_width), (0, unit_width)),
        ),
    )
    got = sum_shrink.send_both(*ready, before=(outer.far,))
    got += sum_joint.send_half(1, *ready, before=(outer.far,))

    ready = got + (outer.far,)
    sum_expand = Reduce(place, (after(normed, *ready), d_pre))
    before = tuple(sum_expand.parts.values())
    got = sum_shrink.send_second(*ready, before=before)
    got += sum_shrink.send_half(0, *ready, before=before)
    outer_sent = outer.by_core(*ready)
    g_joint = returned(sum_joint, *ready)
    g_joint[1] = place.move(g_joint[1], core)
    g_joint[2] = place.move(g_joint[2], side)

    ready = got + before + tuple(outer_sent) + tuple(g_joint[1:3])
    inner_far, inner_near, inner_sums = spread(
        [after(d_joint, *ready), d_pre],
        [joint, expand],
        ((0, 3 * joint_width), (0, unit_width)),
        normed,
        own_vectors,
    )
    inner = GroupSum(place, inner_far, inner_near)
    got = sum_expand.send_both(*ready, before=(inner.far,))
    got += sum_shrink.send_half(1, *ready, before=(inner.far,))
    outer_sent = outer.hop(*ready)
    g_joint[3] = place.move(after(g_joint[3], *ready), side | core)

    ready = got + (inner.far, g_joint[3]) + tuple(outer_sent)
    own_sums = jnp.concatenate([joint_sums[0], unit_sums[0]])
    row_sums = jnp.concatenate(
        [
            inner_sums[0:1] / own_vectors[0:1],
            inner_sums[1:2],
            jnp.sum(masked, axis=0, dtype=WIDE, keepdims=True),
        ]
    )
    sums = SmallReduce(place, own_sums, arrange(place, row_sums, True).reshape(-1))
    sent = inner.by_core(*ready)
    got = sum_expand.send_second(*ready) + sum_expand.send_half(0, *ready)
    branch = outer.last_hop(*ready)
    g_shrink = returned(sum_shrink, *ready)

    ready = got + tuple(sent) + (branch,)
    got = sum_expand.send_half(1, *ready)
    sent = inner.hop(*ready)
    for flip, mask in ((1, core), (2, side), (3, side | core)):
        g_shrink[flip] = place.move(after(g_shrink[flip], *ready), mask)

    ready = got + tuple(sent) + tuple(g_shrink[1:])
    g_expand = returned(sum_expand, *ready)
    for flip, mask in ((1, core), (2, side), (3, side | core)):
        g_expand[flip] = place.move(g_expand[flip], mask)
    d_normed = inner.last_hop(*ready)
    g_joint[0] = after(g_joint[0], *ready)

    def shard_update(pieces, column, weight, moment, square, step_rate):
        news = adam_shard(
            place, pieces, column, weight[None], moment[None], square[None], step_rate
        )
        return [new[0] for new in news]

    joint_new = adam_shard(
        place,
        g_joint,
        0,
        joint_shard,
        kinds_first(joint_mean),
        kinds_first(joint_square),
        D ** (-0.5),
    )
    dense_new = shard_update(
        g_joint, 3 * joint_width, dense_weight, dense_mean, dense_square, (D // 32) ** (-0.5)
    )

    g_shrink[0] = after(g_shrink[0], joint_new[0], dense_new[0])
    shrink_new = shard_update(g_shrink, 0, shrink_weight, shrink_mean, shrink_square, FF ** (-0.5))

    sums.vector = after(sums.vector, shrink_new[0], *g_expand[1:])
    sums.step((core, 0), (0, 1), (core, 1))
    expand_new = shard_update(g_expand, 0, expand_weight, expand_mean, expand_square, D ** (-0.5))
    sums.vector = after(sums.vector, expand_new[0])
    sums.step((side, 0), (second, 0), (side | second, 0))
    for bit in place.ring:
        if bit != second:
            sums.step((bit, 0))
    own_sums, row_sums = sums.results()

    layer_output = mine.astype(WIDE) + branch + own_vectors[2] + own_vectors[3]
    layer_output = arrange(place, layer_output.astype(LOW), True)
    inputs = mine.astype(WIDE)
    centered = inputs - jnp.mean(inputs, axis=-1, keepdims=True)
    inverse = lax.rsqrt(jnp.mean(centered * centered, axis=-1, keepdims=True) + EPS_NORM)
    unit_rows = centered * inverse
    d_unit_rows = d_normed * own_vectors[0]
    d_inputs = inverse * (
        d_unit_rows
        - jnp.mean(d_unit_rows, axis=-1, keepdims=True)
        - unit_rows * jnp.mean(d_unit_rows * unit_rows, axis=-1, keepdims=True)
    )
    input_grad = arrange(place, masked.astype(WIDE) + d_inputs, True)

    features_here = HD // dp_size
    g_head = own_sums[:, : 3 * joint_width].reshape(4, 3, heads, HD)
    g_head = lax.dynamic_slice_in_dim(g_head, place.index * features_here, features_here, 3)
    g_head = g_head.transpose(3, 1, 0, 2).reshape(head_bias.shape)
    g_unit = own_sums[:, 3 * joint_width :].reshape(4 * units, HD)
    g_unit = lax.dynamic_slice_in_dim(g_unit, place.index * features_here, features_here, 1).T
    row_sums = row_sums.reshape(3, features)
    row_width = row_vectors.shape[1]
    g_rows = lax.dynamic_slice_in_dim(
        row_sums, (place.index * tensor_size + place.y) * row_width, row_width, 1
    )
    g_rows = jnp.concatenate([g_rows, g_rows[2:]])

    joint_new = [kinds_first(new) for new in joint_new]
    head_new = adam_update(head_bias, g_head, head_mean, head_square, 0.1, 0.0)
    unit_new = adam_update(unit_bias, g_unit, unit_mean, unit_square, 0.1, 0.0)
    rows_new = adam_update(row_vectors, g_rows, rows_mean, rows_square, 0.1, 0.0)
    return (
        layer_output,
        input_grad,
        joint_new[0],
        joint_new[1],
        joint_new[2],
        dense_new[0],
        dense_new[1],
        dense_new[2],
        expand_new[0],
        expand_new[1],
        expand_new[2],
        shrink_new[0],
        shrink_new[1],
        shrink_new[2],
        head_new[0],
        head_new[1],
        head_new[2],
        unit_new[0],
        unit_new[1],
        unit_new[2],
        rows_new[0],
        rows_new[1],
        rows_new[2],
    )


def solution(mesh):
    return jax.shard_map(
        functools.partial(body, mesh.shape["dp"], mesh.shape["tensor"]),
        mesh=mesh,
        in_specs=(
            P(("dp", "tensor"), None),
            P(("dp", "tensor"), None),
            P("dp"),
            P("dp", None, "tensor"),
            P("dp", "tensor"),
            P("dp", "tensor"),
            P("dp", "tensor"),
            P("dp", None, "tensor"),
            P("dp", "tensor"),
            P(None, ("dp", "tensor")),
            P("dp", None, "tensor"),
            P("dp", None, "tensor"),
            P("dp", "tensor"),
            P("dp", "tensor"),
            P("dp", "tensor"),
            P("dp", "tensor"),
            P("dp", "tensor"),
            P("dp", "tensor"),
            P("dp", None, "tensor"),
            P("dp", None, "tensor"),
            P("dp", "tensor"),
            P("dp", "tensor"),
            P(None, ("dp", "tensor")),
            P(None, ("dp", "tensor")),
        ),
        out_specs=(
            P(("dp", "tensor"), None),
            P(("dp", "tensor"), None),
            P("dp", None, "tensor"),
            P("dp", None, "tensor"),
            P("dp", None, "tensor"),
            P("dp", "tensor"),
            P("dp", "tensor"),
            P("dp", "tensor"),
            P("dp", "tensor"),
            P("dp", "tensor"),
            P("dp", "tensor"),
            P("dp", "tensor"),
            P("dp", "tensor"),
            P("dp", "tensor"),
            P("dp", None, "tensor"),
            P("dp", None, "tensor"),
            P("dp", None, "tensor"),
            P("dp", "tensor"),
            P("dp", "tensor"),
            P("dp", "tensor"),
            P(None, ("dp", "tensor")),
            P(None, ("dp", "tensor")),
            P(None, ("dp", "tensor")),
        ),
        check_vma=False,
    )
```
